256 devices in a mesh: slab: 8 (over x, y_hi), pencil: 32 (over z, y_lo, core).
Axes of the slice: x: 4, y: 4 (y_hi: 2, y_lo: 2; y = y_hi * 2 + y_lo), z: 8, core: 2. Of those that a mesh axis runs over, the one named last changes fastest.
Arguments:
- thermal_deviation: float32 [96, 512, 1024], P('slab', 'pencil'), may hold values from -6 to 6
- downstream_speed: bfloat16 [96, 512, 1024], P('slab', 'pencil'), may hold values from -4 to 4
- crossflow_speed: bfloat16 [96, 512, 1024], P('slab', 'pencil'), may hold values from -4 to 4
- wallward_speed: bfloat16 [96, 512, 1024], P('slab', 'pencil'), may hold values from -4 to 4
- downstream_solver_matrix: float32 [1024, 1024], replicated, may hold values from 0 to 1
- wallward_solver_matrices: float32 [2, 512, 512], replicated, may hold values from 0 to 1
- wall_segments: int32 [16], replicated, may hold values from 1 to 128, 1024 in all
Outputs:
- updated: float32 [96, 512, 1024], P('slab', 'pencil')
The draws below stay inside these ranges and needn't reach their ends.
Inputs may be any that keep to these rules, and one draw needn't show every extreme that they name: `wall_segments`: the 16 patches alternate between conducting and insulating, the first conducting; their lengths sum to 1024 and the longest is exactly 128.
All inputs are finite; a program needn't handle non-finite values.
Results may differ from the reference program's by a relative error of at most 0.0003.
Values sent between devices are 32-bit elements; how exact they have to be, the bound alone decides.
No kernel may reach another device: no remote copies, remote signals or barrier semaphores. Data moves between devices by JAX's collectives and lax.ppermute only.
A program may use at most 128 MiB of HBM per device.

```python
import math
import jax
import jax.numpy as jnp
import numpy as np
from jax import lax

NX = 1024
NZ = 512
NSEG = 16
SEGMAX = 128
NY = 96


def kernel_matrix(key, positions, spacing, periodic):
    extent = positions.shape[0]
    gap = jnp.abs(positions[:, None] - positions[None, :])
    if periodic:
        gap = jnp.minimum(gap, 1.0 - gap)
    noise = jax.random.uniform(key, (extent, extent), jnp.float32, -1.0, 1.0)
    smooth = jnp.exp(-gap / 0.3) * spacing[None, :] / 0.6
    diagonal = jnp.eye(extent, dtype=jnp.float32) * 0.6
    return diagonal + 0.8 * (1.0 + 0.5 * noise) * smooth


def draw_downstream_solver_matrix(key, part):
    levels = jnp.arange(NX).astype(jnp.float32)
    positions = (levels + 0.5) / NX
    spacing = jnp.ones((NX,), jnp.float32) / NX
    return kernel_matrix(jax.random.fold_in(key, 11), positions, spacing, True)


def draw_wallward_solver_matrices(key, part):
    levels = jnp.arange(NZ).astype(jnp.float32)
    angles = jnp.pi * (levels + 0.5) / NZ
    positions = 0.5 * (1.0 - jnp.cos(angles))
    spacing = jnp.pi / (2.0 * NZ) * jnp.sin(angles)
    conducting = kernel_matrix(jax.random.fold_in(key, 21), positions, spacing, False)
    insulating = kernel_matrix(jax.random.fold_in(key, 22), positions, spacing, False)
    return jnp.stack([conducting, insulating], axis=0)


def draw_thermal_deviation(key, part):
    field_shape = (NY, NZ, NX)
    base = jax.random.normal(jax.random.fold_in(key, 32), field_shape, jnp.float32)
    return jnp.clip(base, -6.0, 6.0)


def level_of(rng, shape, cuts, least, largest):
    def one(position, parts):
        heights = jax.random.uniform(jax.random.fold_in(jax.random.fold_in(rng, 6), position), (parts,), jnp.float32, least / len(cuts), largest / len(cuts))
        return jnp.repeat(jnp.exp(heights), shape[position] // parts).reshape((-1,) + (1,) * (len(shape) - position - 1))

    loudness = one(*cuts[0])
    for cut in cuts[1:]:
        loudness = loudness * one(*cut)
    return loudness


def profile(amount, total, limit, skew):
    loads = [(1 << 20) // math.isqrt(rank ** skew) + 1 for rank in range(2, amount + 1)]
    rest, counts = total - limit - (amount - 1), [1] * (amount - 1)
    while rest > 0:
        free = [i for i in range(amount - 1) if counts[i] < limit]
        mass, remaining = sum([loads[i] for i in free]), rest
        for i in free:
            addition = min(limit - counts[i], max(1, remaining * loads[i] // mass), rest)
            counts[i] = counts[i] + addition
            rest = rest - addition
    return np.array([limit] + counts)


def ragged(rng, amount, total, reach, slope):
    if amount == 2:
        one = jax.random.randint(rng, (), max(1, total - reach), min(reach, total - 1) + 1)
        return jnp.stack([one, total - one])
    lengths = jnp.asarray(profile(amount, total, reach, slope), jnp.int32)
    pairs = (amount - 1) // 2
    donor, receiver = lengths[1:1 + 2 * pairs:2], lengths[2:2 + 2 * pairs:2]
    margin = jnp.minimum(donor - 1, reach - receiver)
    shifted = jax.random.randint(jax.random.fold_in(rng, 1), (pairs,), 0, 1 << 20) % (margin + 1)
    lengths = lengths.at[1:1 + 2 * pairs:2].set(donor - shifted).at[2:2 + 2 * pairs:2].set(receiver + shifted)
    return lengths[jax.random.permutation(jax.random.fold_in(rng, 2), amount)]


def centred(own_key, dims, width, reach, shards=(), kind=jnp.bfloat16):
    entries = width * jax.random.normal(own_key, dims, jnp.float32)
    if shards:
        entries = entries * level_of(own_key, dims, shards, -0.22, 0.18)
    return jnp.clip(entries, -reach, reach).astype(kind)


def setup_inputs(seed: int = 0) -> dict:
    key_list = jax.random.split(jax.random.key(seed), 8)
    thermal_deviation = draw_thermal_deviation(jax.random.fold_in(key_list[7], 71), 0)
    downstream_speed = centred(key_list[1], (NY, NZ, NX), 1.0, 4.0, ((0, 8), (1, 32)))
    crossflow_speed = centred(key_list[2], (NY, NZ, NX), 1.0, 4.0, ((0, 8), (1, 32)))
    wallward_speed = centred(key_list[3], (NY, NZ, NX), 1.0, 4.0, ((0, 8), (1, 32)))
    downstream_solver_matrix = draw_downstream_solver_matrix(jax.random.fold_in(key_list[7], 71), 0)
    wallward_solver_matrices = draw_wallward_solver_matrices(jax.random.fold_in(key_list[7], 71), 0)
    wall_segments = ragged(key_list[6], NSEG, NX, SEGMAX, 2).astype(jnp.int32)
    return {"thermal_deviation": thermal_deviation, "downstream_speed": downstream_speed, "crossflow_speed": crossflow_speed, "wallward_speed": wallward_speed, "downstream_solver_matrix": downstream_solver_matrix, "wallward_solver_matrices": wallward_solver_matrices, "wall_segments": wall_segments}


TRANSPORT_PART = 0.25
CONDUCTION_PART = 0.2


def metric_of(levels, extent):
    return 0.5 / (1.0 + jnp.sin(jnp.pi * (levels + 0.5) / extent))


def reference(thermal_deviation, downstream_speed, crossflow_speed, wallward_speed, downstream_solver_matrix, wallward_solver_matrices, wall_segments):
    highest = lax.Precision.HIGHEST
    u_wide = downstream_speed.astype(jnp.float32)
    v_wide = crossflow_speed.astype(jnp.float32)
    w_wide = wallward_speed.astype(jnp.float32)
    downstream_ahead = jnp.roll(thermal_deviation, -1, axis=2)
    downstream_behind = jnp.roll(thermal_deviation, 1, axis=2)
    crossflow_ahead = jnp.roll(thermal_deviation, -1, axis=0)
    crossflow_behind = jnp.roll(thermal_deviation, 1, axis=0)
    bordered_heat = jnp.pad(thermal_deviation, ((0, 0), (1, 1), (0, 0)))
    wallward_above = bordered_heat[:, 2:, :]
    wallward_below = bordered_heat[:, :-2, :]
    mesh_stretching = metric_of(jnp.arange(NZ).astype(jnp.float32), NZ)[None, :, None]
    carried_transport = 0.5 * u_wide * (downstream_ahead - downstream_behind) + 0.5 * v_wide * (crossflow_ahead - crossflow_behind) + w_wide * mesh_stretching * (wallward_above - wallward_below)
    conducted_transport = (crossflow_ahead - 2.0 * thermal_deviation + crossflow_behind) + 0.5 * (downstream_ahead - 2.0 * thermal_deviation + downstream_behind) + 0.5 * mesh_stretching * (wallward_above - 2.0 * thermal_deviation + wallward_below)
    source_vector = thermal_deviation - TRANSPORT_PART * carried_transport + CONDUCTION_PART * conducted_transport
    solved_x = jnp.dot(source_vector.reshape(-1, NX), downstream_solver_matrix.T, precision=highest, preferred_element_type=jnp.float32).reshape(source_vector.shape)
    patch_ends = jnp.cumsum(wall_segments).astype(jnp.int32)
    columns = jnp.arange(NX, dtype=jnp.int32)
    crossed = jnp.sum((patch_ends[None, :] <= columns[:, None]).astype(jnp.int32), axis=1)
    insulated = (crossed % 2) == 1

    def per_plane(y_plane):
        conducting = jnp.dot(wallward_solver_matrices[0], y_plane, precision=highest, preferred_element_type=jnp.float32)
        insulating = jnp.dot(wallward_solver_matrices[1], y_plane, precision=highest, preferred_element_type=jnp.float32)
        return jnp.where(insulated[None, :], insulating, conducting)

    return lax.map(per_plane, solved_x)
```

```python
import jax
import jax.numpy as jnp
from jax import lax
from jax.experimental import pallas as pl
from jax.experimental.pallas import tpu as pltpu
from jax.sharding import PartitionSpec as P

TRANSPORT_PART = 0.25
CONDUCTION_PART = 0.2
LANES = 128
VMEM = pl.BlockSpec(memory_space=pltpu.VMEM)
SMEM = pl.BlockSpec(memory_space=pltpu.SMEM)


def metric_of(levels, extent):
    return 0.5 / (1.0 + jnp.sin(jnp.pi * (levels + 0.5) / extent))


def halves(wide):
    high = wide.astype(jnp.bfloat16)
    return high, (wide - high.astype(jnp.float32)).astype(jnp.bfloat16)


def split_kernel(a_ref, w_ref, ah_ref, al_ref, wh_ref, wl_ref):
    ah_ref[...], al_ref[...] = halves(a_ref[...])
    wh_ref[...], wl_ref[...] = halves(w_ref[...])


def split_matrices(a, w):
    steps = 8
    n, k = a.shape[0], w.shape[1]
    a_spec = pl.BlockSpec((n // steps, n), lambda i: (i, 0))
    w_spec = pl.BlockSpec((2, k // steps, k), lambda i: (0, i, 0))
    a16 = jax.ShapeDtypeStruct(a.shape, jnp.bfloat16)
    w16 = jax.ShapeDtypeStruct(w.shape, jnp.bfloat16)
    return pl.pallas_call(
        split_kernel,
        grid=(steps,),
        in_specs=[a_spec, w_spec],
        out_specs=[a_spec, a_spec, w_spec, w_spec],
        out_shape=[a16, a16, w16, w16],
        compiler_params=pltpu.CompilerParams(vmem_limit_bytes=16 * 2**20),
        cost_estimate=pl.CostEstimate(
            flops=4 * (a.size + w.size), bytes_accessed=8 * (a.size + w.size), transcendentals=0
        ),
        name="split_matrices",
    )(a, w)


def row_kernel(t_ref, u_ref, v_ref, w_ref, yb_ref, ya_ref, zb_ref, za_ref, g_ref, ah_ref, al_ref, out_ref, rh, rl):
    planes, rows, nx = t_ref.shape
    metric = jnp.concatenate([g_ref[...]] * (nx // LANES), axis=1)
    level = lax.broadcasted_iota(jnp.int32, (rows, nx), 0)
    for y in range(planes):
        t = t_ref[y]
        ahead = t_ref[y + 1] if y + 1 < planes else ya_ref[...]
        behind = t_ref[y - 1] if y else yb_ref[...]
        east = pltpu.roll(t, nx - 1, 1)
        west = pltpu.roll(t, 1, 1)
        above = jnp.where(level == rows - 1, za_ref[y : y + 1, :], pltpu.roll(t, rows - 1, 0))
        below = jnp.where(level == 0, zb_ref[y : y + 1, :], pltpu.roll(t, 1, 0))
        u = u_ref[y].astype(jnp.float32)
        v = v_ref[y].astype(jnp.float32)
        w = w_ref[y].astype(jnp.float32)
        carried = 0.5 * u * (east - west) + 0.5 * v * (ahead - behind) + w * metric * (above - below)
        conducted = (
            (ahead - 2.0 * t + behind)
            + 0.5 * (east - 2.0 * t + west)
            + 0.5 * metric * (above - 2.0 * t + below)
        )
        side = t - TRANSPORT_PART * carried + CONDUCTION_PART * conducted
        rh[y * rows : (y + 1) * rows, :], rl[y * rows : (y + 1) * rows, :] = halves(side)
    wide = 2 * LANES
    unit_rows = 3 * rows
    blocks = nx // LANES
    for c in range(nx // wide):
        ah = ah_ref[c * wide : (c + 1) * wide, :]
        al = al_ref[c * wide : (c + 1) * wide, :]

        def dot(x, m):
            return lax.dot_general(x, m, (((1,), (1,)), ((), ())), preferred_element_type=jnp.float32)

        solved = dot(rh[...], ah) + (dot(rh[...], al) + dot(rl[...], ah))
        for q in range(planes // 3):
            for h in range(2):
                piece = solved[q * unit_rows : (q + 1) * unit_rows, h * LANES : (h + 1) * LANES]
                out_ref[q * blocks + 2 * c + h] = piece.reshape(3, rows, LANES)


def row_solve(t, u, v, w, halos, metric, ah, al, groups):
    planes, rows, nx = t.shape
    return pl.pallas_call(
        row_kernel,
        in_specs=[VMEM] * 11,
        out_specs=VMEM,
        out_shape=jax.ShapeDtypeStruct((groups, 3, rows, LANES), jnp.float32),
        scratch_shapes=[pltpu.VMEM((planes * rows, nx), jnp.bfloat16)] * 2,
        compiler_params=pltpu.CompilerParams(vmem_limit_bytes=32 * 2**20),
        cost_estimate=pl.CostEstimate(
            flops=6 * planes * rows * nx * nx, bytes_accessed=8 * 2**20, transcendentals=0
        ),
        name="row_solve",
    )(t, u, v, w, *halos, metric, ah, al)


def column_kernel(first_ref, seg_ref, x_ref, wh_ref, wl_ref, out_ref):
    groups, units, rows, lanes = x_ref.shape
    column = lax.broadcasted_iota(jnp.int32, (1, lanes), 1) + first_ref[0]
    crossed = jnp.zeros((1, lanes), jnp.int32)
    end = jnp.int32(0)
    for s in range(seg_ref.shape[0]):
        end = end + seg_ref[s]
        crossed = crossed + jnp.where(column >= end, 1, 0)
    insulated = jnp.concatenate([crossed % 2] * units, axis=1) == 1
    extent = groups * rows
    lines = jnp.concatenate([x_ref[:, i].reshape(extent, lanes) for i in range(units)], axis=1)
    xh, xl = halves(lines)
    both = jnp.concatenate([xh, xl], axis=1)
    width = units * lanes

    def solve(c, lo, hi):
        d = jnp.dot(wh_ref[c, lo:hi, :], both, preferred_element_type=jnp.float32)
        e = jnp.dot(wl_ref[c, lo:hi, :], xh, preferred_element_type=jnp.float32)
        return d[:, :width] + (d[:, width:] + e)

    step = 128
    for k in range(0, extent, step):
        solved = jnp.where(insulated, solve(1, k, k + step), solve(0, k, k + step))
        for i in range(units):
            out_ref[k // rows : (k + step) // rows, i] = solved[:, i * lanes : (i + 1) * lanes].reshape(
                step // rows, rows, lanes
            )


def column_solve(first, segments, x, wh, wl):
    return pl.pallas_call(
        column_kernel,
        in_specs=[SMEM, SMEM, VMEM, VMEM, VMEM],
        out_specs=VMEM,
        out_shape=jax.ShapeDtypeStruct(x.shape, jnp.float32),
        compiler_params=pltpu.CompilerParams(vmem_limit_bytes=32 * 2**20),
        cost_estimate=pl.CostEstimate(
            flops=12 * wh.shape[1] * x.size, bytes_accessed=4 * 2**20, transcendentals=0
        ),
        name="column_solve",
    )(first, segments, x, wh, wl)


def place_kernel(x_ref, out_ref):
    groups = x_ref.shape[0]
    blocks = out_ref.shape[2] // LANES
    for p in range(groups):
        q, b = p // blocks, p % blocks
        out_ref[3 * q : 3 * q + 3, :, b * LANES : (b + 1) * LANES] = x_ref[p]


def place(x, shape):
    return pl.pallas_call(
        place_kernel,
        in_specs=[VMEM],
        out_specs=VMEM,
        out_shape=jax.ShapeDtypeStruct(shape, jnp.float32),
        compiler_params=pltpu.CompilerParams(vmem_limit_bytes=16 * 2**20),
        name="place",
    )(x)


def swapped(x):
    return lax.all_to_all(x, "pencil", split_axis=0, concat_axis=0, tiled=True)


def on_device(t, u, v, w, downstream_solver_matrix, wallward_solver_matrices, wall_segments):
    planes, rows, nx = t.shape
    slabs, groups = lax.axis_size("slab"), lax.axis_size("pencil")
    here = lax.axis_index("pencil")
    up = [(i, i + 1) for i in range(groups - 1)]
    down = [(i + 1, i) for i in range(groups - 1)]
    halos = (
        lax.ppermute(t[-1], "slab", [(i, (i + 1) % slabs) for i in range(slabs)]),
        lax.ppermute(t[0], "slab", [((i + 1) % slabs, i) for i in range(slabs)]),
        lax.ppermute(t[:, -1], "pencil", up),
        lax.ppermute(t[:, 0], "pencil", down),
    )
    levels = (here * rows + jnp.arange(rows, dtype=jnp.int32)).astype(jnp.float32)
    metric = jnp.broadcast_to(metric_of(levels, groups * rows)[:, None], (rows, LANES))
    ah, al, wh, wl = split_matrices(downstream_solver_matrix, wallward_solver_matrices)
    x = swapped(row_solve(t, u, v, w, halos, metric, ah, al, groups))
    first = (here % (nx // LANES) * LANES).astype(jnp.int32).reshape(1)
    x = swapped(column_solve(first, wall_segments, x, wh, wl))
    return place(x, t.shape)


def solution(mesh):
    field = P("slab", "pencil", None)
    return jax.shard_map(
        on_device,
        mesh=mesh,
        in_specs=(field, field, field, field, P(), P(), P()),
        out_specs=field,
        check_vma=False,
    )
```

```python
import jax
import jax.numpy as jnp
from jax import lax
from jax.experimental import pallas as pl
from jax.experimental.pallas import tpu as pltpu
from jax.sharding import PartitionSpec as P

TRANSPORT_PART = 0.25
CONDUCTION_PART = 0.2
LANES = 128
EDGE = 53
PREP = 46
VMEM = pl.BlockSpec(memory_space=pltpu.VMEM)
HBM = pl.BlockSpec(memory_space=pltpu.HBM)
SMEM = pl.BlockSpec(memory_space=pltpu.SMEM)


def metric_of(levels, extent):
    return 0.5 / (1.0 + jnp.sin(jnp.pi * (levels + 0.5) / extent))


def halves(wide):
    high = wide.astype(jnp.bfloat16)
    return high, (wide - high.astype(jnp.float32)).astype(jnp.bfloat16)


def edge_kernel(t_hbm, yf_ref, yl_ref, zl_ref, zh_ref, buf, sems):
    planes, rows, _ = t_hbm.shape
    half = buf.shape[2]
    copies = [
        pltpu.make_async_copy(t_hbm.at[:, pl.ds(0, half)], buf.at[0], sems.at[0]),
        pltpu.make_async_copy(t_hbm.at[:, pl.ds(rows - half, half)], buf.at[1], sems.at[1]),
        pltpu.make_async_copy(t_hbm.at[0], yf_ref, sems.at[2]),
        pltpu.make_async_copy(t_hbm.at[planes - 1], yl_ref, sems.at[3]),
    ]
    for copy in copies:
        copy.start()
    copies[0].wait()
    for y in range(planes):
        zl_ref[y : y + 1, :] = buf[0, y, :1, :]
    copies[1].wait()
    for y in range(planes):
        zh_ref[y : y + 1, :] = buf[1, y, half - 1 :, :]
    copies[2].wait()
    copies[3].wait()


def edges(t):
    planes, rows, nx = t.shape
    half = 8
    plane = jax.ShapeDtypeStruct((rows, nx), t.dtype)
    level = jax.ShapeDtypeStruct((planes, nx), t.dtype)
    return pl.pallas_call(
        edge_kernel,
        in_specs=[HBM],
        out_specs=[VMEM] * 4,
        out_shape=[plane, plane, level, level],
        scratch_shapes=[pltpu.VMEM((2, planes, half, nx), t.dtype), pltpu.SemaphoreType.DMA((4,))],
        compiler_params=pltpu.CompilerParams(vmem_limit_bytes=EDGE * 2**20),
        name="edges",
    )(t)


def prepare_kernel(here_ref, seg_ref, a_hbm, w_hbm, ah_ref, al_ref, wh_ref, wl_ref, mask_ref, g_ref, a_buf, w_buf, sems):
    parts = sems.shape[0] // 2
    a_rows, w_rows = a_buf.shape[0] // parts, w_buf.shape[1] // parts
    copies = []
    for i in range(parts):
        cut = slice(i * a_rows, (i + 1) * a_rows)
        copies.append(pltpu.make_async_copy(a_hbm.at[cut], a_buf.at[cut], sems.at[i]))
    for i in range(parts):
        cut = slice(i * w_rows, (i + 1) * w_rows)
        copies.append(pltpu.make_async_copy(w_hbm.at[:, cut], w_buf.at[:, cut], sems.at[parts + i]))
    for copy in copies:
        copy.start()
    here = here_ref[0]
    rows, lanes = g_ref.shape
    blocks = a_buf.shape[0] // lanes
    column = lax.broadcasted_iota(jnp.int32, mask_ref.shape, 1) + here % blocks * lanes
    crossed = jnp.zeros(mask_ref.shape, jnp.int32)
    end = jnp.int32(0)
    for s in range(seg_ref.shape[0]):
        end = end + seg_ref[s]
        crossed = crossed + jnp.where(column >= end, 1, 0)
    mask_ref[...] = crossed % 2
    levels = (lax.broadcasted_iota(jnp.int32, (rows, lanes), 0) + here * rows).astype(jnp.float32)
    g_ref[...] = metric_of(levels, w_buf.shape[1])
    for i in range(parts):
        cut = slice(i * a_rows, (i + 1) * a_rows)
        copies[i].wait()
        ah_ref[cut], al_ref[cut] = halves(a_buf[cut])
    for i in range(parts):
        cut = slice(i * w_rows, (i + 1) * w_rows)
        copies[parts + i].wait()
        wh_ref[:, cut], wl_ref[:, cut] = halves(w_buf[:, cut])


def prepare(here, segments, a, w, rows):
    a16 = jax.ShapeDtypeStruct(a.shape, jnp.bfloat16)
    w16 = jax.ShapeDtypeStruct(w.shape, jnp.bfloat16)
    parts = 4
    return pl.pallas_call(
        prepare_kernel,
        in_specs=[SMEM, SMEM, HBM, HBM],
        out_specs=[VMEM] * 6,
        out_shape=[
            a16,
            a16,
            w16,
            w16,
            jax.ShapeDtypeStruct((8, LANES), jnp.int32),
            jax.ShapeDtypeStruct((rows, LANES), jnp.float32),
        ],
        scratch_shapes=[
            pltpu.VMEM(a.shape, a.dtype),
            pltpu.VMEM(w.shape, w.dtype),
            pltpu.SemaphoreType.DMA((2 * parts,)),
        ],
        compiler_params=pltpu.CompilerParams(vmem_limit_bytes=PREP * 2**20),
        cost_estimate=pl.CostEstimate(
            flops=4 * (a.size + w.size), bytes_accessed=8 * (a.size + w.size), transcendentals=0
        ),
        name="prepare",
    )(here, segments, a, w)


def row_kernel(t_ref, u_ref, v_ref, w_ref, yb_ref, ya_ref, zb_ref, za_ref, g_ref, ah_ref, al_ref, out_ref, rh, rl):
    planes, rows, nx = t_ref.shape
    metric = jnp.concatenate([g_ref[...]] * (nx // LANES), axis=1)
    level = lax.broadcasted_iota(jnp.int32, (rows, nx), 0)
    for y in range(planes):
        t = t_ref[y]
        ahead = t_ref[y + 1] if y + 1 < planes else ya_ref[...]
        behind = t_ref[y - 1] if y else yb_ref[...]
        east = pltpu.roll(t, nx - 1, 1)
        west = pltpu.roll(t, 1, 1)
        above = jnp.where(level == rows - 1, za_ref[y : y + 1, :], pltpu.roll(t, rows - 1, 0))
        below = jnp.where(level == 0, zb_ref[y : y + 1, :], pltpu.roll(t, 1, 0))
        u = u_ref[y].astype(jnp.float32)
        v = v_ref[y].astype(jnp.float32)
        w = w_ref[y].astype(jnp.float32)
        carried = 0.5 * u * (east - west) + 0.5 * v * (ahead - behind) + w * metric * (above - below)
        conducted = (
            (ahead - 2.0 * t + behind)
            + 0.5 * (east - 2.0 * t + west)
            + 0.5 * metric * (above - 2.0 * t + below)
        )
        side = t - TRANSPORT_PART * carried + CONDUCTION_PART * conducted
        rh[y * rows : (y + 1) * rows, :], rl[y * rows : (y + 1) * rows, :] = halves(side)
    wide = 2 * LANES
    unit_rows = 3 * rows
    blocks = nx // LANES
    for c in range(nx // wide):
        ah = ah_ref[c * wide : (c + 1) * wide, :]
        al = al_ref[c * wide : (c + 1) * wide, :]

        def dot(x, m):
            return lax.dot_general(x, m, (((1,), (1,)), ((), ())), preferred_element_type=jnp.float32)

        solved = dot(rh[...], ah) + (dot(rh[...], al) + dot(rl[...], ah))
        for q in range(planes // 3):
            for h in range(2):
                piece = solved[q * unit_rows : (q + 1) * unit_rows, h * LANES : (h + 1) * LANES]
                out_ref[q * blocks + 2 * c + h] = piece.reshape(3, rows, LANES)


def row_solve(t, u, v, w, halos, metric, ah, al, groups):
    planes, rows, nx = t.shape
    return pl.pallas_call(
        row_kernel,
        in_specs=[VMEM] * 11,
        out_specs=VMEM,
        out_shape=jax.ShapeDtypeStruct((groups, 3, rows, LANES), jnp.float32),
        scratch_shapes=[pltpu.VMEM((planes * rows, nx), jnp.bfloat16)] * 2,
        compiler_params=pltpu.CompilerParams(vmem_limit_bytes=32 * 2**20),
        cost_estimate=pl.CostEstimate(
            flops=6 * planes * rows * nx * nx, bytes_accessed=8 * 2**20, transcendentals=0
        ),
        name="row_solve",
    )(t, u, v, w, *halos, metric, ah, al)


def column_kernel(mask_ref, x_ref, wh_ref, wl_ref, out_ref):
    groups, units, rows, lanes = x_ref.shape
    insulated = jnp.concatenate([mask_ref[:1, :]] * units, axis=1) == 1
    extent = groups * rows
    lines = jnp.concatenate([x_ref[:, i].reshape(extent, lanes) for i in range(units)], axis=1)
    xh, xl = halves(lines)
    both = jnp.concatenate([xh, xl], axis=1)
    width = units * lanes

    def solve(c, lo, hi):
        d = jnp.dot(wh_ref[c, lo:hi, :], both, preferred_element_type=jnp.float32)
        e = jnp.dot(wl_ref[c, lo:hi, :], xh, preferred_element_type=jnp.float32)
        return d[:, :width] + (d[:, width:] + e)

    step = 128
    for k in range(0, extent, step):
        solved = jnp.where(insulated, solve(1, k, k + step), solve(0, k, k + step))
        for i in range(units):
            out_ref[k // rows : (k + step) // rows, i] = solved[:, i * lanes : (i + 1) * lanes].reshape(
                step // rows, rows, lanes
            )


def column_solve(mask, x, wh, wl):
    return pl.pallas_call(
        column_kernel,
        in_specs=[VMEM] * 4,
        out_specs=VMEM,
        out_shape=jax.ShapeDtypeStruct(x.shape, jnp.float32),
        compiler_params=pltpu.CompilerParams(vmem_limit_bytes=32 * 2**20),
        cost_estimate=pl.CostEstimate(
            flops=12 * wh.shape[1] * x.size, bytes_accessed=4 * 2**20, transcendentals=0
        ),
        name="column_solve",
    )(mask, x, wh, wl)


def place_kernel(x_ref, out_ref):
    groups = x_ref.shape[0]
    blocks = out_ref.shape[2] // LANES
    for p in range(groups):
        q, b = p // blocks, p % blocks
        out_ref[3 * q : 3 * q + 3, :, b * LANES : (b + 1) * LANES] = x_ref[p]


def place(x, shape):
    return pl.pallas_call(
        place_kernel,
        in_specs=[VMEM],
        out_specs=VMEM,
        out_shape=jax.ShapeDtypeStruct(shape, jnp.float32),
        compiler_params=pltpu.CompilerParams(vmem_limit_bytes=16 * 2**20),
        name="place",
    )(x)


def swapped(x):
    return lax.all_to_all(x, "pencil", split_axis=0, concat_axis=0, tiled=True)


def on_device(t, u, v, w, downstream_solver_matrix, wallward_solver_matrices, wall_segments):
    planes, rows, nx = t.shape
    slabs, groups = lax.axis_size("slab"), lax.axis_size("pencil")
    here = lax.axis_index("pencil")
    up = [(i, i + 1) for i in range(groups - 1)]
    down = [(i + 1, i) for i in range(groups - 1)]
    y_first, y_last, z_low, z_high = edges(t)
    halos = (
        lax.ppermute(y_last, "slab", [(i, (i + 1) % slabs) for i in range(slabs)]),
        lax.ppermute(y_first, "slab", [((i + 1) % slabs, i) for i in range(slabs)]),
        lax.ppermute(z_high, "pencil", up),
        lax.ppermute(z_low, "pencil", down),
    )
    ah, al, wh, wl, mask, metric = prepare(
        here.astype(jnp.int32).reshape(1), wall_segments, downstream_solver_matrix, wallward_solver_matrices, rows
    )
    x = swapped(row_solve(t, u, v, w, halos, metric, ah, al, groups))
    x = swapped(column_solve(mask, x, wh, wl))
    return place(x, t.shape)


def solution(mesh):
    field = P("slab", "pencil", None)
    return jax.shard_map(
        on_device,
        mesh=mesh,
        in_specs=(field, field, field, field, P(), P(), P()),
        out_specs=field,
        check_vma=False,
    )
```

```python
import jax
import jax.numpy as jnp
from jax import lax
from jax.experimental import pallas as pl
from jax.experimental.pallas import tpu as pltpu
from jax.sharding import PartitionSpec as P

TRANSPORT_PART = 0.25
CONDUCTION_PART = 0.2
LANES = 128
LAYER = 4
BULK = 2
EDGE = 53
PREP = 46
VMEM = pl.BlockSpec(memory_space=pltpu.VMEM)
HBM = pl.BlockSpec(memory_space=pltpu.HBM)
SMEM = pl.BlockSpec(memory_space=pltpu.SMEM)


def metric_of(levels, extent):
    return 0.5 / (1.0 + jnp.sin(jnp.pi * (levels + 0.5) / extent))


def halves(wide):
    high = wide.astype(jnp.bfloat16)
    return high, (wide - high.astype(jnp.float32)).astype(jnp.bfloat16)


def edge_kernel(here_ref, seg_hbm, t_hbm, yf_ref, yl_ref, zl_ref, zh_ref, mask_ref, buf, seg_ref, sems):
    planes, rows, _ = t_hbm.shape
    half = buf.shape[2]
    copies = [
        pltpu.make_async_copy(t_hbm.at[:, pl.ds(0, half)], buf.at[0], sems.at[0]),
        pltpu.make_async_copy(t_hbm.at[:, pl.ds(rows - half, half)], buf.at[1], sems.at[1]),
        pltpu.make_async_copy(t_hbm.at[0], yf_ref, sems.at[2]),
        pltpu.make_async_copy(t_hbm.at[planes - 1], yl_ref, sems.at[3]),
        pltpu.make_async_copy(seg_hbm, seg_ref, sems.at[4]),
    ]
    for copy in copies:
        copy.start()
    copies[4].wait()
    column = lax.broadcasted_iota(jnp.int32, mask_ref.shape, 1) + here_ref[0] // LAYER * LANES
    crossed = jnp.zeros(mask_ref.shape, jnp.int32)
    end = jnp.int32(0)
    for s in range(seg_ref.shape[0]):
        end = end + seg_ref[s]
        crossed = crossed + jnp.where(column >= end, 1, 0)
    mask_ref[...] = crossed % 2
    copies[0].wait()
    for y in range(planes):
        zl_ref[y : y + 1, :] = buf[0, y, :1, :]
    copies[1].wait()
    for y in range(planes):
        zh_ref[y : y + 1, :] = buf[1, y, half - 1 :, :]
    copies[2].wait()
    copies[3].wait()


def edges(here, segments, t):
    planes, rows, nx = t.shape
    half = 8
    plane = jax.ShapeDtypeStruct((rows, nx), t.dtype)
    level = jax.ShapeDtypeStruct((planes, nx), t.dtype)
    return pl.pallas_call(
        edge_kernel,
        in_specs=[SMEM, HBM, HBM],
        out_specs=[VMEM] * 5,
        out_shape=[plane, plane, level, level, jax.ShapeDtypeStruct((8, LANES), jnp.int32)],
        scratch_shapes=[
            pltpu.VMEM((2, planes, half, nx), t.dtype),
            pltpu.SMEM(segments.shape, jnp.int32),
            pltpu.SemaphoreType.DMA((5,)),
        ],
        compiler_params=pltpu.CompilerParams(vmem_limit_bytes=EDGE * 2**20),
        name="edges",
    )(here, segments, t)


def prepare_kernel(here_ref, a_hbm, w_hbm, ah_ref, al_ref, wh_ref, wl_ref, g_ref, a_buf, w_buf, sems):
    parts = sems.shape[0] // 2
    a_rows, w_rows = a_buf.shape[0] // parts, w_buf.shape[1] // parts
    copies = []
    for i in range(parts):
        cut = slice(i * a_rows, (i + 1) * a_rows)
        copies.append(pltpu.make_async_copy(a_hbm.at[cut], a_buf.at[cut], sems.at[i]))
    for i in range(parts):
        cut = slice(i * w_rows, (i + 1) * w_rows)
        copies.append(pltpu.make_async_copy(w_hbm.at[:, cut], w_buf.at[:, cut], sems.at[parts + i]))
    for copy in copies:
        copy.start()
    rows, lanes = g_ref.shape
    levels = (lax.broadcasted_iota(jnp.int32, (rows, lanes), 0) + here_ref[0] * rows).astype(jnp.float32)
    g_ref[...] = metric_of(levels, w_buf.shape[1])
    for i in range(parts):
        cut = slice(i * a_rows, (i + 1) * a_rows)
        copies[i].wait()
        ah_ref[cut], al_ref[cut] = halves(a_buf[cut])
    for i in range(parts):
        cut = slice(i * w_rows, (i + 1) * w_rows)
        copies[parts + i].wait()
        wh_ref[:, cut], wl_ref[:, cut] = halves(w_buf[:, cut])


def prepare(here, a, w, rows):
    a16 = jax.ShapeDtypeStruct(a.shape, jnp.bfloat16)
    w16 = jax.ShapeDtypeStruct(w.shape, jnp.bfloat16)
    parts = 4
    return pl.pallas_call(
        prepare_kernel,
        in_specs=[SMEM, HBM, HBM],
        out_specs=[VMEM] * 5,
        out_shape=[a16, a16, w16, w16, jax.ShapeDtypeStruct((rows, LANES), jnp.float32)],
        scratch_shapes=[
            pltpu.VMEM(a.shape, a.dtype),
            pltpu.VMEM(w.shape, w.dtype),
            pltpu.SemaphoreType.DMA((2 * parts,)),
        ],
        compiler_params=pltpu.CompilerParams(vmem_limit_bytes=PREP * 2**20),
        cost_estimate=pl.CostEstimate(
            flops=4 * (a.size + w.size), bytes_accessed=8 * (a.size + w.size), transcendentals=0
        ),
        name="prepare",
    )(here, a, w)


def row_kernel(
    here_ref, t_ref, u_ref, v_ref, w_ref, yb_ref, ya_ref, zb_ref, za_ref, g_ref, ah_ref, al_ref, out_ref, *rest
):
    by_place, (rh, rl, kept) = rest[:LAYER], rest[LAYER:]
    planes, rows, nx = t_ref.shape
    metric = jnp.concatenate([g_ref[...]] * (nx // LANES), axis=1)
    level = lax.broadcasted_iota(jnp.int32, (rows, nx), 0)
    for y in range(planes):
        t = t_ref[y]
        ahead = t_ref[y + 1] if y + 1 < planes else ya_ref[...]
        behind = t_ref[y - 1] if y else yb_ref[...]
        east = pltpu.roll(t, nx - 1, 1)
        west = pltpu.roll(t, 1, 1)
        above = jnp.where(level == rows - 1, za_ref[y : y + 1, :], pltpu.roll(t, rows - 1, 0))
        below = jnp.where(level == 0, zb_ref[y : y + 1, :], pltpu.roll(t, 1, 0))
        u = u_ref[y].astype(jnp.float32)
        v = v_ref[y].astype(jnp.float32)
        w = w_ref[y].astype(jnp.float32)
        carried = 0.5 * u * (east - west) + 0.5 * v * (ahead - behind) + w * metric * (above - below)
        conducted = (
            (ahead - 2.0 * t + behind)
            + 0.5 * (east - 2.0 * t + west)
            + 0.5 * metric * (above - 2.0 * t + below)
        )
        side = t - TRANSPORT_PART * carried + CONDUCTION_PART * conducted
        rh[y * rows : (y + 1) * rows, :], rl[y * rows : (y + 1) * rows, :] = halves(side)
    wide = 2 * LANES
    unit_rows = 3 * rows
    blocks = nx // LANES
    for c in range(nx // wide):
        ah = ah_ref[c * wide : (c + 1) * wide, :]
        al = al_ref[c * wide : (c + 1) * wide, :]

        def dot(x, m):
            return lax.dot_general(x, m, (((1,), (1,)), ((), ())), preferred_element_type=jnp.float32)

        solved = dot(rh[...], ah) + (dot(rh[...], al) + dot(rl[...], ah))
        for q in range(planes // 3):
            for h in range(2):
                block = 2 * c + h
                piece = solved[q * unit_rows : (q + 1) * unit_rows, h * LANES : (h + 1) * LANES]
                piece = piece.reshape(3, rows, LANES)
                out_ref[LAYER * block + q] = piece[:BULK]
                kept[q, block] = piece[BULK]
    layer, place_ = here_ref[0] // LAYER, here_ref[0] % LAYER
    for s in range(LAYER):
        for d in range(blocks):
            by_place[s][d] = kept[place_ ^ s, (layer + d) % blocks]


def row_solve(here, t, u, v, w, halos, metric, ah, al, groups):
    planes, rows, nx = t.shape
    layers = groups // LAYER
    lines = jax.ShapeDtypeStruct((layers, rows, LANES), jnp.float32)
    return pl.pallas_call(
        row_kernel,
        in_specs=[SMEM] + [VMEM] * 11,
        out_specs=[VMEM] * (1 + LAYER),
        out_shape=[jax.ShapeDtypeStruct((groups, BULK, rows, LANES), jnp.float32)] + [lines] * LAYER,
        scratch_shapes=[pltpu.VMEM((planes * rows, nx), jnp.bfloat16)] * 2
        + [pltpu.VMEM((LAYER, layers, rows, LANES), jnp.float32)],
        compiler_params=pltpu.CompilerParams(vmem_limit_bytes=32 * 2**20),
        cost_estimate=pl.CostEstimate(
            flops=6 * planes * rows * nx * nx, bytes_accessed=8 * 2**20, transcendentals=0
        ),
        name="row_solve",
    )(here, t, u, v, w, *halos, metric, ah, al)


def solved_lines(lines, insulated, wh_ref, wl_ref, k, step):
    xh, both = lines
    width = xh.shape[1]

    def solve(c):
        d = jnp.dot(wh_ref[c, k : k + step, :], both, preferred_element_type=jnp.float32)
        e = jnp.dot(wl_ref[c, k : k + step, :], xh, preferred_element_type=jnp.float32)
        return d[:, :width] + (d[:, width:] + e)

    return jnp.where(insulated, solve(1), solve(0))


def column_kernel(mask_ref, x_ref, wh_ref, wl_ref, _, out_ref):
    groups, units, rows, lanes = x_ref.shape
    insulated = jnp.concatenate([mask_ref[:1, :]] * units, axis=1) == 1
    extent = groups * rows
    lines = jnp.concatenate([x_ref[:, i].reshape(extent, lanes) for i in range(units)], axis=1)
    xh, xl = halves(lines)
    lines = xh, jnp.concatenate([xh, xl], axis=1)
    step = 128
    for k in range(0, extent, step):
        solved = solved_lines(lines, insulated, wh_ref, wl_ref, k, step)
        for i in range(units):
            out_ref[k // rows : (k + step) // rows, i] = solved[:, i * lanes : (i + 1) * lanes].reshape(
                step // rows, rows, lanes
            )


def column_solve(mask, x, wh, wl, after):
    return pl.pallas_call(
        column_kernel,
        in_specs=[VMEM] * 4 + [pl.BlockSpec(memory_space=pl.ANY)],
        out_specs=VMEM,
        out_shape=jax.ShapeDtypeStruct(x.shape, jnp.float32),
        compiler_params=pltpu.CompilerParams(vmem_limit_bytes=32 * 2**20),
        cost_estimate=pl.CostEstimate(
            flops=12 * wh.shape[1] * x.size, bytes_accessed=4 * 2**20, transcendentals=0
        ),
        name="column_solve",
    )(mask, x, wh, wl, after)


def single_kernel(here_ref, mask_ref, *refs):
    layers = (len(refs) - 3 - LAYER)
    arrived, (wh_ref, wl_ref), by_place, lines = refs[:layers], refs[layers : layers + 2], refs[layers + 2 : -1], refs[-1]
    rows, lanes = lines.shape[1:]
    layer, place_ = here_ref[0] // LAYER, here_ref[0] % LAYER
    for d in range(layers):
        source = (layer + layers - d) % layers
        for s in range(LAYER):
            lines[LAYER * source + (place_ ^ s)] = arrived[d][s]
    insulated = mask_ref[:1, :] == 1
    extent = lines.shape[0] * rows
    xh, xl = halves(lines[...].reshape(extent, lanes))
    both = xh, jnp.concatenate([xh, xl], axis=1)
    step = 128
    for k in range(0, extent, step):
        solved = solved_lines(both, insulated, wh_ref, wl_ref, k, step)
        lines[k // rows : (k + step) // rows] = solved.reshape(step // rows, rows, lanes)
    for s in range(LAYER):
        for d in range(layers):
            by_place[s][d] = lines[LAYER * ((layer + d) % layers) + (place_ ^ s)]


def single_solve(here, mask, arrived, wh, wl):
    layers = len(arrived)
    rows, lanes = arrived[0].shape[1:]
    return pl.pallas_call(
        single_kernel,
        in_specs=[SMEM] + [VMEM] * (3 + layers),
        out_specs=[VMEM] * LAYER,
        out_shape=[jax.ShapeDtypeStruct((layers, rows, lanes), jnp.float32)] * LAYER,
        scratch_shapes=[pltpu.VMEM((LAYER * layers, rows, lanes), jnp.float32)],
        compiler_params=pltpu.CompilerParams(vmem_limit_bytes=32 * 2**20),
        cost_estimate=pl.CostEstimate(
            flops=12 * wh.shape[1] * LAYER * layers * rows * lanes, bytes_accessed=4 * 2**20, transcendentals=0
        ),
        name="single_solve",
    )(here, mask, *arrived, wh, wl)


def pack_kernel(*refs):
    by_place, by_layer = refs[:LAYER], refs[LAYER:]
    for d, out in enumerate(by_layer):
        for s in range(LAYER):
            out[s] = by_place[s][d]


def packed(by_place):
    layers, rows, lanes = by_place[0].shape
    return pl.pallas_call(
        pack_kernel,
        in_specs=[VMEM] * LAYER,
        out_specs=[VMEM] * layers,
        out_shape=[jax.ShapeDtypeStruct((LAYER, rows, lanes), jnp.float32)] * layers,
        compiler_params=pltpu.CompilerParams(vmem_limit_bytes=8 * 2**20),
        name="pack",
    )(*by_place)


def place_kernel(here_ref, x_ref, *rest):
    arrived, out_ref = rest[:-1], rest[-1]
    layers = len(arrived)
    layer, place_ = here_ref[0] // LAYER, here_ref[0] % LAYER
    for p in range(x_ref.shape[0]):
        q, b = p % LAYER, p // LAYER
        for i in range(BULK):
            out_ref[3 * q + i, :, b * LANES : (b + 1) * LANES] = x_ref[p, i]
    for d in range(layers):
        block = (layer + layers - d) % layers
        lanes = pl.ds(pl.multiple_of(block * LANES, LANES), LANES)
        for s in range(LAYER):
            out_ref[3 * (place_ ^ s) + BULK, :, lanes] = arrived[d][s]


def place(here, x, arrived, shape):
    return pl.pallas_call(
        place_kernel,
        in_specs=[SMEM] + [VMEM] * (1 + len(arrived)),
        out_specs=VMEM,
        out_shape=jax.ShapeDtypeStruct(shape, jnp.float32),
        compiler_params=pltpu.CompilerParams(vmem_limit_bytes=16 * 2**20),
        name="place",
    )(here, x, *arrived)


def swapped(x):
    return lax.all_to_all(x, "pencil", split_axis=0, concat_axis=0, tiled=True)


def moved(by_place):
    groups = lax.axis_size("pencil")
    by_place = [
        lax.ppermute(x, "pencil", [(i, i ^ s) for i in range(groups)]) if s else x for s, x in enumerate(by_place)
    ]
    return [
        lax.ppermute(x, "pencil", [(i, (i + LAYER * d) % groups) for i in range(groups)]) if d else x
        for d, x in enumerate(packed(by_place))
    ]


def on_device(t, u, v, w, downstream_solver_matrix, wallward_solver_matrices, wall_segments):
    planes, rows, nx = t.shape
    slabs, groups = lax.axis_size("slab"), lax.axis_size("pencil")
    here = lax.axis_index("pencil").astype(jnp.int32).reshape(1)
    up = [(i, i + 1) for i in range(groups - 1)]
    down = [(i + 1, i) for i in range(groups - 1)]
    y_first, y_last, z_low, z_high, mask = edges(here, wall_segments, t)
    halos = (
        lax.ppermute(y_last, "slab", [(i, (i + 1) % slabs) for i in range(slabs)]),
        lax.ppermute(y_first, "slab", [((i + 1) % slabs, i) for i in range(slabs)]),
        lax.ppermute(z_high, "pencil", up),
        lax.ppermute(z_low, "pencil", down),
    )
    ah, al, wh, wl, metric = prepare(here, downstream_solver_matrix, wallward_solver_matrices, rows)
    bulk, *single = row_solve(here, t, u, v, w, halos, metric, ah, al, groups)
    single = single_solve(here, mask, moved(single), wh, wl)
    bulk = swapped(column_solve(mask, swapped(bulk), wh, wl, single[0]))
    return place(here, bulk, moved(single), t.shape)


def solution(mesh):
    field = P("slab", "pencil", None)
    return jax.shard_map(
        on_device,
        mesh=mesh,
        in_specs=(field, field, field, field, P(), P(), P()),
        out_specs=field,
        check_vma=False,
    )
```

```python
import jax
import jax.numpy as jnp
from jax import lax
from jax.experimental import pallas as pl
from jax.experimental.pallas import tpu as pltpu
from jax.sharding import PartitionSpec as P

TRANSPORT_PART = 0.25
CONDUCTION_PART = 0.2
LANES = 128
EDGE = 53
PREP = 46
VMEM = pl.BlockSpec(memory_space=pltpu.VMEM)
HBM = pl.BlockSpec(memory_space=pltpu.HBM)
SMEM = pl.BlockSpec(memory_space=pltpu.SMEM)


def metric_of(levels, extent):
    return 0.5 / (1.0 + jnp.sin(jnp.pi * (levels + 0.5) / extent))


def halves(wide):
    high = wide.astype(jnp.bfloat16)
    return high, (wide - high.astype(jnp.float32)).astype(jnp.bfloat16)


def edge_kernel(here_ref, t_hbm, yc_ref, yd_ref, za_ref, zb_ref, buf, sems):
    planes, rows, _ = t_hbm.shape
    half = buf.shape[2]
    pencil_even, slab_even = here_ref[0] % 2 == 0, here_ref[1] % 2 == 0
    copies = [
        pltpu.make_async_copy(t_hbm.at[:, pl.ds(0, half)], buf.at[0], sems.at[0]),
        pltpu.make_async_copy(t_hbm.at[:, pl.ds(rows - half, half)], buf.at[1], sems.at[1]),
        pltpu.make_async_copy(t_hbm.at[jnp.where(slab_even, planes - 1, 0)], yc_ref, sems.at[2]),
        pltpu.make_async_copy(t_hbm.at[jnp.where(slab_even, 0, planes - 1)], yd_ref, sems.at[3]),
    ]
    for copy in copies:
        copy.start()
    copies[0].wait()
    copies[1].wait()
    for y in range(planes):
        low, high = buf[0, y, :1, :], buf[1, y, half - 1 :, :]
        za_ref[y : y + 1, :] = jnp.where(pencil_even, high, low)
        zb_ref[y : y + 1, :] = jnp.where(pencil_even, low, high)
    copies[2].wait()
    copies[3].wait()


def edges(here, t):
    planes, rows, nx = t.shape
    half = 8
    plane = jax.ShapeDtypeStruct((rows, nx), t.dtype)
    level = jax.ShapeDtypeStruct((planes, nx), t.dtype)
    return pl.pallas_call(
        edge_kernel,
        in_specs=[SMEM, HBM],
        out_specs=[VMEM] * 4,
        out_shape=[plane, plane, level, level],
        scratch_shapes=[pltpu.VMEM((2, planes, half, nx), t.dtype), pltpu.SemaphoreType.DMA((4,))],
        compiler_params=pltpu.CompilerParams(vmem_limit_bytes=EDGE * 2**20),
        name="edges",
    )(here, t)


def prepare_kernel(here_ref, a_hbm, ah_ref, al_ref, g_ref, a_buf, sems):
    parts = sems.shape[0]
    a_rows = a_buf.shape[0] // parts
    copies = []
    for i in range(parts):
        cut = slice(i * a_rows, (i + 1) * a_rows)
        copies.append(pltpu.make_async_copy(a_hbm.at[cut], a_buf.at[cut], sems.at[i]))
    for copy in copies:
        copy.start()
    rows, lanes = g_ref.shape
    levels = (lax.broadcasted_iota(jnp.int32, (rows, lanes), 0) + here_ref[0] * rows).astype(jnp.float32)
    g_ref[...] = metric_of(levels, (here_ref[2] * rows).astype(jnp.float32))
    for i in range(parts):
        cut = slice(i * a_rows, (i + 1) * a_rows)
        copies[i].wait()
        ah_ref[cut], al_ref[cut] = halves(a_buf[cut])


def prepare(here, a, rows):
    a16 = jax.ShapeDtypeStruct(a.shape, jnp.bfloat16)
    parts = 4
    return pl.pallas_call(
        prepare_kernel,
        in_specs=[SMEM, HBM],
        out_specs=[VMEM] * 3,
        out_shape=[a16, a16, jax.ShapeDtypeStruct((rows, LANES), jnp.float32)],
        scratch_shapes=[pltpu.VMEM(a.shape, a.dtype), pltpu.SemaphoreType.DMA((parts,))],
        compiler_params=pltpu.CompilerParams(vmem_limit_bytes=PREP * 2**20),
        cost_estimate=pl.CostEstimate(flops=4 * a.size, bytes_accessed=8 * a.size, transcendentals=0),
        name="prepare",
    )(here, a)


def row_kernel(
    here_ref, t_ref, u_ref, v_ref, w_ref, yc_ref, yd_ref, za_ref, zb_ref, g_ref, ah_ref, al_ref, out_ref, rh, rl
):
    planes, rows, nx = t_ref.shape
    metric = jnp.concatenate([g_ref[...]] * (nx // LANES), axis=1)
    pencil_even, slab_even = here_ref[0] % 2 == 0, here_ref[1] % 2 == 0
    over = jnp.where(pencil_even, za_ref[...], zb_ref[...])
    under = jnp.where(pencil_even, zb_ref[...], za_ref[...])
    level = lax.broadcasted_iota(jnp.int32, (rows, nx), 0)
    for y in range(planes):
        t = t_ref[y]
        ahead = t_ref[y + 1] if y + 1 < planes else jnp.where(slab_even, yc_ref[...], yd_ref[...])
        behind = t_ref[y - 1] if y else jnp.where(slab_even, yd_ref[...], yc_ref[...])
        east = pltpu.roll(t, nx - 1, 1)
        west = pltpu.roll(t, 1, 1)
        above = jnp.where(level == rows - 1, over[y : y + 1, :], pltpu.roll(t, rows - 1, 0))
        below = jnp.where(level == 0, under[y : y + 1, :], pltpu.roll(t, 1, 0))
        u = u_ref[y].astype(jnp.float32)
        v = v_ref[y].astype(jnp.float32)
        w = w_ref[y].astype(jnp.float32)
        carried = 0.5 * u * (east - west) + 0.5 * v * (ahead - behind) + w * metric * (above - below)
        conducted = (
            (ahead - 2.0 * t + behind)
            + 0.5 * (east - 2.0 * t + west)
            + 0.5 * metric * (above - 2.0 * t + below)
        )
        side = t - TRANSPORT_PART * carried + CONDUCTION_PART * conducted
        rh[y * rows : (y + 1) * rows, :], rl[y * rows : (y + 1) * rows, :] = halves(side)
    wide = 2 * LANES
    unit_rows = 3 * rows
    blocks = nx // LANES
    for c in range(nx // wide):
        ah = ah_ref[c * wide : (c + 1) * wide, :]
        al = al_ref[c * wide : (c + 1) * wide, :]

        def dot(x, m):
            return lax.dot_general(x, m, (((1,), (1,)), ((), ())), preferred_element_type=jnp.float32)

        solved = dot(rh[...], ah) + (dot(rh[...], al) + dot(rl[...], ah))
        for q in range(planes // 3):
            for h in range(2):
                piece = solved[q * unit_rows : (q + 1) * unit_rows, h * LANES : (h + 1) * LANES]
                out_ref[q * blocks + 2 * c + h] = piece.reshape(3, rows, LANES)


def row_solve(here, t, u, v, w, halos, metric, ah, al, groups):
    planes, rows, nx = t.shape
    return pl.pallas_call(
        row_kernel,
        in_specs=[SMEM] + [VMEM] * 11,
        out_specs=VMEM,
        out_shape=jax.ShapeDtypeStruct((groups, 3, rows, LANES), jnp.float32),
        scratch_shapes=[pltpu.VMEM((planes * rows, nx), jnp.bfloat16)] * 2,
        compiler_params=pltpu.CompilerParams(vmem_limit_bytes=32 * 2**20),
        cost_estimate=pl.CostEstimate(
            flops=6 * planes * rows * nx * nx, bytes_accessed=8 * 2**20, transcendentals=0
        ),
        name="row_solve",
    )(here, t, u, v, w, *halos, metric, ah, al)


def column_kernel(here_ref, seg_ref, w_ref, x_ref, out_ref):
    groups, units, rows, lanes = x_ref.shape
    column = lax.broadcasted_iota(jnp.int32, (8, lanes), 1) + here_ref[0] % here_ref[3] * lanes
    crossed = jnp.zeros((8, lanes), jnp.int32)
    end = jnp.int32(0)
    for s in range(seg_ref.shape[0]):
        end = end + seg_ref[s]
        crossed = crossed + jnp.where(column >= end, 1, 0)
    insulated = jnp.concatenate([(crossed % 2)[:1, :]] * units, axis=1) == 1
    extent = groups * rows
    lines = jnp.concatenate([x_ref[:, i].reshape(extent, lanes) for i in range(units)], axis=1)
    xh, xl = halves(lines)
    both = jnp.concatenate([xh, xl], axis=1)
    width = units * lanes

    def solve(c, lo, hi):
        wh, wl = halves(w_ref[c, lo:hi, :])
        d = jnp.dot(wh, both, preferred_element_type=jnp.float32)
        e = jnp.dot(wl, xh, preferred_element_type=jnp.float32)
        return d[:, :width] + (d[:, width:] + e)

    step = 128
    for k in range(0, extent, step):
        solved = jnp.where(insulated, solve(1, k, k + step), solve(0, k, k + step))
        for i in range(units):
            out_ref[k // rows : (k + step) // rows, i] = solved[:, i * lanes : (i + 1) * lanes].reshape(
                step // rows, rows, lanes
            )


def column_solve(here, segments, w, x):
    return pl.pallas_call(
        column_kernel,
        in_specs=[SMEM, SMEM, VMEM, VMEM],
        out_specs=VMEM,
        out_shape=jax.ShapeDtypeStruct(x.shape, jnp.float32),
        compiler_params=pltpu.CompilerParams(vmem_limit_bytes=32 * 2**20),
        cost_estimate=pl.CostEstimate(
            flops=12 * w.shape[1] * x.size, bytes_accessed=4 * 2**20, transcendentals=0
        ),
        name="column_solve",
    )(here, segments, w, x)


def place_kernel(x_ref, out_ref):
    groups = x_ref.shape[0]
    blocks = out_ref.shape[2] // LANES
    for p in range(groups):
        q, b = p // blocks, p % blocks
        out_ref[3 * q : 3 * q + 3, :, b * LANES : (b + 1) * LANES] = x_ref[p]


def place(x, shape):
    return pl.pallas_call(
        place_kernel,
        in_specs=[VMEM],
        out_specs=VMEM,
        out_shape=jax.ShapeDtypeStruct(shape, jnp.float32),
        compiler_params=pltpu.CompilerParams(vmem_limit_bytes=16 * 2**20),
        name="place",
    )(x)


def swapped(x):
    return lax.all_to_all(x, "pencil", split_axis=0, concat_axis=0, tiled=True)


def on_device(t, u, v, w, downstream_solver_matrix, wallward_solver_matrices, wall_segments):
    planes, rows, nx = t.shape
    slabs, groups = lax.axis_size("slab"), lax.axis_size("pencil")
    here = jnp.stack(
        [
            lax.axis_index("pencil").astype(jnp.int32),
            lax.axis_index("slab").astype(jnp.int32),
            jnp.int32(groups),
            jnp.int32(nx // LANES),
        ]
    )
    yc, yd, za, zb = edges(here, t)
    halos = (
        lax.ppermute(yc, "slab", [(i, i ^ 1) for i in range(slabs)]),
        lax.ppermute(yd, "slab", [(i, ((i - 1) ^ 1) + 1 & slabs - 1) for i in range(slabs)]),
        lax.ppermute(za, "pencil", [(i, i ^ 1) for i in range(groups)]),
        lax.ppermute(zb, "pencil", [(i, ((i - 1) ^ 1) + 1) for i in range(1, groups - 1)]),
    )
    ah, al, metric = prepare(here, downstream_solver_matrix, rows)
    x = swapped(row_solve(here, t, u, v, w, halos, metric, ah, al, groups))
    x = swapped(column_solve(here, wall_segments, wallward_solver_matrices, x))
    return place(x, t.shape)


def solution(mesh):
    field = P("slab", "pencil", None)
    return jax.shard_map(
        on_device,
        mesh=mesh,
        in_specs=(field, field, field, field, P(), P(), P()),
        out_specs=field,
        check_vma=False,
    )
```

```python
import functools

import jax
import jax.numpy as jnp
from jax import lax
from jax.experimental import pallas as pl
from jax.experimental.pallas import tpu as pltpu
from jax.sharding import PartitionSpec as P

TRANSPORT_PART = 0.25
CONDUCTION_PART = 0.2
LANES = 128
EDGE = 53
PREP = 46
VMEM = pl.BlockSpec(memory_space=pltpu.VMEM)
HBM = pl.BlockSpec(memory_space=pltpu.HBM)
SMEM = pl.BlockSpec(memory_space=pltpu.SMEM)


def metric_of(levels, extent):
    return 0.5 / (1.0 + jnp.sin(jnp.pi * (levels + 0.5) / extent))


def halves(wide):
    high = wide.astype(jnp.bfloat16)
    return high, (wide - high.astype(jnp.float32)).astype(jnp.bfloat16)


def edge_kernel(groups, here_ref, t_hbm, yc_ref, yd_ref, za_ref, zb_ref, buf, sems):
    planes, rows, _ = t_hbm.shape
    half = buf.shape[2]
    pencil_even, slab_even = here_ref[0] % 2 == 0, here_ref[0] // groups % 2 == 0
    copies = [
        pltpu.make_async_copy(t_hbm.at[:, pl.ds(0, half)], buf.at[0], sems.at[0]),
        pltpu.make_async_copy(t_hbm.at[:, pl.ds(rows - half, half)], buf.at[1], sems.at[1]),
        pltpu.make_async_copy(t_hbm.at[jnp.where(slab_even, planes - 1, 0)], yc_ref, sems.at[2]),
        pltpu.make_async_copy(t_hbm.at[jnp.where(slab_even, 0, planes - 1)], yd_ref, sems.at[3]),
    ]
    for copy in copies:
        copy.start()
    copies[0].wait()
    copies[1].wait()
    for y in range(planes):
        low, high = buf[0, y, :1, :], buf[1, y, half - 1 :, :]
        za_ref[y : y + 1, :] = jnp.where(pencil_even, high, low)
        zb_ref[y : y + 1, :] = jnp.where(pencil_even, low, high)
    copies[2].wait()
    copies[3].wait()


def edges(here, t, groups):
    planes, rows, nx = t.shape
    half = 8
    plane = jax.ShapeDtypeStruct((rows, nx), t.dtype)
    level = jax.ShapeDtypeStruct((planes, nx), t.dtype)
    return pl.pallas_call(
        functools.partial(edge_kernel, groups),
        in_specs=[SMEM, HBM],
        out_specs=[VMEM] * 4,
        out_shape=[plane, plane, level, level],
        scratch_shapes=[pltpu.VMEM((2, planes, half, nx), t.dtype), pltpu.SemaphoreType.DMA((4,))],
        compiler_params=pltpu.CompilerParams(vmem_limit_bytes=EDGE * 2**20),
        name="edges",
    )(here, t)


def prepare_kernel(groups, here_ref, a_hbm, ah_ref, al_ref, g_ref, a_buf, sems):
    parts = sems.shape[0]
    a_rows = a_buf.shape[0] // parts
    copies = []
    for i in range(parts):
        cut = slice(i * a_rows, (i + 1) * a_rows)
        copies.append(pltpu.make_async_copy(a_hbm.at[cut], a_buf.at[cut], sems.at[i]))
    for copy in copies:
        copy.start()
    rows, lanes = g_ref.shape
    levels = (lax.broadcasted_iota(jnp.int32, (rows, lanes), 0) + here_ref[0] % groups * rows).astype(jnp.float32)
    g_ref[...] = metric_of(levels, groups * rows)
    for i in range(parts):
        cut = slice(i * a_rows, (i + 1) * a_rows)
        copies[i].wait()
        ah_ref[cut], al_ref[cut] = halves(a_buf[cut])


def prepare(here, a, rows, groups):
    a16 = jax.ShapeDtypeStruct(a.shape, jnp.bfloat16)
    parts = 4
    return pl.pallas_call(
        functools.partial(prepare_kernel, groups),
        in_specs=[SMEM, HBM],
        out_specs=[VMEM] * 3,
        out_shape=[a16, a16, jax.ShapeDtypeStruct((rows, LANES), jnp.float32)],
        scratch_shapes=[pltpu.VMEM(a.shape, a.dtype), pltpu.SemaphoreType.DMA((parts,))],
        compiler_params=pltpu.CompilerParams(vmem_limit_bytes=PREP * 2**20),
        cost_estimate=pl.CostEstimate(flops=4 * a.size, bytes_accessed=8 * a.size, transcendentals=0),
        name="prepare",
    )(here, a)


def row_kernel(
    here_ref, t_ref, u_ref, v_ref, w_ref, yc_ref, yd_ref, za_ref, zb_ref, g_ref, ah_ref, al_ref, out_ref, rh, rl
):
    planes, rows, nx = t_ref.shape
    metric = jnp.concatenate([g_ref[...]] * (nx // LANES), axis=1)
    groups = out_ref.shape[0]
    pencil_even, slab_even = here_ref[0] % 2 == 0, here_ref[0] // groups % 2 == 0
    over = jnp.where(pencil_even, za_ref[...], zb_ref[...])
    under = jnp.where(pencil_even, zb_ref[...], za_ref[...])
    level = lax.broadcasted_iota(jnp.int32, (rows, nx), 0)
    for y in range(planes):
        t = t_ref[y]
        ahead = t_ref[y + 1] if y + 1 < planes else jnp.where(slab_even, yc_ref[...], yd_ref[...])
        behind = t_ref[y - 1] if y else jnp.where(slab_even, yd_ref[...], yc_ref[...])
        east = pltpu.roll(t, nx - 1, 1)
        west = pltpu.roll(t, 1, 1)
        above = jnp.where(level == rows - 1, over[y : y + 1, :], pltpu.roll(t, rows - 1, 0))
        below = jnp.where(level == 0, under[y : y + 1, :], pltpu.roll(t, 1, 0))
        u = u_ref[y].astype(jnp.float32)
        v = v_ref[y].astype(jnp.float32)
        w = w_ref[y].astype(jnp.float32)
        carried = 0.5 * u * (east - west) + 0.5 * v * (ahead - behind) + w * metric * (above - below)
        conducted = (
            (ahead - 2.0 * t + behind)
            + 0.5 * (east - 2.0 * t + west)
            + 0.5 * metric * (above - 2.0 * t + below)
        )
        side = t - TRANSPORT_PART * carried + CONDUCTION_PART * conducted
        rh[y * rows : (y + 1) * rows, :], rl[y * rows : (y + 1) * rows, :] = halves(side)
    wide = 2 * LANES
    unit_rows = 3 * rows
    blocks = nx // LANES
    for c in range(nx // wide):
        ah = ah_ref[c * wide : (c + 1) * wide, :]
        al = al_ref[c * wide : (c + 1) * wide, :]

        def dot(x, m):
            return lax.dot_general(x, m, (((1,), (1,)), ((), ())), preferred_element_type=jnp.float32)

        solved = dot(rh[...], ah) + (dot(rh[...], al) + dot(rl[...], ah))
        for q in range(planes // 3):
            for h in range(2):
                piece = solved[q * unit_rows : (q + 1) * unit_rows, h * LANES : (h + 1) * LANES]
                out_ref[q * blocks + 2 * c + h] = piece.reshape(3, rows, LANES)


def row_solve(here, t, u, v, w, halos, metric, ah, al, groups):
    planes, rows, nx = t.shape
    return pl.pallas_call(
        row_kernel,
        in_specs=[SMEM] + [VMEM] * 11,
        out_specs=VMEM,
        out_shape=jax.ShapeDtypeStruct((groups, 3, rows, LANES), jnp.float32),
        scratch_shapes=[pltpu.VMEM((planes * rows, nx), jnp.bfloat16)] * 2,
        compiler_params=pltpu.CompilerParams(vmem_limit_bytes=32 * 2**20),
        cost_estimate=pl.CostEstimate(
            flops=6 * planes * rows * nx * nx, bytes_accessed=8 * 2**20, transcendentals=0
        ),
        name="row_solve",
    )(here, t, u, v, w, *halos, metric, ah, al)


def column_kernel(blocks, here_ref, seg_ref, w_ref, x_ref, out_ref):
    groups, units, rows, lanes = x_ref.shape
    column = lax.broadcasted_iota(jnp.int32, (8, lanes), 1) + here_ref[0] % blocks * lanes
    crossed = jnp.zeros((8, lanes), jnp.int32)
    end = jnp.int32(0)
    for s in range(seg_ref.shape[0]):
        end = end + seg_ref[s]
        crossed = crossed + jnp.where(column >= end, 1, 0)
    insulated = jnp.concatenate([(crossed % 2)[:1, :]] * units, axis=1) == 1
    extent = groups * rows
    lines = jnp.concatenate([x_ref[:, i].reshape(extent, lanes) for i in range(units)], axis=1)
    xh, xl = halves(lines)
    both = jnp.concatenate([xh, xl], axis=1)
    width = units * lanes

    def solve(c, lo, hi):
        wh, wl = halves(w_ref[c, lo:hi, :])
        d = jnp.dot(wh, both, preferred_element_type=jnp.float32)
        e = jnp.dot(wl, xh, preferred_element_type=jnp.float32)
        return d[:, :width] + (d[:, width:] + e)

    step = 128
    for k in range(0, extent, step):
        solved = jnp.where(insulated, solve(1, k, k + step), solve(0, k, k + step))
        for i in range(units):
            out_ref[k // rows : (k + step) // rows, i] = solved[:, i * lanes : (i + 1) * lanes].reshape(
                step // rows, rows, lanes
            )


def column_solve(here, segments, w, x, blocks):
    return pl.pallas_call(
        functools.partial(column_kernel, blocks),
        in_specs=[SMEM, SMEM, VMEM, VMEM],
        out_specs=VMEM,
        out_shape=jax.ShapeDtypeStruct(x.shape, jnp.float32),
        compiler_params=pltpu.CompilerParams(vmem_limit_bytes=32 * 2**20),
        cost_estimate=pl.CostEstimate(
            flops=12 * w.shape[1] * x.size, bytes_accessed=4 * 2**20, transcendentals=0
        ),
        name="column_solve",
    )(here, segments, w, x)


def place_kernel(x_ref, out_ref):
    groups = x_ref.shape[0]
    blocks = out_ref.shape[2] // LANES
    for p in range(groups):
        q, b = p // blocks, p % blocks
        out_ref[3 * q : 3 * q + 3, :, b * LANES : (b + 1) * LANES] = x_ref[p]


def place(x, shape):
    return pl.pallas_call(
        place_kernel,
        in_specs=[VMEM],
        out_specs=VMEM,
        out_shape=jax.ShapeDtypeStruct(shape, jnp.float32),
        compiler_params=pltpu.CompilerParams(vmem_limit_bytes=16 * 2**20),
        name="place",
    )(x)


def swapped(x):
    return lax.all_to_all(x, "pencil", split_axis=0, concat_axis=0, tiled=True)


def on_device(t, u, v, w, downstream_solver_matrix, wallward_solver_matrices, wall_segments):
    planes, rows, nx = t.shape
    slabs, groups = lax.axis_size("slab"), lax.axis_size("pencil")
    here = lax.axis_index(("slab", "pencil")).astype(jnp.int32).reshape(1)
    yc, yd, za, zb = edges(here, t, groups)
    halos = (
        lax.ppermute(yc, "slab", [(i, i ^ 1) for i in range(slabs)]),
        lax.ppermute(yd, "slab", [(i, ((i - 1) ^ 1) + 1 & slabs - 1) for i in range(slabs)]),
        lax.ppermute(za, "pencil", [(i, i ^ 1) for i in range(groups)]),
        lax.ppermute(zb, "pencil", [(i, ((i - 1) ^ 1) + 1) for i in range(1, groups - 1)]),
    )
    ah, al, metric = prepare(here, downstream_solver_matrix, rows, groups)
    x = swapped(row_solve(here, t, u, v, w, halos, metric, ah, al, groups))
    x = swapped(column_solve(here, wall_segments, wallward_solver_matrices, x, nx // LANES))
    return place(x, t.shape)


def solution(mesh):
    field = P("slab", "pencil", None)
    return jax.shard_map(
        on_device,
        mesh=mesh,
        in_specs=(field, field, field, field, P(), P(), P()),
        out_specs=field,
        check_vma=False,
    )
```

```python
import functools

import jax
import jax.numpy as jnp
from jax import lax
from jax.experimental import pallas as pl
from jax.experimental.pallas import tpu as pltpu
from jax.sharding import PartitionSpec as P

TRANSPORT_PART = 0.25
CONDUCTION_PART = 0.2
LANES = 128
VMEM = pl.BlockSpec(memory_space=pltpu.VMEM)
HBM = pl.BlockSpec(memory_space=pltpu.HBM)
SMEM = pl.BlockSpec(memory_space=pltpu.SMEM)


def metric_of(levels, extent):
    return 0.5 / (1.0 + jnp.sin(jnp.pi * (levels + 0.5) / extent))


def pinned(x):
    return pltpu.with_memory_space_constraint(x, pltpu.HBM)


def halves(wide):
    high = wide.astype(jnp.bfloat16)
    return high, (wide - high.astype(jnp.float32)).astype(jnp.bfloat16)


def edge_kernel(groups, here_ref, t_hbm, yc_ref, yd_ref, za_ref, zb_ref, buf, sems):
    planes, rows, _ = t_hbm.shape
    half = buf.shape[2]
    pencil_even, slab_even = here_ref[0] % 2 == 0, here_ref[0] // groups % 2 == 0
    copies = [
        pltpu.make_async_copy(t_hbm.at[:, pl.ds(0, half)], buf.at[0], sems.at[0]),
        pltpu.make_async_copy(t_hbm.at[:, pl.ds(rows - half, half)], buf.at[1], sems.at[1]),
        pltpu.make_async_copy(t_hbm.at[jnp.where(slab_even, planes - 1, 0)], yc_ref, sems.at[2]),
        pltpu.make_async_copy(t_hbm.at[jnp.where(slab_even, 0, planes - 1)], yd_ref, sems.at[3]),
    ]
    for copy in copies:
        copy.start()
    copies[0].wait()
    copies[1].wait()
    for y in range(planes):
        low, high = buf[0, y, :1, :], buf[1, y, half - 1 :, :]
        za_ref[y : y + 1, :] = jnp.where(pencil_even, high, low)
        zb_ref[y : y + 1, :] = jnp.where(pencil_even, low, high)
    copies[2].wait()
    copies[3].wait()


def edges(here, t, groups):
    planes, rows, nx = t.shape
    half = 8
    plane = jax.ShapeDtypeStruct((rows, nx), t.dtype)
    level = jax.ShapeDtypeStruct((planes, nx), t.dtype)
    return pl.pallas_call(
        functools.partial(edge_kernel, groups),
        in_specs=[SMEM, HBM],
        out_specs=[VMEM] * 4,
        out_shape=[plane, plane, level, level],
        scratch_shapes=[pltpu.VMEM((2, planes, half, nx), t.dtype), pltpu.SemaphoreType.DMA((4,))],
        compiler_params=pltpu.CompilerParams(vmem_limit_bytes=8 * 2**20),
        name="edges",
    )(here, pinned(t))


def prepare_kernel(
    groups,
    here_ref,
    t_hbm,
    u_hbm,
    v_hbm,
    w_hbm,
    a_hbm,
    side_ref,
    cb_ref,
    ca_ref,
    cl_ref,
    ch_ref,
    ah_ref,
    al_ref,
    t_ref,
    u_ref,
    v_ref,
    w_ref,
    a_buf,
    sems,
):
    planes, rows, nx = t_ref.shape
    parts = sems.shape[0] - 4
    a_rows = a_buf.shape[0] // parts
    fields = [
        pltpu.make_async_copy(source, target, sems.at[i])
        for i, (source, target) in enumerate(((t_hbm, t_ref), (u_hbm, u_ref), (v_hbm, v_ref), (w_hbm, w_ref)))
    ]
    copies = []
    for i in range(parts):
        cut = slice(i * a_rows, (i + 1) * a_rows)
        copies.append(pltpu.make_async_copy(a_hbm.at[cut], a_buf.at[cut], sems.at[4 + i]))
    for copy in fields + copies:
        copy.start()
    levels = (lax.broadcasted_iota(jnp.int32, (rows, LANES), 0) + here_ref[0] % groups * rows).astype(jnp.float32)
    metric = jnp.concatenate([metric_of(levels, groups * rows)] * (nx // LANES), axis=1)
    level = lax.broadcasted_iota(jnp.int32, (rows, nx), 0)
    for copy in fields:
        copy.wait()
    for y in range(planes):
        t = t_ref[y]
        ahead = t_ref[y + 1] if y + 1 < planes else jnp.zeros_like(t)
        behind = t_ref[y - 1] if y else jnp.zeros_like(t)
        east = pltpu.roll(t, nx - 1, 1)
        west = pltpu.roll(t, 1, 1)
        above = jnp.where(level == rows - 1, 0.0, pltpu.roll(t, rows - 1, 0))
        below = jnp.where(level == 0, 0.0, pltpu.roll(t, 1, 0))
        u = u_ref[y].astype(jnp.float32)
        v = v_ref[y].astype(jnp.float32)
        w = w_ref[y].astype(jnp.float32)
        carried = 0.5 * u * (east - west) + 0.5 * v * (ahead - behind) + w * metric * (above - below)
        conducted = (
            (ahead - 2.0 * t + behind)
            + 0.5 * (east - 2.0 * t + west)
            + 0.5 * metric * (above - 2.0 * t + below)
        )
        side_ref[y] = t - TRANSPORT_PART * carried + CONDUCTION_PART * conducted
        cl_ref[y : y + 1, :] = (metric * (0.5 * CONDUCTION_PART + TRANSPORT_PART * w))[:1, :]
        ch_ref[y : y + 1, :] = (metric * (0.5 * CONDUCTION_PART - TRANSPORT_PART * w))[rows - 1 :, :]
        if y == 0:
            cb_ref[...] = CONDUCTION_PART + 0.5 * TRANSPORT_PART * v
        if y == planes - 1:
            ca_ref[...] = CONDUCTION_PART - 0.5 * TRANSPORT_PART * v
    for i in range(parts):
        cut = slice(i * a_rows, (i + 1) * a_rows)
        copies[i].wait()
        ah_ref[cut], al_ref[cut] = halves(a_buf[cut])


def prepare(here, t, u, v, w, a, groups):
    planes, rows, nx = t.shape
    a16 = jax.ShapeDtypeStruct(a.shape, jnp.bfloat16)
    plane = jax.ShapeDtypeStruct((rows, nx), t.dtype)
    level = jax.ShapeDtypeStruct((planes, nx), t.dtype)
    parts = 4
    return pl.pallas_call(
        functools.partial(prepare_kernel, groups),
        in_specs=[SMEM] + [HBM] * 5,
        out_specs=[VMEM] * 7,
        out_shape=[jax.ShapeDtypeStruct(t.shape, t.dtype), plane, plane, level, level, a16, a16],
        scratch_shapes=[pltpu.VMEM(x.shape, x.dtype) for x in (t, u, v, w, a)]
        + [pltpu.SemaphoreType.DMA((4 + parts,))],
        compiler_params=pltpu.CompilerParams(vmem_limit_bytes=16 * 2**20),
        cost_estimate=pl.CostEstimate(
            flops=4 * a.size + 40 * t.size, bytes_accessed=8 * a.size + 14 * t.size, transcendentals=0
        ),
        name="prepare",
    )(here, *(pinned(x) for x in (t, u, v, w, a)))


def row_kernel(
    here_ref, side_ref, cb_ref, ca_ref, cl_ref, ch_ref, yc_ref, yd_ref, za_ref, zb_ref, ah_ref, al_ref, out_ref, rh, rl
):
    planes, rows, nx = side_ref.shape
    groups = out_ref.shape[0]
    pencil_even, slab_even = here_ref[0] % 2 == 0, here_ref[0] // groups % 2 == 0
    low = cl_ref[...] * jnp.where(pencil_even, zb_ref[...], za_ref[...])
    high = ch_ref[...] * jnp.where(pencil_even, za_ref[...], zb_ref[...])
    level = lax.broadcasted_iota(jnp.int32, (rows, nx), 0)
    for y in range(planes):
        side = side_ref[y]
        if y == 0:
            side = side + cb_ref[...] * jnp.where(slab_even, yd_ref[...], yc_ref[...])
        if y == planes - 1:
            side = side + ca_ref[...] * jnp.where(slab_even, yc_ref[...], yd_ref[...])
        side = side + jnp.where(level == 0, low[y : y + 1, :], 0.0)
        side = side + jnp.where(level == rows - 1, high[y : y + 1, :], 0.0)
        rh[y * rows : (y + 1) * rows, :], rl[y * rows : (y + 1) * rows, :] = halves(side)
    wide = 2 * LANES
    unit_rows = 3 * rows
    blocks = nx // LANES
    for c in range(nx // wide):
        ah = ah_ref[c * wide : (c + 1) * wide, :]
        al = al_ref[c * wide : (c + 1) * wide, :]

        def dot(x, m):
            return lax.dot_general(x, m, (((1,), (1,)), ((), ())), preferred_element_type=jnp.float32)

        solved = dot(rh[...], ah) + (dot(rh[...], al) + dot(rl[...], ah))
        for q in range(planes // 3):
            for h in range(2):
                piece = solved[q * unit_rows : (q + 1) * unit_rows, h * LANES : (h + 1) * LANES]
                out_ref[q * blocks + 2 * c + h] = piece.reshape(3, rows, LANES)


def row_solve(here, parts, halos, ah, al, groups):
    planes, rows, nx = parts[0].shape
    return pl.pallas_call(
        row_kernel,
        in_specs=[SMEM] + [VMEM] * 11,
        out_specs=VMEM,
        out_shape=jax.ShapeDtypeStruct((groups, 3, rows, LANES), jnp.float32),
        scratch_shapes=[pltpu.VMEM((planes * rows, nx), jnp.bfloat16)] * 2,
        compiler_params=pltpu.CompilerParams(vmem_limit_bytes=32 * 2**20),
        cost_estimate=pl.CostEstimate(
            flops=6 * planes * rows * nx * nx, bytes_accessed=8 * 2**20, transcendentals=0
        ),
        name="row_solve",
    )(here, *parts, *halos, ah, al)


def column_kernel(blocks, here_ref, seg_ref, w_ref, x_ref, out_ref):
    groups, units, rows, lanes = x_ref.shape
    column = lax.broadcasted_iota(jnp.int32, (8, lanes), 1) + here_ref[0] % blocks * lanes
    crossed = jnp.zeros((8, lanes), jnp.int32)
    end = jnp.int32(0)
    for s in range(seg_ref.shape[0]):
        end = end + seg_ref[s]
        crossed = crossed + jnp.where(column >= end, 1, 0)
    insulated = jnp.concatenate([(crossed % 2)[:1, :]] * units, axis=1) == 1
    extent = groups * rows
    lines = jnp.concatenate([x_ref[:, i].reshape(extent, lanes) for i in range(units)], axis=1)
    xh, xl = halves(lines)
    both = jnp.concatenate([xh, xl], axis=1)
    width = units * lanes

    def solve(c, lo, hi):
        wh, wl = halves(w_ref[c, lo:hi, :])
        d = jnp.dot(wh, both, preferred_element_type=jnp.float32)
        e = jnp.dot(wl, xh, preferred_element_type=jnp.float32)
        return d[:, :width] + (d[:, width:] + e)

    step = 128
    for k in range(0, extent, step):
        solved = jnp.where(insulated, solve(1, k, k + step), solve(0, k, k + step))
        for i in range(units):
            out_ref[k // rows : (k + step) // rows, i] = solved[:, i * lanes : (i + 1) * lanes].reshape(
                step // rows, rows, lanes
            )


def column_solve(here, segments, w, x, blocks):
    return pl.pallas_call(
        functools.partial(column_kernel, blocks),
        in_specs=[SMEM, SMEM, VMEM, VMEM],
        out_specs=VMEM,
        out_shape=jax.ShapeDtypeStruct(x.shape, jnp.float32),
        compiler_params=pltpu.CompilerParams(vmem_limit_bytes=32 * 2**20),
        cost_estimate=pl.CostEstimate(
            flops=12 * w.shape[1] * x.size, bytes_accessed=4 * 2**20, transcendentals=0
        ),
        name="column_solve",
    )(here, segments, w, x)


def place_kernel(x_ref, out_ref):
    groups = x_ref.shape[0]
    blocks = out_ref.shape[2] // LANES
    for p in range(groups):
        q, b = p // blocks, p % blocks
        out_ref[3 * q : 3 * q + 3, :, b * LANES : (b + 1) * LANES] = x_ref[p]


def place(x, shape):
    return pl.pallas_call(
        place_kernel,
        in_specs=[VMEM],
        out_specs=VMEM,
        out_shape=jax.ShapeDtypeStruct(shape, jnp.float32),
        compiler_params=pltpu.CompilerParams(vmem_limit_bytes=16 * 2**20),
        name="place",
    )(x)


def swapped(x):
    return lax.all_to_all(x, "pencil", split_axis=0, concat_axis=0, tiled=True)


def on_device(t, u, v, w, downstream_solver_matrix, wallward_solver_matrices, wall_segments):
    planes, rows, nx = t.shape
    slabs, groups = lax.axis_size("slab"), lax.axis_size("pencil")
    here = lax.axis_index(("slab", "pencil")).astype(jnp.int32).reshape(1)
    yc, yd, za, zb = edges(here, t, groups)
    halos = (
        lax.ppermute(yc, "slab", [(i, i ^ 1) for i in range(slabs)]),
        lax.ppermute(yd, "slab", [(i, ((i - 1) ^ 1) + 1 & slabs - 1) for i in range(slabs)]),
        lax.ppermute(za, "pencil", [(i, i ^ 1) for i in range(groups)]),
        lax.ppermute(zb, "pencil", [(i, ((i - 1) ^ 1) + 1) for i in range(1, groups - 1)]),
    )
    *parts, ah, al = prepare(here, t, u, v, w, downstream_solver_matrix, groups)
    x = swapped(row_solve(here, parts, halos, ah, al, groups))
    x = swapped(column_solve(here, wall_segments, wallward_solver_matrices, x, nx // LANES))
    return place(x, t.shape)


def solution(mesh):
    field = P("slab", "pencil", None)
    return jax.shard_map(
        on_device,
        mesh=mesh,
        in_specs=(field, field, field, field, P(), P(), P()),
        out_specs=field,
        check_vma=False,
    )
```

```python
import functools

import jax
import jax.numpy as jnp
from jax import lax
from jax.experimental import pallas as pl
from jax.experimental.pallas import tpu as pltpu
from jax.sharding import PartitionSpec as P

TRANSPORT_PART = 0.25
CONDUCTION_PART = 0.2
LANES = 128
VMEM = pl.BlockSpec(memory_space=pltpu.VMEM)
HBM = pl.BlockSpec(memory_space=pltpu.HBM)
SMEM = pl.BlockSpec(memory_space=pltpu.SMEM)


def metric_of(levels, extent):
    return 0.5 / (1.0 + jnp.sin(jnp.pi * (levels + 0.5) / extent))


def pinned(x):
    return pltpu.with_memory_space_constraint(x, pltpu.HBM)


def halves(wide):
    high = wide.astype(jnp.bfloat16)
    return high, (wide - high.astype(jnp.float32)).astype(jnp.bfloat16)


def edge_kernel(groups, here_ref, t_hbm, yc_ref, yd_ref, za_ref, zb_ref, buf, sems):
    planes, rows, _ = t_hbm.shape
    half = buf.shape[2]
    pencil_even, slab_even = here_ref[0] % 2 == 0, here_ref[0] // groups % 2 == 0
    copies = [
        pltpu.make_async_copy(t_hbm.at[:, pl.ds(0, half)], buf.at[0], sems.at[0]),
        pltpu.make_async_copy(t_hbm.at[:, pl.ds(rows - half, half)], buf.at[1], sems.at[1]),
        pltpu.make_async_copy(t_hbm.at[jnp.where(slab_even, planes - 1, 0)], yc_ref, sems.at[2]),
        pltpu.make_async_copy(t_hbm.at[jnp.where(slab_even, 0, planes - 1)], yd_ref, sems.at[3]),
    ]
    for copy in copies:
        copy.start()
    copies[0].wait()
    copies[1].wait()
    for y in range(planes):
        low, high = buf[0, y, :1, :], buf[1, y, half - 1 :, :]
        za_ref[y : y + 1, :] = jnp.where(pencil_even, low, high)
        zb_ref[y : y + 1, :] = jnp.where(pencil_even, high, low)
    copies[2].wait()
    copies[3].wait()


def edges(here, t, groups):
    planes, rows, nx = t.shape
    half = rows // 2
    plane = jax.ShapeDtypeStruct((rows, nx), t.dtype)
    level = jax.ShapeDtypeStruct((planes, nx), t.dtype)
    return pl.pallas_call(
        functools.partial(edge_kernel, groups),
        in_specs=[SMEM, HBM],
        out_specs=[VMEM] * 5,
        out_shape=[plane, plane, level, level, jax.ShapeDtypeStruct((2, planes, half, nx), t.dtype)],
        scratch_shapes=[pltpu.SemaphoreType.DMA((4,))],
        compiler_params=pltpu.CompilerParams(vmem_limit_bytes=8 * 2**20),
        name="edges",
    )(here, pinned(t))


def prepare_kernel(
    groups,
    here_ref,
    t_ref,
    u_hbm,
    v_hbm,
    w_hbm,
    a_hbm,
    side_ref,
    cb_ref,
    ca_ref,
    cl_ref,
    ch_ref,
    ah_ref,
    al_ref,
    u_ref,
    v_ref,
    w_ref,
    a_buf,
    sems,
):
    planes, rows, nx = side_ref.shape
    parts = sems.shape[0] - 3
    a_rows = a_buf.shape[0] // parts
    fields = [
        pltpu.make_async_copy(source, target, sems.at[i])
        for i, (source, target) in enumerate(((u_hbm, u_ref), (v_hbm, v_ref), (w_hbm, w_ref)))
    ]
    copies = []
    for i in range(parts):
        cut = slice(i * a_rows, (i + 1) * a_rows)
        copies.append(pltpu.make_async_copy(a_hbm.at[cut], a_buf.at[cut], sems.at[3 + i]))
    for copy in fields:
        copy.start()
    levels = (lax.broadcasted_iota(jnp.int32, (rows, LANES), 0) + here_ref[0] % groups * rows).astype(jnp.float32)
    metric = jnp.concatenate([metric_of(levels, groups * rows)] * (nx // LANES), axis=1)
    level = lax.broadcasted_iota(jnp.int32, (rows, nx), 0)
    for copy in fields:
        copy.wait()
    for copy in copies:
        copy.start()

    def plane(y):
        if y < 0 or y == planes:
            return jnp.zeros((rows, nx), jnp.float32)
        return jnp.concatenate([t_ref[0, y], t_ref[1, y]], axis=0)

    for y in range(planes):
        t, ahead, behind = plane(y), plane(y + 1), plane(y - 1)
        east = pltpu.roll(t, nx - 1, 1)
        west = pltpu.roll(t, 1, 1)
        above = jnp.where(level == rows - 1, 0.0, pltpu.roll(t, rows - 1, 0))
        below = jnp.where(level == 0, 0.0, pltpu.roll(t, 1, 0))
        u = u_ref[y].astype(jnp.float32)
        v = v_ref[y].astype(jnp.float32)
        w = w_ref[y].astype(jnp.float32)
        carried = 0.5 * u * (east - west) + 0.5 * v * (ahead - behind) + w * metric * (above - below)
        conducted = (
            (ahead - 2.0 * t + behind)
            + 0.5 * (east - 2.0 * t + west)
            + 0.5 * metric * (above - 2.0 * t + below)
        )
        side_ref[y] = t - TRANSPORT_PART * carried + CONDUCTION_PART * conducted
        cl_ref[y : y + 1, :] = (metric * (0.5 * CONDUCTION_PART + TRANSPORT_PART * w))[:1, :]
        ch_ref[y : y + 1, :] = (metric * (0.5 * CONDUCTION_PART - TRANSPORT_PART * w))[rows - 1 :, :]
        if y == 0:
            cb_ref[...] = CONDUCTION_PART + 0.5 * TRANSPORT_PART * v
        if y == planes - 1:
            ca_ref[...] = CONDUCTION_PART - 0.5 * TRANSPORT_PART * v
    for i in range(parts):
        cut = slice(i * a_rows, (i + 1) * a_rows)
        copies[i].wait()
        ah_ref[cut], al_ref[cut] = halves(a_buf[cut])


def prepare(here, t, u, v, w, a, groups):
    planes, rows, nx = u.shape
    a16 = jax.ShapeDtypeStruct(a.shape, jnp.bfloat16)
    plane = jax.ShapeDtypeStruct((rows, nx), t.dtype)
    level = jax.ShapeDtypeStruct((planes, nx), t.dtype)
    parts = 4
    return pl.pallas_call(
        functools.partial(prepare_kernel, groups),
        in_specs=[SMEM, VMEM] + [HBM] * 4,
        out_specs=[VMEM] * 7,
        out_shape=[jax.ShapeDtypeStruct(u.shape, t.dtype), plane, plane, level, level, a16, a16],
        scratch_shapes=[pltpu.VMEM(x.shape, x.dtype) for x in (u, v, w, a)]
        + [pltpu.SemaphoreType.DMA((3 + parts,))],
        compiler_params=pltpu.CompilerParams(vmem_limit_bytes=16 * 2**20),
        cost_estimate=pl.CostEstimate(
            flops=4 * a.size + 40 * t.size, bytes_accessed=8 * a.size + 14 * t.size, transcendentals=0
        ),
        name="prepare",
    )(here, t, *(pinned(x) for x in (u, v, w, a)))


def row_kernel(
    here_ref, side_ref, cb_ref, ca_ref, cl_ref, ch_ref, yc_ref, yd_ref, za_ref, zb_ref, ah_ref, al_ref, out_ref, both
):
    planes, rows, nx = side_ref.shape
    groups = out_ref.shape[0]
    pencil_even, slab_even = here_ref[0] % 2 == 0, here_ref[0] // groups % 2 == 0
    low = cl_ref[...] * jnp.where(pencil_even, za_ref[...], zb_ref[...])
    high = ch_ref[...] * jnp.where(pencil_even, zb_ref[...], za_ref[...])
    level = lax.broadcasted_iota(jnp.int32, (rows, nx), 0)
    extent = planes * rows
    for y in range(planes):
        side = side_ref[y]
        if y == 0:
            side = side + cb_ref[...] * jnp.where(slab_even, yd_ref[...], yc_ref[...])
        if y == planes - 1:
            side = side + ca_ref[...] * jnp.where(slab_even, yc_ref[...], yd_ref[...])
        side = side + jnp.where(level == 0, low[y : y + 1, :], 0.0)
        side = side + jnp.where(level == rows - 1, high[y : y + 1, :], 0.0)
        high_part, low_part = halves(side)
        both[y * rows : (y + 1) * rows, :] = high_part
        both[extent + y * rows : extent + (y + 1) * rows, :] = low_part
    wide = 2 * LANES
    unit_rows = 3 * rows
    blocks = nx // LANES
    for c in range(nx // wide):
        ah = ah_ref[c * wide : (c + 1) * wide, :]
        al = al_ref[c * wide : (c + 1) * wide, :]

        def dot(x, m):
            return lax.dot_general(x, m, (((1,), (1,)), ((), ())), preferred_element_type=jnp.float32)

        main = dot(both[...], ah)
        solved = main[:extent] + (dot(both[:extent, :], al) + main[extent:])
        for q in range(planes // 3):
            for h in range(2):
                piece = solved[q * unit_rows : (q + 1) * unit_rows, h * LANES : (h + 1) * LANES]
                out_ref[q * blocks + 2 * c + h] = piece.reshape(3, rows, LANES)


def row_solve(here, parts, halos, ah, al, groups):
    planes, rows, nx = parts[0].shape
    return pl.pallas_call(
        row_kernel,
        in_specs=[SMEM] + [VMEM] * 11,
        out_specs=VMEM,
        out_shape=jax.ShapeDtypeStruct((groups, 3, rows, LANES), jnp.float32),
        scratch_shapes=[pltpu.VMEM((2 * planes * rows, nx), jnp.bfloat16)],
        compiler_params=pltpu.CompilerParams(vmem_limit_bytes=32 * 2**20),
        cost_estimate=pl.CostEstimate(
            flops=6 * planes * rows * nx * nx, bytes_accessed=8 * 2**20, transcendentals=0
        ),
        name="row_solve",
    )(here, *parts, *halos, ah, al)


def column_kernel(blocks, here_ref, seg_ref, w_ref, x_ref, out_ref):
    groups, units, rows, lanes = x_ref.shape
    column = lax.broadcasted_iota(jnp.int32, (8, lanes), 1) + here_ref[0] % blocks * lanes
    crossed = jnp.zeros((8, lanes), jnp.int32)
    end = jnp.int32(0)
    for s in range(seg_ref.shape[0]):
        end = end + seg_ref[s]
        crossed = crossed + jnp.where(column >= end, 1, 0)
    insulated = jnp.concatenate([(crossed % 2)[:1, :]] * units, axis=1) == 1
    extent = groups * rows
    lines = jnp.concatenate([x_ref[:, i].reshape(extent, lanes) for i in range(units)], axis=1)
    xh, xl = halves(lines)
    both = jnp.concatenate([xh, xl], axis=1)
    width = units * lanes

    def solve(c):
        wh, wl = halves(w_ref[c])
        d = jnp.dot(wh, both, preferred_element_type=jnp.float32)
        e = jnp.dot(wl, xh, preferred_element_type=jnp.float32)
        return d[:, :width] + (d[:, width:] + e)

    solved = jnp.where(insulated, solve(1), solve(0))
    for i in range(units):
        out_ref[:, i] = solved[:, i * lanes : (i + 1) * lanes].reshape(groups, rows, lanes)


def column_solve(here, segments, w, x, blocks):
    return pl.pallas_call(
        functools.partial(column_kernel, blocks),
        in_specs=[SMEM, SMEM, VMEM, VMEM],
        out_specs=VMEM,
        out_shape=jax.ShapeDtypeStruct(x.shape, jnp.float32),
        compiler_params=pltpu.CompilerParams(vmem_limit_bytes=32 * 2**20),
        cost_estimate=pl.CostEstimate(
            flops=12 * w.shape[1] * x.size, bytes_accessed=4 * 2**20, transcendentals=0
        ),
        name="column_solve",
    )(here, segments, w, x)


def place_kernel(x_ref, out_hbm, sems):
    groups, units, _, lanes = x_ref.shape
    blocks = out_hbm.shape[2] // lanes
    copies = []
    for p in range(groups):
        q, b = p // blocks, p % blocks
        target = out_hbm.at[pl.ds(units * q, units), :, pl.ds(b * lanes, lanes)]
        copies.append(pltpu.make_async_copy(x_ref.at[p], target, sems.at[p]))
    for copy in copies:
        copy.start()
    for copy in copies:
        copy.wait()


def place(x, shape):
    return pl.pallas_call(
        place_kernel,
        in_specs=[VMEM],
        out_specs=HBM,
        out_shape=jax.ShapeDtypeStruct(shape, jnp.float32),
        scratch_shapes=[pltpu.SemaphoreType.DMA((x.shape[0],))],
        compiler_params=pltpu.CompilerParams(vmem_limit_bytes=16 * 2**20),
        name="place",
    )(x)


def swapped(x):
    return lax.all_to_all(x, "pencil", split_axis=0, concat_axis=0, tiled=True)


def on_device(t, u, v, w, downstream_solver_matrix, wallward_solver_matrices, wall_segments):
    planes, rows, nx = t.shape
    slabs, groups = lax.axis_size("slab"), lax.axis_size("pencil")
    here = lax.axis_index(("slab", "pencil")).astype(jnp.int32).reshape(1)
    yc, yd, za, zb, t_halves = edges(here, t, groups)
    yc = lax.ppermute(yc, "slab", [(i, i ^ 1) for i in range(slabs)])
    yd = lax.ppermute(yd, "slab", [(i, ((i - 1) ^ 1) + 1 & slabs - 1) for i in range(slabs)])
    za = lax.ppermute(za, "pencil", [(i, ((i - 1) ^ 1) + 1) for i in range(1, groups - 1)])
    zb = lax.ppermute(zb, "pencil", [(i, i ^ 1) for i in range(groups)])
    halos = yc, yd, za, zb
    *parts, ah, al = prepare(here, t_halves, u, v, w, downstream_solver_matrix, groups)
    x = swapped(row_solve(here, parts, halos, ah, al, groups))
    x = swapped(column_solve(here, wall_segments, wallward_solver_matrices, x, nx // LANES))
    return place(x, t.shape)


def solution(mesh):
    field = P("slab", "pencil", None)
    return jax.shard_map(
        on_device,
        mesh=mesh,
        in_specs=(field, field, field, field, P(), P(), P()),
        out_specs=field,
        check_vma=False,
    )
```

```python
import functools

import jax
import jax.numpy as jnp
from jax import lax
from jax.experimental import pallas as pl
from jax.experimental.pallas import tpu as pltpu
from jax.sharding import PartitionSpec as P

TRANSPORT_PART = 0.25
CONDUCTION_PART = 0.2
LANES = 128
VMEM = pl.BlockSpec(memory_space=pltpu.VMEM)
HBM = pl.BlockSpec(memory_space=pltpu.HBM)
SMEM = pl.BlockSpec(memory_space=pltpu.SMEM)


def metric_of(levels, extent):
    return 0.5 / (1.0 + jnp.sin(jnp.pi * (levels + 0.5) / extent))


def pinned(x):
    return pltpu.with_memory_space_constraint(x, pltpu.HBM)


def halves(wide):
    high = wide.astype(jnp.bfloat16)
    return high, (wide - high.astype(jnp.float32)).astype(jnp.bfloat16)


def edge_kernel(groups, here_ref, t_hbm, yc_ref, yd_ref, za_ref, zb_ref, buf, sems):
    planes, rows, _ = t_hbm.shape
    half = buf.shape[2]
    pencil_even, slab_even = here_ref[0] % 2 == 0, here_ref[0] // groups % 2 == 0
    copies = [
        pltpu.make_async_copy(t_hbm.at[:, pl.ds(0, half)], buf.at[0], sems.at[0]),
        pltpu.make_async_copy(t_hbm.at[:, pl.ds(rows - half, half)], buf.at[1], sems.at[1]),
        pltpu.make_async_copy(t_hbm.at[jnp.where(slab_even, planes - 1, 0)], yc_ref, sems.at[2]),
        pltpu.make_async_copy(t_hbm.at[jnp.where(slab_even, 0, planes - 1)], yd_ref, sems.at[3]),
    ]
    for copy in copies:
        copy.start()
    copies[0].wait()
    copies[1].wait()
    for y in range(planes):
        low, high = buf[0, y, :1, :], buf[1, y, half - 1 :, :]
        za_ref[y : y + 1, :] = jnp.where(pencil_even, low, high)
        zb_ref[y : y + 1, :] = jnp.where(pencil_even, high, low)
    copies[2].wait()
    copies[3].wait()


def edges(here, t, groups):
    planes, rows, nx = t.shape
    half = rows // 2
    plane = jax.ShapeDtypeStruct((rows, nx), t.dtype)
    level = jax.ShapeDtypeStruct((planes, nx), t.dtype)
    return pl.pallas_call(
        functools.partial(edge_kernel, groups),
        in_specs=[SMEM, HBM],
        out_specs=[VMEM] * 5,
        out_shape=[plane, plane, level, level, jax.ShapeDtypeStruct((2, planes, half, nx), t.dtype)],
        scratch_shapes=[pltpu.SemaphoreType.DMA((4,))],
        compiler_params=pltpu.CompilerParams(vmem_limit_bytes=8 * 2**20),
        name="edges",
    )(here, pinned(t))


def prepare_kernel(
    groups,
    here_ref,
    t_ref,
    u_hbm,
    v_hbm,
    w_hbm,
    a_hbm,
    side_ref,
    cb_ref,
    ca_ref,
    cl_ref,
    ch_ref,
    ah_ref,
    al_ref,
    u_ref,
    v_ref,
    w_ref,
    a_buf,
    sems,
):
    planes, rows, nx = side_ref.shape
    parts = sems.shape[0] - 3
    a_rows = a_buf.shape[0] // parts
    fields = [
        pltpu.make_async_copy(source, target, sems.at[i])
        for i, (source, target) in enumerate(((u_hbm, u_ref), (v_hbm, v_ref), (w_hbm, w_ref)))
    ]
    copies = []
    for i in range(parts):
        cut = slice(i * a_rows, (i + 1) * a_rows)
        copies.append(pltpu.make_async_copy(a_hbm.at[cut], a_buf.at[cut], sems.at[3 + i]))
    for copy in fields + copies:
        copy.start()
    levels = (lax.broadcasted_iota(jnp.int32, (rows, LANES), 0) + here_ref[0] % groups * rows).astype(jnp.float32)
    metric = jnp.concatenate([metric_of(levels, groups * rows)] * (nx // LANES), axis=1)
    level = lax.broadcasted_iota(jnp.int32, (rows, nx), 0)
    for copy in fields:
        copy.wait()

    def plane(y):
        if y < 0 or y == planes:
            return jnp.zeros((rows, nx), jnp.float32)
        return jnp.concatenate([t_ref[0, y], t_ref[1, y]], axis=0)

    for y in range(planes):
        t, ahead, behind = plane(y), plane(y + 1), plane(y - 1)
        east = pltpu.roll(t, nx - 1, 1)
        west = pltpu.roll(t, 1, 1)
        above = jnp.where(level == rows - 1, 0.0, pltpu.roll(t, rows - 1, 0))
        below = jnp.where(level == 0, 0.0, pltpu.roll(t, 1, 0))
        u = u_ref[y].astype(jnp.float32)
        v = v_ref[y].astype(jnp.float32)
        w = w_ref[y].astype(jnp.float32)
        carried = 0.5 * u * (east - west) + 0.5 * v * (ahead - behind) + w * metric * (above - below)
        conducted = (
            (ahead - 2.0 * t + behind)
            + 0.5 * (east - 2.0 * t + west)
            + 0.5 * metric * (above - 2.0 * t + below)
        )
        side_ref[y] = t - TRANSPORT_PART * carried + CONDUCTION_PART * conducted
        cl_ref[y : y + 1, :] = (metric * (0.5 * CONDUCTION_PART + TRANSPORT_PART * w))[:1, :]
        ch_ref[y : y + 1, :] = (metric * (0.5 * CONDUCTION_PART - TRANSPORT_PART * w))[rows - 1 :, :]
        if y == 0:
            cb_ref[...] = CONDUCTION_PART + 0.5 * TRANSPORT_PART * v
        if y == planes - 1:
            ca_ref[...] = CONDUCTION_PART - 0.5 * TRANSPORT_PART * v
    for i in range(parts):
        cut = slice(i * a_rows, (i + 1) * a_rows)
        copies[i].wait()
        ah_ref[cut], al_ref[cut] = halves(a_buf[cut])


def prepare(here, t, u, v, w, a, groups):
    planes, rows, nx = u.shape
    a16 = jax.ShapeDtypeStruct(a.shape, jnp.bfloat16)
    plane = jax.ShapeDtypeStruct((rows, nx), t.dtype)
    level = jax.ShapeDtypeStruct((planes, nx), t.dtype)
    parts = 4
    return pl.pallas_call(
        functools.partial(prepare_kernel, groups),
        in_specs=[SMEM, VMEM] + [HBM] * 4,
        out_specs=[VMEM] * 7,
        out_shape=[jax.ShapeDtypeStruct(u.shape, t.dtype), plane, plane, level, level, a16, a16],
        scratch_shapes=[pltpu.VMEM(x.shape, x.dtype) for x in (u, v, w, a)]
        + [pltpu.SemaphoreType.DMA((3 + parts,))],
        compiler_params=pltpu.CompilerParams(vmem_limit_bytes=16 * 2**20),
        cost_estimate=pl.CostEstimate(
            flops=4 * a.size + 40 * t.size, bytes_accessed=8 * a.size + 14 * t.size, transcendentals=0
        ),
        name="prepare",
    )(here, t, *(pinned(x) for x in (u, v, w, a)))


def row_kernel(
    here_ref, side_ref, cb_ref, ca_ref, cl_ref, ch_ref, yc_ref, yd_ref, za_ref, zb_ref, ah_ref, al_ref, out_ref, both
):
    planes, rows, nx = side_ref.shape
    groups = out_ref.shape[0]
    pencil_even, slab_even = here_ref[0] % 2 == 0, here_ref[0] // groups % 2 == 0
    low = cl_ref[...] * jnp.where(pencil_even, za_ref[...], zb_ref[...])
    high = ch_ref[...] * jnp.where(pencil_even, zb_ref[...], za_ref[...])
    level = lax.broadcasted_iota(jnp.int32, (rows, nx), 0)
    extent = planes * rows
    for y in range(planes):
        side = side_ref[y]
        if y == 0:
            side = side + cb_ref[...] * jnp.where(slab_even, yd_ref[...], yc_ref[...])
        if y == planes - 1:
            side = side + ca_ref[...] * jnp.where(slab_even, yc_ref[...], yd_ref[...])
        side = side + jnp.where(level == 0, low[y : y + 1, :], 0.0)
        side = side + jnp.where(level == rows - 1, high[y : y + 1, :], 0.0)
        high_part, low_part = halves(side)
        both[y * rows : (y + 1) * rows, :] = high_part
        both[extent + y * rows : extent + (y + 1) * rows, :] = low_part
    wide = 2 * LANES
    unit_rows = 3 * rows
    blocks = nx // LANES
    for c in range(nx // wide):
        ah = ah_ref[c * wide : (c + 1) * wide, :]
        al = al_ref[c * wide : (c + 1) * wide, :]

        def dot(x, m):
            return lax.dot_general(x, m, (((1,), (1,)), ((), ())), preferred_element_type=jnp.float32)

        main = dot(both[...], ah)
        solved = main[:extent] + (dot(both[:extent, :], al) + main[extent:])
        for q in range(planes // 3):
            for h in range(2):
                piece = solved[q * unit_rows : (q + 1) * unit_rows, h * LANES : (h + 1) * LANES]
                out_ref[q * blocks + 2 * c + h] = piece.reshape(3, rows, LANES)


def row_solve(here, parts, halos, ah, al, groups):
    planes, rows, nx = parts[0].shape
    return pl.pallas_call(
        row_kernel,
        in_specs=[SMEM] + [VMEM] * 11,
        out_specs=VMEM,
        out_shape=jax.ShapeDtypeStruct((groups, 3, rows, LANES), jnp.float32),
        scratch_shapes=[pltpu.VMEM((2 * planes * rows, nx), jnp.bfloat16)],
        compiler_params=pltpu.CompilerParams(vmem_limit_bytes=32 * 2**20),
        cost_estimate=pl.CostEstimate(
            flops=6 * planes * rows * nx * nx, bytes_accessed=8 * 2**20, transcendentals=0
        ),
        name="row_solve",
    )(here, *parts, *halos, ah, al)


def column_kernel(blocks, here_ref, seg_ref, w_ref, x_ref, out_ref):
    groups, units, rows, lanes = x_ref.shape
    column = lax.broadcasted_iota(jnp.int32, (8, lanes), 1) + here_ref[0] % blocks * lanes
    crossed = jnp.zeros((8, lanes), jnp.int32)
    end = jnp.int32(0)
    for s in range(seg_ref.shape[0]):
        end = end + seg_ref[s]
        crossed = crossed + jnp.where(column >= end, 1, 0)
    insulated = jnp.concatenate([(crossed % 2)[:1, :]] * units, axis=1) == 1
    extent = groups * rows
    lines = jnp.concatenate([x_ref[:, i].reshape(extent, lanes) for i in range(units)], axis=1)
    xh, xl = halves(lines)
    both = jnp.concatenate([xh, xl], axis=1)
    width = units * lanes

    def solve(c):
        wh, wl = halves(w_ref[c])
        d = jnp.dot(wh, both, preferred_element_type=jnp.float32)
        e = jnp.dot(wl, xh, preferred_element_type=jnp.float32)
        return d[:, :width] + (d[:, width:] + e)

    solved = jnp.where(insulated, solve(1), solve(0))
    for i in range(units):
        out_ref[:, i] = solved[:, i * lanes : (i + 1) * lanes].reshape(groups, rows, lanes)


def column_solve(here, segments, w, x, blocks):
    return pl.pallas_call(
        functools.partial(column_kernel, blocks),
        in_specs=[SMEM, SMEM, VMEM, VMEM],
        out_specs=VMEM,
        out_shape=jax.ShapeDtypeStruct(x.shape, jnp.float32),
        compiler_params=pltpu.CompilerParams(vmem_limit_bytes=32 * 2**20),
        cost_estimate=pl.CostEstimate(
            flops=12 * w.shape[1] * x.size, bytes_accessed=4 * 2**20, transcendentals=0
        ),
        name="column_solve",
    )(here, segments, w, x)


def place_kernel(x_ref, out_ref):
    groups = x_ref.shape[0]
    blocks = out_ref.shape[2] // LANES
    for p in range(groups):
        q, b = p // blocks, p % blocks
        out_ref[3 * q : 3 * q + 3, :, b * LANES : (b + 1) * LANES] = x_ref[p]


def place(x, shape):
    return pl.pallas_call(
        place_kernel,
        in_specs=[VMEM],
        out_specs=VMEM,
        out_shape=jax.ShapeDtypeStruct(shape, jnp.float32),
        compiler_params=pltpu.CompilerParams(vmem_limit_bytes=16 * 2**20),
        name="place",
    )(x)


def swapped(x):
    return lax.all_to_all(x, "pencil", split_axis=0, concat_axis=0, tiled=True)


def on_device(t, u, v, w, downstream_solver_matrix, wallward_solver_matrices, wall_segments):
    planes, rows, nx = t.shape
    slabs, groups = lax.axis_size("slab"), lax.axis_size("pencil")
    here = lax.axis_index(("slab", "pencil")).astype(jnp.int32).reshape(1)
    yc, yd, za, zb, t_halves = edges(here, t, groups)
    yc = lax.ppermute(yc, "slab", [(i, i ^ 1) for i in range(slabs)])
    yd = lax.ppermute(yd, "slab", [(i, ((i - 1) ^ 1) + 1 & slabs - 1) for i in range(slabs)])
    za = lax.ppermute(za, "pencil", [(i, ((i - 1) ^ 1) + 1) for i in range(1, groups - 1)])
    zb = lax.ppermute(zb, "pencil", [(i, i ^ 1) for i in range(groups)])
    halos = yc, yd, za, zb
    *parts, ah, al = prepare(here, t_halves, u, v, w, downstream_solver_matrix, groups)
    x = swapped(row_solve(here, parts, halos, ah, al, groups))
    x = swapped(column_solve(here, wall_segments, wallward_solver_matrices, x, nx // LANES))
    return place(x, t.shape)


def solution(mesh):
    field = P("slab", "pencil", None)
    return jax.shard_map(
        on_device,
        mesh=mesh,
        in_specs=(field, field, field, field, P(), P(), P()),
        out_specs=field,
        check_vma=False,
    )
```

```python
import functools

import jax
import jax.numpy as jnp
from jax import lax
from jax.experimental import pallas as pl
from jax.experimental.pallas import tpu as pltpu
from jax.sharding import PartitionSpec as P

TRANSPORT_PART = 0.25
CONDUCTION_PART = 0.2
LANES = 128
VMEM = pl.BlockSpec(memory_space=pltpu.VMEM)
HBM = pl.BlockSpec(memory_space=pltpu.HBM)
SMEM = pl.BlockSpec(memory_space=pltpu.SMEM)


def metric_of(levels, extent):
    return 0.5 / (1.0 + jnp.sin(jnp.pi * (levels + 0.5) / extent))


def pinned(x):
    return pltpu.with_memory_space_constraint(x, pltpu.HBM)


def halves(wide):
    high = wide.astype(jnp.bfloat16)
    return high, (wide - high.astype(jnp.float32)).astype(jnp.bfloat16)


def edge_kernel(groups, here_ref, t_hbm, yc_ref, yd_ref, za_ref, zb_ref, buf, sems):
    planes, rows, _ = t_hbm.shape
    half = buf.shape[2]
    pencil_even, slab_even = here_ref[0] % 2 == 0, here_ref[0] // groups % 2 == 0
    copies = [
        pltpu.make_async_copy(t_hbm.at[:, pl.ds(0, half)], buf.at[0], sems.at[0]),
        pltpu.make_async_copy(t_hbm.at[:, pl.ds(rows - half, half)], buf.at[1], sems.at[1]),
        pltpu.make_async_copy(t_hbm.at[jnp.where(slab_even, planes - 1, 0)], yc_ref, sems.at[2]),
        pltpu.make_async_copy(t_hbm.at[jnp.where(slab_even, 0, planes - 1)], yd_ref, sems.at[3]),
    ]
    for copy in copies:
        copy.start()
    copies[0].wait()
    copies[1].wait()
    for y in range(planes):
        low, high = buf[0, y, :1, :], buf[1, y, half - 1 :, :]
        za_ref[y : y + 1, :] = jnp.where(pencil_even, low, high)
        zb_ref[y : y + 1, :] = jnp.where(pencil_even, high, low)
    copies[2].wait()
    copies[3].wait()


def edges(here, t, groups):
    planes, rows, nx = t.shape
    half = rows // 2
    plane = jax.ShapeDtypeStruct((rows, nx), t.dtype)
    level = jax.ShapeDtypeStruct((planes, nx), t.dtype)
    return pl.pallas_call(
        functools.partial(edge_kernel, groups),
        in_specs=[SMEM, HBM],
        out_specs=[VMEM] * 5,
        out_shape=[plane, plane, level, level, jax.ShapeDtypeStruct((2, planes, half, nx), t.dtype)],
        scratch_shapes=[pltpu.SemaphoreType.DMA((4,))],
        compiler_params=pltpu.CompilerParams(vmem_limit_bytes=8 * 2**20),
        name="edges",
    )(here, pinned(t))


def prepare_kernel(
    groups,
    here_ref,
    t_ref,
    u_hbm,
    v_hbm,
    w_hbm,
    a_hbm,
    side_ref,
    cb_ref,
    ca_ref,
    cl_ref,
    ch_ref,
    ah_ref,
    al_ref,
    u_ref,
    v_ref,
    w_ref,
    a_buf,
    sems,
):
    planes, rows, nx = side_ref.shape
    parts = sems.shape[0] - 3
    a_rows = a_buf.shape[0] // parts
    fields = [
        pltpu.make_async_copy(source, target, sems.at[i])
        for i, (source, target) in enumerate(((u_hbm, u_ref), (v_hbm, v_ref), (w_hbm, w_ref)))
    ]
    copies = []
    for i in range(parts):
        cut = slice(i * a_rows, (i + 1) * a_rows)
        copies.append(pltpu.make_async_copy(a_hbm.at[cut], a_buf.at[cut], sems.at[3 + i]))
    for copy in fields + copies:
        copy.start()
    levels = (lax.broadcasted_iota(jnp.int32, (rows, LANES), 0) + here_ref[0] % groups * rows).astype(jnp.float32)
    metric = jnp.concatenate([metric_of(levels, groups * rows)] * (nx // LANES), axis=1)
    level = lax.broadcasted_iota(jnp.int32, (rows, nx), 0)
    for copy in fields:
        copy.wait()

    def plane(y):
        if y < 0 or y == planes:
            return jnp.zeros((rows, nx), jnp.float32)
        return jnp.concatenate([t_ref[0, y], t_ref[1, y]], axis=0)

    for y in range(planes):
        t, ahead, behind = plane(y), plane(y + 1), plane(y - 1)
        east = pltpu.roll(t, nx - 1, 1)
        west = pltpu.roll(t, 1, 1)
        above = jnp.where(level == rows - 1, 0.0, pltpu.roll(t, rows - 1, 0))
        below = jnp.where(level == 0, 0.0, pltpu.roll(t, 1, 0))
        u = u_ref[y].astype(jnp.float32)
        v = v_ref[y].astype(jnp.float32)
        w = w_ref[y].astype(jnp.float32)
        carried = 0.5 * u * (east - west) + 0.5 * v * (ahead - behind) + w * metric * (above - below)
        conducted = (
            (ahead - 2.0 * t + behind)
            + 0.5 * (east - 2.0 * t + west)
            + 0.5 * metric * (above - 2.0 * t + below)
        )
        side_ref[y] = t - TRANSPORT_PART * carried + CONDUCTION_PART * conducted
        cl_ref[y : y + 1, :] = (metric * (0.5 * CONDUCTION_PART + TRANSPORT_PART * w))[:1, :]
        ch_ref[y : y + 1, :] = (metric * (0.5 * CONDUCTION_PART - TRANSPORT_PART * w))[rows - 1 :, :]
        if y == 0:
            cb_ref[...] = CONDUCTION_PART + 0.5 * TRANSPORT_PART * v
        if y == planes - 1:
            ca_ref[...] = CONDUCTION_PART - 0.5 * TRANSPORT_PART * v
    for i in range(parts):
        cut = slice(i * a_rows, (i + 1) * a_rows)
        copies[i].wait()
        ah_ref[cut], al_ref[cut] = halves(a_buf[cut])


def prepare(here, t, u, v, w, a, groups):
    planes, rows, nx = u.shape
    half = (a.shape[0] // 2, a.shape[1])
    a16 = jax.ShapeDtypeStruct(half, jnp.bfloat16)
    plane = jax.ShapeDtypeStruct((rows, nx), t.dtype)
    level = jax.ShapeDtypeStruct((planes, nx), t.dtype)
    parts = 2
    return pl.pallas_call(
        functools.partial(prepare_kernel, groups),
        in_specs=[SMEM, VMEM] + [HBM] * 4,
        out_specs=[VMEM] * 7,
        out_shape=[jax.ShapeDtypeStruct(u.shape, t.dtype), plane, plane, level, level, a16, a16],
        scratch_shapes=[pltpu.VMEM(x.shape, x.dtype) for x in (u, v, w)]
        + [pltpu.VMEM(half, a.dtype), pltpu.SemaphoreType.DMA((3 + parts,))],
        compiler_params=pltpu.CompilerParams(vmem_limit_bytes=16 * 2**20),
        cost_estimate=pl.CostEstimate(
            flops=2 * a.size + 40 * t.size, bytes_accessed=4 * a.size + 14 * t.size, transcendentals=0
        ),
        name="prepare",
    )(here, t, *(pinned(x) for x in (u, v, w, a)))


def row_kernel(
    here_ref,
    side_ref,
    cb_ref,
    ca_ref,
    cl_ref,
    ch_ref,
    yc_ref,
    yd_ref,
    za_ref,
    zb_ref,
    ah_ref,
    al_ref,
    a_hbm,
    out_ref,
    both,
    a_buf,
    sems,
):
    planes, rows, nx = side_ref.shape
    wide = 2 * LANES
    ready = ah_ref.shape[0] // wide
    copies = []
    for c in range(sems.shape[0]):
        source = a_hbm.at[pl.ds((ready + c) * wide, wide)]
        copies.append(pltpu.make_async_copy(source, a_buf.at[pl.ds(c * wide, wide)], sems.at[c]))
    for copy in copies:
        copy.start()
    groups = out_ref.shape[0]
    pencil_even, slab_even = here_ref[0] % 2 == 0, here_ref[0] // groups % 2 == 0
    low = cl_ref[...] * jnp.where(pencil_even, za_ref[...], zb_ref[...])
    high = ch_ref[...] * jnp.where(pencil_even, zb_ref[...], za_ref[...])
    level = lax.broadcasted_iota(jnp.int32, (rows, nx), 0)
    extent = planes * rows
    for y in range(planes):
        side = side_ref[y]
        if y == 0:
            side = side + cb_ref[...] * jnp.where(slab_even, yd_ref[...], yc_ref[...])
        if y == planes - 1:
            side = side + ca_ref[...] * jnp.where(slab_even, yc_ref[...], yd_ref[...])
        side = side + jnp.where(level == 0, low[y : y + 1, :], 0.0)
        side = side + jnp.where(level == rows - 1, high[y : y + 1, :], 0.0)
        high_part, low_part = halves(side)
        both[y * rows : (y + 1) * rows, :] = high_part
        both[extent + y * rows : extent + (y + 1) * rows, :] = low_part
    unit_rows = 3 * rows
    blocks = nx // LANES
    for c in range(nx // wide):
        if c < ready:
            ah, al = ah_ref[c * wide : (c + 1) * wide, :], al_ref[c * wide : (c + 1) * wide, :]
        else:
            copies[c - ready].wait()
            ah, al = halves(a_buf[(c - ready) * wide : (c - ready + 1) * wide, :])

        def dot(x, m):
            return lax.dot_general(x, m, (((1,), (1,)), ((), ())), preferred_element_type=jnp.float32)

        main = dot(both[...], ah)
        solved = main[:extent] + (dot(both[:extent, :], al) + main[extent:])
        for q in range(planes // 3):
            for h in range(2):
                piece = solved[q * unit_rows : (q + 1) * unit_rows, h * LANES : (h + 1) * LANES]
                out_ref[q * blocks + 2 * c + h] = piece.reshape(3, rows, LANES)


def row_solve(here, parts, halos, ah, al, a, groups):
    planes, rows, nx = parts[0].shape
    return pl.pallas_call(
        row_kernel,
        in_specs=[SMEM] + [VMEM] * 11 + [HBM],
        out_specs=VMEM,
        out_shape=jax.ShapeDtypeStruct((groups, 3, rows, LANES), jnp.float32),
        scratch_shapes=[
            pltpu.VMEM((2 * planes * rows, nx), jnp.bfloat16),
            pltpu.VMEM((nx - ah.shape[0], nx), a.dtype),
            pltpu.SemaphoreType.DMA(((nx - ah.shape[0]) // (2 * LANES),)),
        ],
        compiler_params=pltpu.CompilerParams(vmem_limit_bytes=32 * 2**20),
        cost_estimate=pl.CostEstimate(
            flops=6 * planes * rows * nx * nx, bytes_accessed=8 * 2**20, transcendentals=0
        ),
        name="row_solve",
    )(here, *parts, *halos, ah, al, pinned(a))


def column_kernel(blocks, here_ref, seg_ref, w_ref, x_ref, out_ref):
    groups, units, rows, lanes = x_ref.shape
    column = lax.broadcasted_iota(jnp.int32, (8, lanes), 1) + here_ref[0] % blocks * lanes
    crossed = jnp.zeros((8, lanes), jnp.int32)
    end = jnp.int32(0)
    for s in range(seg_ref.shape[0]):
        end = end + seg_ref[s]
        crossed = crossed + jnp.where(column >= end, 1, 0)
    insulated = jnp.concatenate([(crossed % 2)[:1, :]] * units, axis=1) == 1
    extent = groups * rows
    lines = jnp.concatenate([x_ref[:, i].reshape(extent, lanes) for i in range(units)], axis=1)
    xh, xl = halves(lines)
    both = jnp.concatenate([xh, xl], axis=1)
    width = units * lanes

    def solve(c):
        wh, wl = halves(w_ref[c])
        d = jnp.dot(wh, both, preferred_element_type=jnp.float32)
        e = jnp.dot(wl, xh, preferred_element_type=jnp.float32)
        return d[:, :width] + (d[:, width:] + e)

    solved = jnp.where(insulated, solve(1), solve(0))
    for i in range(units):
        out_ref[:, i] = solved[:, i * lanes : (i + 1) * lanes].reshape(groups, rows, lanes)


def column_solve(here, segments, w, x, blocks):
    return pl.pallas_call(
        functools.partial(column_kernel, blocks),
        in_specs=[SMEM, SMEM, VMEM, VMEM],
        out_specs=VMEM,
        out_shape=jax.ShapeDtypeStruct(x.shape, jnp.float32),
        compiler_params=pltpu.CompilerParams(vmem_limit_bytes=32 * 2**20),
        cost_estimate=pl.CostEstimate(
            flops=12 * w.shape[1] * x.size, bytes_accessed=4 * 2**20, transcendentals=0
        ),
        name="column_solve",
    )(here, segments, w, x)


def place_kernel(x_ref, out_ref):
    groups = x_ref.shape[0]
    blocks = out_ref.shape[2] // LANES
    for p in range(groups):
        q, b = p // blocks, p % blocks
        out_ref[3 * q : 3 * q + 3, :, b * LANES : (b + 1) * LANES] = x_ref[p]


def place(x, shape):
    return pl.pallas_call(
        place_kernel,
        in_specs=[VMEM],
        out_specs=VMEM,
        out_shape=jax.ShapeDtypeStruct(shape, jnp.float32),
        compiler_params=pltpu.CompilerParams(vmem_limit_bytes=16 * 2**20),
        name="place",
    )(x)


def swapped(x):
    return lax.all_to_all(x, "pencil", split_axis=0, concat_axis=0, tiled=True)


def on_device(t, u, v, w, downstream_solver_matrix, wallward_solver_matrices, wall_segments):
    planes, rows, nx = t.shape
    slabs, groups = lax.axis_size("slab"), lax.axis_size("pencil")
    here = lax.axis_index(("slab", "pencil")).astype(jnp.int32).reshape(1)
    yc, yd, za, zb, t_halves = edges(here, t, groups)
    yc = lax.ppermute(yc, "slab", [(i, i ^ 1) for i in range(slabs)])
    yd = lax.ppermute(yd, "slab", [(i, ((i - 1) ^ 1) + 1 & slabs - 1) for i in range(slabs)])
    za = lax.ppermute(za, "pencil", [(i, ((i - 1) ^ 1) + 1) for i in range(1, groups - 1)])
    zb = lax.ppermute(zb, "pencil", [(i, i ^ 1) for i in range(groups)])
    halos = yc, yd, za, zb
    *parts, ah, al = prepare(here, t_halves, u, v, w, downstream_solver_matrix, groups)
    x = swapped(row_solve(here, parts, halos, ah, al, downstream_solver_matrix, groups))
    x = swapped(column_solve(here, wall_segments, wallward_solver_matrices, x, nx // LANES))
    return place(x, t.shape)


def solution(mesh):
    field = P("slab", "pencil", None)
    return jax.shard_map(
        on_device,
        mesh=mesh,
        in_specs=(field, field, field, field, P(), P(), P()),
        out_specs=field,
        check_vma=False,
    )
```

```python
import functools

import jax
import jax.numpy as jnp
from jax import lax
from jax.experimental import pallas as pl
from jax.experimental.pallas import tpu as pltpu
from jax.sharding import PartitionSpec as P

TRANSPORT_PART = 0.25
CONDUCTION_PART = 0.2
LANES = 128
VMEM = pl.BlockSpec(memory_space=pltpu.VMEM)
HBM = pl.BlockSpec(memory_space=pltpu.HBM)
SMEM = pl.BlockSpec(memory_space=pltpu.SMEM)


def metric_of(levels, extent):
    return 0.5 / (1.0 + jnp.sin(jnp.pi * (levels + 0.5) / extent))


def pinned(x):
    return pltpu.with_memory_space_constraint(x, pltpu.HBM)


def halves(wide):
    high = wide.astype(jnp.bfloat16)
    return high, (wide - high.astype(jnp.float32)).astype(jnp.bfloat16)


def edge_kernel(groups, here_ref, t_hbm, yc_ref, yd_ref, za_ref, zb_ref, buf, sems):
    planes, rows, _ = t_hbm.shape
    half = buf.shape[2]
    pencil_even, slab_even = here_ref[0] % 2 == 0, here_ref[0] // groups % 2 == 0
    copies = [
        pltpu.make_async_copy(t_hbm.at[:, pl.ds(0, half)], buf.at[0], sems.at[0]),
        pltpu.make_async_copy(t_hbm.at[:, pl.ds(rows - half, half)], buf.at[1], sems.at[1]),
        pltpu.make_async_copy(t_hbm.at[jnp.where(slab_even, planes - 1, 0)], yc_ref, sems.at[2]),
        pltpu.make_async_copy(t_hbm.at[jnp.where(slab_even, 0, planes - 1)], yd_ref, sems.at[3]),
    ]
    for copy in copies:
        copy.start()
    copies[0].wait()
    copies[1].wait()
    for y in range(planes):
        low, high = buf[0, y, :1, :], buf[1, y, half - 1 :, :]
        za_ref[y : y + 1, :] = jnp.where(pencil_even, low, high)
        zb_ref[y : y + 1, :] = jnp.where(pencil_even, high, low)
    copies[2].wait()
    copies[3].wait()


def edges(here, t, groups):
    planes, rows, nx = t.shape
    half = rows // 2
    plane = jax.ShapeDtypeStruct((rows, nx), t.dtype)
    level = jax.ShapeDtypeStruct((planes, nx), t.dtype)
    return pl.pallas_call(
        functools.partial(edge_kernel, groups),
        in_specs=[SMEM, HBM],
        out_specs=[VMEM] * 5,
        out_shape=[plane, plane, level, level, jax.ShapeDtypeStruct((2, planes, half, nx), t.dtype)],
        scratch_shapes=[pltpu.SemaphoreType.DMA((4,))],
        compiler_params=pltpu.CompilerParams(vmem_limit_bytes=8 * 2**20),
        name="edges",
    )(here, pinned(t))


def prepare_kernel(
    groups,
    here_ref,
    t_ref,
    u_hbm,
    v_hbm,
    w_hbm,
    a_hbm,
    side_ref,
    cb_ref,
    ca_ref,
    cl_ref,
    ch_ref,
    ah_ref,
    al_ref,
    u_ref,
    v_ref,
    w_ref,
    along_ref,
    wallward_ref,
    a_buf,
    sems,
):
    planes, rows, nx = side_ref.shape
    parts = sems.shape[0] - 3
    a_rows = a_buf.shape[0] // parts
    fields = [
        pltpu.make_async_copy(source, target, sems.at[i])
        for i, (source, target) in enumerate(((u_hbm, u_ref), (v_hbm, v_ref), (w_hbm, w_ref)))
    ]
    copies = []
    for i in range(parts):
        cut = slice(i * a_rows, (i + 1) * a_rows)
        copies.append(pltpu.make_async_copy(a_hbm.at[cut], a_buf.at[cut], sems.at[3 + i]))
    for copy in fields + copies:
        copy.start()
    levels = (lax.broadcasted_iota(jnp.int32, (rows, LANES), 0) + here_ref[0] % groups * rows).astype(jnp.float32)
    metric = jnp.concatenate([metric_of(levels, groups * rows)] * (nx // LANES), axis=1)
    level = lax.broadcasted_iota(jnp.int32, (rows, nx), 0)

    def plane(y):
        if y < 0 or y == planes:
            return jnp.zeros((rows, nx), jnp.float32)
        return jnp.concatenate([t_ref[0, y], t_ref[1, y]], axis=0)

    own = (1.0 - 3.0 * CONDUCTION_PART) - CONDUCTION_PART * metric
    near, far = 0.5 * CONDUCTION_PART * metric, TRANSPORT_PART * metric
    for y in range(planes):
        t, ahead, behind = plane(y), plane(y + 1), plane(y - 1)
        east = pltpu.roll(t, nx - 1, 1)
        west = pltpu.roll(t, 1, 1)
        above = jnp.where(level == rows - 1, 0.0, pltpu.roll(t, rows - 1, 0))
        below = jnp.where(level == 0, 0.0, pltpu.roll(t, 1, 0))
        side_ref[y] = (
            own * t
            + CONDUCTION_PART * (ahead + behind)
            + 0.5 * CONDUCTION_PART * (east + west)
            + near * (above + below)
        )
        along_ref[y] = 0.5 * TRANSPORT_PART * (east - west)
        wallward_ref[y] = far * (above - below)
    for copy in fields:
        copy.wait()
    for y in range(planes):
        u = u_ref[y].astype(jnp.float32)
        v = v_ref[y].astype(jnp.float32)
        w = w_ref[y].astype(jnp.float32)
        across = 0.5 * TRANSPORT_PART * (plane(y + 1) - plane(y - 1))
        side_ref[y] = side_ref[y] - (u * along_ref[y] + v * across + w * wallward_ref[y])
        cl_ref[y : y + 1, :] = (metric * (0.5 * CONDUCTION_PART + TRANSPORT_PART * w))[:1, :]
        ch_ref[y : y + 1, :] = (metric * (0.5 * CONDUCTION_PART - TRANSPORT_PART * w))[rows - 1 :, :]
        if y == 0:
            cb_ref[...] = CONDUCTION_PART + 0.5 * TRANSPORT_PART * v
        if y == planes - 1:
            ca_ref[...] = CONDUCTION_PART - 0.5 * TRANSPORT_PART * v
    for i in range(parts):
        cut = slice(i * a_rows, (i + 1) * a_rows)
        copies[i].wait()
        ah_ref[cut], al_ref[cut] = halves(a_buf[cut])


def prepare(here, t, u, v, w, a, groups):
    planes, rows, nx = u.shape
    a16 = jax.ShapeDtypeStruct(a.shape, jnp.bfloat16)
    plane = jax.ShapeDtypeStruct((rows, nx), t.dtype)
    level = jax.ShapeDtypeStruct((planes, nx), t.dtype)
    parts = 4
    return pl.pallas_call(
        functools.partial(prepare_kernel, groups),
        in_specs=[SMEM, VMEM] + [HBM] * 4,
        out_specs=[VMEM] * 7,
        out_shape=[jax.ShapeDtypeStruct(u.shape, t.dtype), plane, plane, level, level, a16, a16],
        scratch_shapes=[pltpu.VMEM(x.shape, x.dtype) for x in (u, v, w)]
        + [pltpu.VMEM(u.shape, t.dtype)] * 2
        + [pltpu.VMEM(a.shape, a.dtype)]
        + [pltpu.SemaphoreType.DMA((3 + parts,))],
        compiler_params=pltpu.CompilerParams(vmem_limit_bytes=20 * 2**20),
        cost_estimate=pl.CostEstimate(
            flops=4 * a.size + 40 * t.size, bytes_accessed=8 * a.size + 14 * t.size, transcendentals=0
        ),
        name="prepare",
    )(here, t, *(pinned(x) for x in (u, v, w, a)))


def row_kernel(
    here_ref, side_ref, cb_ref, ca_ref, cl_ref, ch_ref, yc_ref, yd_ref, za_ref, zb_ref, ah_ref, al_ref, out_ref, both
):
    planes, rows, nx = side_ref.shape
    groups = out_ref.shape[0]
    pencil_even, slab_even = here_ref[0] % 2 == 0, here_ref[0] // groups % 2 == 0
    low = cl_ref[...] * jnp.where(pencil_even, za_ref[...], zb_ref[...])
    high = ch_ref[...] * jnp.where(pencil_even, zb_ref[...], za_ref[...])
    level = lax.broadcasted_iota(jnp.int32, (rows, nx), 0)
    extent = planes * rows
    for y in range(planes):
        side = side_ref[y]
        if y == 0:
            side = side + cb_ref[...] * jnp.where(slab_even, yd_ref[...], yc_ref[...])
        if y == planes - 1:
            side = side + ca_ref[...] * jnp.where(slab_even, yc_ref[...], yd_ref[...])
        side = side + jnp.where(level == 0, low[y : y + 1, :], 0.0)
        side = side + jnp.where(level == rows - 1, high[y : y + 1, :], 0.0)
        high_part, low_part = halves(side)
        both[y * rows : (y + 1) * rows, :] = high_part
        both[extent + y * rows : extent + (y + 1) * rows, :] = low_part
    wide = 2 * LANES
    unit_rows = 3 * rows
    blocks = nx // LANES
    for c in range(nx // wide):
        ah = ah_ref[c * wide : (c + 1) * wide, :]
        al = al_ref[c * wide : (c + 1) * wide, :]

        def dot(x, m):
            return lax.dot_general(x, m, (((1,), (1,)), ((), ())), preferred_element_type=jnp.float32)

        main = dot(both[...], ah)
        solved = main[:extent] + (dot(both[:extent, :], al) + main[extent:])
        for q in range(planes // 3):
            for h in range(2):
                piece = solved[q * unit_rows : (q + 1) * unit_rows, h * LANES : (h + 1) * LANES]
                out_ref[q * blocks + 2 * c + h] = piece.reshape(3, rows, LANES)


def row_solve(here, parts, halos, ah, al, groups):
    planes, rows, nx = parts[0].shape
    return pl.pallas_call(
        row_kernel,
        in_specs=[SMEM] + [VMEM] * 11,
        out_specs=VMEM,
        out_shape=jax.ShapeDtypeStruct((groups, 3, rows, LANES), jnp.float32),
        scratch_shapes=[pltpu.VMEM((2 * planes * rows, nx), jnp.bfloat16)],
        compiler_params=pltpu.CompilerParams(vmem_limit_bytes=32 * 2**20),
        cost_estimate=pl.CostEstimate(
            flops=6 * planes * rows * nx * nx, bytes_accessed=8 * 2**20, transcendentals=0
        ),
        name="row_solve",
    )(here, *parts, *halos, ah, al)


def column_kernel(blocks, here_ref, seg_ref, w_ref, x_ref, out_ref):
    groups, units, rows, lanes = x_ref.shape
    column = lax.broadcasted_iota(jnp.int32, (8, lanes), 1) + here_ref[0] % blocks * lanes
    crossed = jnp.zeros((8, lanes), jnp.int32)
    end = jnp.int32(0)
    for s in range(seg_ref.shape[0]):
        end = end + seg_ref[s]
        crossed = crossed + jnp.where(column >= end, 1, 0)
    insulated = jnp.concatenate([(crossed % 2)[:1, :]] * units, axis=1) == 1
    extent = groups * rows
    lines = jnp.concatenate([x_ref[:, i].reshape(extent, lanes) for i in range(units)], axis=1)
    xh, xl = halves(lines)
    both = jnp.concatenate([xh, xl], axis=1)
    width = units * lanes

    def solve(c, cut):
        wh, wl = halves(w_ref[c, cut])
        d = jnp.dot(wh, both, preferred_element_type=jnp.float32)
        e = jnp.dot(wl, xh, preferred_element_type=jnp.float32)
        return d[:, :width] + (d[:, width:] + e)

    step = 256
    for k in range(0, extent, step):
        cut = slice(k, k + step)
        solved = jnp.where(insulated, solve(1, cut), solve(0, cut))
        for i in range(units):
            piece = solved[:, i * lanes : (i + 1) * lanes]
            out_ref[k // rows : (k + step) // rows, i] = piece.reshape(step // rows, rows, lanes)


def column_solve(here, segments, w, x, blocks):
    return pl.pallas_call(
        functools.partial(column_kernel, blocks),
        in_specs=[SMEM, SMEM, VMEM, VMEM],
        out_specs=VMEM,
        out_shape=jax.ShapeDtypeStruct(x.shape, jnp.float32),
        compiler_params=pltpu.CompilerParams(vmem_limit_bytes=32 * 2**20),
        cost_estimate=pl.CostEstimate(
            flops=12 * w.shape[1] * x.size, bytes_accessed=4 * 2**20, transcendentals=0
        ),
        name="column_solve",
    )(here, segments, w, x)


def place_kernel(x_ref, out_ref):
    groups = x_ref.shape[0]
    blocks = out_ref.shape[2] // LANES
    for p in range(groups):
        q, b = p // blocks, p % blocks
        out_ref[3 * q : 3 * q + 3, :, b * LANES : (b + 1) * LANES] = x_ref[p]


def place(x, shape):
    return pl.pallas_call(
        place_kernel,
        in_specs=[VMEM],
        out_specs=VMEM,
        out_shape=jax.ShapeDtypeStruct(shape, jnp.float32),
        compiler_params=pltpu.CompilerParams(vmem_limit_bytes=16 * 2**20),
        name="place",
    )(x)


def swapped(x):
    return lax.all_to_all(x, "pencil", split_axis=0, concat_axis=0, tiled=True)


def on_device(t, u, v, w, downstream_solver_matrix, wallward_solver_matrices, wall_segments):
    planes, rows, nx = t.shape
    slabs, groups = lax.axis_size("slab"), lax.axis_size("pencil")
    here = lax.axis_index(("slab", "pencil")).astype(jnp.int32).reshape(1)
    yc, yd, za, zb, t_halves = edges(here, t, groups)
    yc = lax.ppermute(yc, "slab", [(i, i ^ 1) for i in range(slabs)])
    yd = lax.ppermute(yd, "slab", [(i, ((i - 1) ^ 1) + 1 & slabs - 1) for i in range(slabs)])
    za = lax.ppermute(za, "pencil", [(i, ((i - 1) ^ 1) + 1) for i in range(1, groups - 1)])
    zb = lax.ppermute(zb, "pencil", [(i, i ^ 1) for i in range(groups)])
    halos = yc, yd, za, zb
    *parts, ah, al = prepare(here, t_halves, u, v, w, downstream_solver_matrix, groups)
    x = swapped(row_solve(here, parts, halos, ah, al, groups))
    x = swapped(column_solve(here, wall_segments, wallward_solver_matrices, x, nx // LANES))
    return place(x, t.shape)


def solution(mesh):
    field = P("slab", "pencil", None)
    return jax.shard_map(
        on_device,
        mesh=mesh,
        in_specs=(field, field, field, field, P(), P(), P()),
        out_specs=field,
        check_vma=False,
    )
```

```python
import functools

import jax
import jax.numpy as jnp
from jax import lax
from jax.experimental import pallas as pl
from jax.experimental.pallas import tpu as pltpu
from jax.sharding import PartitionSpec as P

TRANSPORT_PART = 0.25
CONDUCTION_PART = 0.2
LANES = 128
VMEM = pl.BlockSpec(memory_space=pltpu.VMEM)
HBM = pl.BlockSpec(memory_space=pltpu.HBM)
SMEM = pl.BlockSpec(memory_space=pltpu.SMEM)


def metric_of(levels, extent):
    return 0.5 / (1.0 + jnp.sin(jnp.pi * (levels + 0.5) / extent))


def pinned(x):
    return pltpu.with_memory_space_constraint(x, pltpu.HBM)


def halves(wide):
    high = wide.astype(jnp.bfloat16)
    return high, (wide - high.astype(jnp.float32)).astype(jnp.bfloat16)


def edge_kernel(groups, here_ref, t_hbm, yc_ref, yd_ref, za_ref, zb_ref, buf, sems):
    planes, rows, _ = t_hbm.shape
    half = buf.shape[2]
    pencil_even, slab_even = here_ref[0] % 2 == 0, here_ref[0] // groups % 2 == 0
    copies = [
        pltpu.make_async_copy(t_hbm.at[:, pl.ds(0, half)], buf.at[0], sems.at[0]),
        pltpu.make_async_copy(t_hbm.at[:, pl.ds(rows - half, half)], buf.at[1], sems.at[1]),
        pltpu.make_async_copy(t_hbm.at[jnp.where(slab_even, planes - 1, 0)], yc_ref, sems.at[2]),
        pltpu.make_async_copy(t_hbm.at[jnp.where(slab_even, 0, planes - 1)], yd_ref, sems.at[3]),
    ]
    for copy in copies:
        copy.start()
    copies[0].wait()
    copies[1].wait()
    for y in range(planes):
        low, high = buf[0, y, :1, :], buf[1, y, half - 1 :, :]
        za_ref[y : y + 1, :] = jnp.where(pencil_even, low, high)
        zb_ref[y : y + 1, :] = jnp.where(pencil_even, high, low)
    copies[2].wait()
    copies[3].wait()


def edges(here, t, groups):
    planes, rows, nx = t.shape
    half = rows // 2
    plane = jax.ShapeDtypeStruct((rows, nx), t.dtype)
    level = jax.ShapeDtypeStruct((planes, nx), t.dtype)
    return pl.pallas_call(
        functools.partial(edge_kernel, groups),
        in_specs=[SMEM, HBM],
        out_specs=[VMEM] * 5,
        out_shape=[plane, plane, level, level, jax.ShapeDtypeStruct((2, planes, half, nx), t.dtype)],
        scratch_shapes=[pltpu.SemaphoreType.DMA((4,))],
        compiler_params=pltpu.CompilerParams(vmem_limit_bytes=8 * 2**20),
        name="edges",
    )(here, pinned(t))


def prepare_kernel(
    groups,
    here_ref,
    t_ref,
    u_hbm,
    v_hbm,
    w_hbm,
    a_hbm,
    side_ref,
    cb_ref,
    ca_ref,
    cl_ref,
    ch_ref,
    ah_ref,
    al_ref,
    u_ref,
    v_ref,
    w_ref,
    along_ref,
    wallward_ref,
    a_buf,
    sems,
):
    planes, rows, nx = side_ref.shape
    parts = sems.shape[0] - 3
    a_rows = a_buf.shape[0] // parts
    fields = [
        pltpu.make_async_copy(source, target, sems.at[i])
        for i, (source, target) in enumerate(((u_hbm, u_ref), (v_hbm, v_ref), (w_hbm, w_ref)))
    ]
    copies = []
    for i in range(parts):
        cut = slice(i * a_rows, (i + 1) * a_rows)
        copies.append(pltpu.make_async_copy(a_hbm.at[cut], a_buf.at[cut], sems.at[3 + i]))
    for copy in fields + copies:
        copy.start()
    levels = (lax.broadcasted_iota(jnp.int32, (rows, LANES), 0) + here_ref[0] % groups * rows).astype(jnp.float32)
    metric = jnp.concatenate([metric_of(levels, groups * rows)] * (nx // LANES), axis=1)
    level = lax.broadcasted_iota(jnp.int32, (rows, nx), 0)

    def plane(y):
        if y < 0 or y == planes:
            return jnp.zeros((rows, nx), jnp.float32)
        return jnp.concatenate([t_ref[0, y], t_ref[1, y]], axis=0)

    own = (1.0 - 3.0 * CONDUCTION_PART) - CONDUCTION_PART * metric
    near, far = 0.5 * CONDUCTION_PART * metric, TRANSPORT_PART * metric
    for y in range(planes):
        t, ahead, behind = plane(y), plane(y + 1), plane(y - 1)
        east = pltpu.roll(t, nx - 1, 1)
        west = pltpu.roll(t, 1, 1)
        above = jnp.where(level == rows - 1, 0.0, pltpu.roll(t, rows - 1, 0))
        below = jnp.where(level == 0, 0.0, pltpu.roll(t, 1, 0))
        side_ref[y] = (
            own * t
            + CONDUCTION_PART * (ahead + behind)
            + 0.5 * CONDUCTION_PART * (east + west)
            + near * (above + below)
        )
        along_ref[y] = 0.5 * TRANSPORT_PART * (east - west)
        wallward_ref[y] = far * (above - below)
    for copy in fields:
        copy.wait()
    for y in range(planes):
        u = u_ref[y].astype(jnp.float32)
        v = v_ref[y].astype(jnp.float32)
        w = w_ref[y].astype(jnp.float32)
        across = 0.5 * TRANSPORT_PART * (plane(y + 1) - plane(y - 1))
        side_ref[y] = side_ref[y] - (u * along_ref[y] + v * across + w * wallward_ref[y])
        cl_ref[y : y + 1, :] = (metric * (0.5 * CONDUCTION_PART + TRANSPORT_PART * w))[:1, :]
        ch_ref[y : y + 1, :] = (metric * (0.5 * CONDUCTION_PART - TRANSPORT_PART * w))[rows - 1 :, :]
        if y == 0:
            cb_ref[...] = CONDUCTION_PART + 0.5 * TRANSPORT_PART * v
        if y == planes - 1:
            ca_ref[...] = CONDUCTION_PART - 0.5 * TRANSPORT_PART * v
    for i in range(parts):
        cut = slice(i * a_rows, (i + 1) * a_rows)
        copies[i].wait()
        ah_ref[cut], al_ref[cut] = halves(a_buf[cut])


def prepare(here, t, u, v, w, a, groups):
    planes, rows, nx = u.shape
    half = (a.shape[0] // 2, a.shape[1])
    a16 = jax.ShapeDtypeStruct(half, jnp.bfloat16)
    plane = jax.ShapeDtypeStruct((rows, nx), t.dtype)
    level = jax.ShapeDtypeStruct((planes, nx), t.dtype)
    parts = 2
    return pl.pallas_call(
        functools.partial(prepare_kernel, groups),
        in_specs=[SMEM, VMEM] + [HBM] * 4,
        out_specs=[VMEM] * 7,
        out_shape=[jax.ShapeDtypeStruct(u.shape, t.dtype), plane, plane, level, level, a16, a16],
        scratch_shapes=[pltpu.VMEM(x.shape, x.dtype) for x in (u, v, w)]
        + [pltpu.VMEM(u.shape, t.dtype)] * 2
        + [pltpu.VMEM(half, a.dtype)]
        + [pltpu.SemaphoreType.DMA((3 + parts,))],
        compiler_params=pltpu.CompilerParams(vmem_limit_bytes=20 * 2**20),
        cost_estimate=pl.CostEstimate(
            flops=2 * a.size + 40 * t.size, bytes_accessed=4 * a.size + 14 * t.size, transcendentals=0
        ),
        name="prepare",
    )(here, t, *(pinned(x) for x in (u, v, w, a)))


def row_kernel(
    here_ref,
    side_ref,
    cb_ref,
    ca_ref,
    cl_ref,
    ch_ref,
    yc_ref,
    yd_ref,
    za_ref,
    zb_ref,
    ah_ref,
    al_ref,
    a_hbm,
    out_ref,
    both,
    a_buf,
    sems,
):
    planes, rows, nx = side_ref.shape
    wide = 2 * LANES
    ready = ah_ref.shape[0] // wide
    copies = []
    for c in range(sems.shape[0]):
        source = a_hbm.at[pl.ds((ready + c) * wide, wide)]
        copies.append(pltpu.make_async_copy(source, a_buf.at[pl.ds(c * wide, wide)], sems.at[c]))
    for copy in copies:
        copy.start()
    groups = out_ref.shape[0]
    pencil_even, slab_even = here_ref[0] % 2 == 0, here_ref[0] // groups % 2 == 0
    low = cl_ref[...] * jnp.where(pencil_even, za_ref[...], zb_ref[...])
    high = ch_ref[...] * jnp.where(pencil_even, zb_ref[...], za_ref[...])
    level = lax.broadcasted_iota(jnp.int32, (rows, nx), 0)
    extent = planes * rows
    for y in range(planes):
        side = side_ref[y]
        if y == 0:
            side = side + cb_ref[...] * jnp.where(slab_even, yd_ref[...], yc_ref[...])
        if y == planes - 1:
            side = side + ca_ref[...] * jnp.where(slab_even, yc_ref[...], yd_ref[...])
        side = side + jnp.where(level == 0, low[y : y + 1, :], 0.0)
        side = side + jnp.where(level == rows - 1, high[y : y + 1, :], 0.0)
        high_part, low_part = halves(side)
        both[y * rows : (y + 1) * rows, :] = high_part
        both[extent + y * rows : extent + (y + 1) * rows, :] = low_part
    unit_rows = 3 * rows
    blocks = nx // LANES
    for c in range(nx // wide):
        if c < ready:
            ah, al = ah_ref[c * wide : (c + 1) * wide, :], al_ref[c * wide : (c + 1) * wide, :]
        else:
            copies[c - ready].wait()
            ah, al = halves(a_buf[(c - ready) * wide : (c - ready + 1) * wide, :])

        def dot(x, m):
            return lax.dot_general(x, m, (((1,), (1,)), ((), ())), preferred_element_type=jnp.float32)

        main = dot(both[...], ah)
        solved = main[:extent] + (dot(both[:extent, :], al) + main[extent:])
        for q in range(planes // 3):
            for h in range(2):
                piece = solved[q * unit_rows : (q + 1) * unit_rows, h * LANES : (h + 1) * LANES]
                out_ref[q * blocks + 2 * c + h] = piece.reshape(3, rows, LANES)


def row_solve(here, parts, halos, ah, al, a, groups):
    planes, rows, nx = parts[0].shape
    return pl.pallas_call(
        row_kernel,
        in_specs=[SMEM] + [VMEM] * 11 + [HBM],
        out_specs=VMEM,
        out_shape=jax.ShapeDtypeStruct((groups, 3, rows, LANES), jnp.float32),
        scratch_shapes=[
            pltpu.VMEM((2 * planes * rows, nx), jnp.bfloat16),
            pltpu.VMEM((nx - ah.shape[0], nx), a.dtype),
            pltpu.SemaphoreType.DMA(((nx - ah.shape[0]) // (2 * LANES),)),
        ],
        compiler_params=pltpu.CompilerParams(vmem_limit_bytes=32 * 2**20),
        cost_estimate=pl.CostEstimate(
            flops=6 * planes * rows * nx * nx, bytes_accessed=8 * 2**20, transcendentals=0
        ),
        name="row_solve",
    )(here, *parts, *halos, ah, al, pinned(a))


def column_kernel(blocks, here_ref, seg_ref, w_ref, x_ref, out_ref):
    groups, units, rows, lanes = x_ref.shape
    column = lax.broadcasted_iota(jnp.int32, (8, lanes), 1) + here_ref[0] % blocks * lanes
    crossed = jnp.zeros((8, lanes), jnp.int32)
    end = jnp.int32(0)
    for s in range(seg_ref.shape[0]):
        end = end + seg_ref[s]
        crossed = crossed + jnp.where(column >= end, 1, 0)
    insulated = jnp.concatenate([(crossed % 2)[:1, :]] * units, axis=1) == 1
    extent = groups * rows
    lines = jnp.concatenate([x_ref[:, i].reshape(extent, lanes) for i in range(units)], axis=1)
    xh, xl = halves(lines)
    both = jnp.concatenate([xh, xl], axis=1)
    width = units * lanes

    def solve(c, cut):
        wh, wl = halves(w_ref[c, cut])
        d = jnp.dot(wh, both, preferred_element_type=jnp.float32)
        e = jnp.dot(wl, xh, preferred_element_type=jnp.float32)
        return d[:, :width] + (d[:, width:] + e)

    step = 256
    for k in range(0, extent, step):
        cut = slice(k, k + step)
        solved = jnp.where(insulated, solve(1, cut), solve(0, cut))
        for i in range(units):
            piece = solved[:, i * lanes : (i + 1) * lanes]
            out_ref[k // rows : (k + step) // rows, i] = piece.reshape(step // rows, rows, lanes)


def column_solve(here, segments, w, x, blocks):
    return pl.pallas_call(
        functools.partial(column_kernel, blocks),
        in_specs=[SMEM, SMEM, VMEM, VMEM],
        out_specs=VMEM,
        out_shape=jax.ShapeDtypeStruct(x.shape, jnp.float32),
        compiler_params=pltpu.CompilerParams(vmem_limit_bytes=32 * 2**20),
        cost_estimate=pl.CostEstimate(
            flops=12 * w.shape[1] * x.size, bytes_accessed=4 * 2**20, transcendentals=0
        ),
        name="column_solve",
    )(here, segments, w, x)


def place_kernel(x_ref, out_ref):
    groups = x_ref.shape[0]
    blocks = out_ref.shape[2] // LANES
    for p in range(groups):
        q, b = p // blocks, p % blocks
        out_ref[3 * q : 3 * q + 3, :, b * LANES : (b + 1) * LANES] = x_ref[p]


def place(x, shape):
    return pl.pallas_call(
        place_kernel,
        in_specs=[VMEM],
        out_specs=VMEM,
        out_shape=jax.ShapeDtypeStruct(shape, jnp.float32),
        compiler_params=pltpu.CompilerParams(vmem_limit_bytes=16 * 2**20),
        name="place",
    )(x)


def fetched(x):
    groups = lax.axis_size("pencil")
    return lax.ppermute(x, "pencil", [(i, i) for i in range(groups)])


def swapped(x):
    return lax.all_to_all(x, "pencil", split_axis=0, concat_axis=0, tiled=True)


def on_device(t, u, v, w, downstream_solver_matrix, wallward_solver_matrices, wall_segments):
    planes, rows, nx = t.shape
    slabs, groups = lax.axis_size("slab"), lax.axis_size("pencil")
    here = lax.axis_index(("slab", "pencil")).astype(jnp.int32).reshape(1)
    w_z = fetched(wallward_solver_matrices)
    yc, yd, za, zb, t_halves = edges(here, t, groups)
    yc = lax.ppermute(yc, "slab", [(i, i ^ 1) for i in range(slabs)])
    yd = lax.ppermute(yd, "slab", [(i, ((i - 1) ^ 1) + 1 & slabs - 1) for i in range(slabs)])
    za = lax.ppermute(za, "pencil", [(i, ((i - 1) ^ 1) + 1) for i in range(1, groups - 1)])
    zb = lax.ppermute(zb, "pencil", [(i, i ^ 1) for i in range(groups)])
    halos = yc, yd, za, zb
    *parts, ah, al = prepare(here, t_halves, u, v, w, downstream_solver_matrix, groups)
    x = swapped(row_solve(here, parts, halos, ah, al, downstream_solver_matrix, groups))
    x = swapped(column_solve(here, wall_segments, w_z, x, nx // LANES))
    return place(x, t.shape)


def solution(mesh):
    field = P("slab", "pencil", None)
    return jax.shard_map(
        on_device,
        mesh=mesh,
        in_specs=(field, field, field, field, P(), P(), P()),
        out_specs=field,
        check_vma=False,
    )
```

```python
import functools

import jax
import jax.numpy as jnp
from jax import lax
from jax.experimental import pallas as pl
from jax.experimental.pallas import tpu as pltpu
from jax.sharding import PartitionSpec as P

TRANSPORT_PART = 0.25
CONDUCTION_PART = 0.2
LANES = 128
VMEM = pl.BlockSpec(memory_space=pltpu.VMEM)
HBM = pl.BlockSpec(memory_space=pltpu.HBM)
SMEM = pl.BlockSpec(memory_space=pltpu.SMEM)


def metric_of(levels, extent):
    return 0.5 / (1.0 + jnp.sin(jnp.pi * (levels + 0.5) / extent))


def pinned(x):
    return pltpu.with_memory_space_constraint(x, pltpu.HBM)


def halves(wide):
    high = wide.astype(jnp.bfloat16)
    return high, (wide - high.astype(jnp.float32)).astype(jnp.bfloat16)


def edge_kernel(groups, here_ref, t_hbm, yc_ref, yd_ref, za_ref, zb_ref, buf, sems):
    planes, rows, _ = t_hbm.shape
    half = buf.shape[2]
    pencil_even, slab_even = here_ref[0] % 2 == 0, here_ref[0] // groups % 2 == 0
    copies = [
        pltpu.make_async_copy(t_hbm.at[:, pl.ds(0, half)], buf.at[0], sems.at[0]),
        pltpu.make_async_copy(t_hbm.at[:, pl.ds(rows - half, half)], buf.at[1], sems.at[1]),
        pltpu.make_async_copy(t_hbm.at[jnp.where(slab_even, planes - 1, 0)], yc_ref, sems.at[2]),
        pltpu.make_async_copy(t_hbm.at[jnp.where(slab_even, 0, planes - 1)], yd_ref, sems.at[3]),
    ]
    for copy in copies:
        copy.start()
    copies[0].wait()
    copies[1].wait()
    for y in range(planes):
        low, high = buf[0, y, :1, :], buf[1, y, half - 1 :, :]
        za_ref[y : y + 1, :] = jnp.where(pencil_even, low, high)
        zb_ref[y : y + 1, :] = jnp.where(pencil_even, high, low)
    copies[2].wait()
    copies[3].wait()


def edges(here, t, groups):
    planes, rows, nx = t.shape
    half = rows // 2
    plane = jax.ShapeDtypeStruct((rows, nx), t.dtype)
    level = jax.ShapeDtypeStruct((planes, nx), t.dtype)
    return pl.pallas_call(
        functools.partial(edge_kernel, groups),
        in_specs=[SMEM, HBM],
        out_specs=[VMEM] * 5,
        out_shape=[plane, plane, level, level, jax.ShapeDtypeStruct((2, planes, half, nx), t.dtype)],
        scratch_shapes=[pltpu.SemaphoreType.DMA((4,))],
        compiler_params=pltpu.CompilerParams(vmem_limit_bytes=8 * 2**20),
        name="edges",
    )(here, pinned(t))


def prepare_kernel(
    groups,
    here_ref,
    t_ref,
    u_hbm,
    v_hbm,
    w_hbm,
    a_hbm,
    side_ref,
    cb_ref,
    ca_ref,
    cl_ref,
    ch_ref,
    ah_ref,
    al_ref,
    u_ref,
    v_ref,
    w_ref,
    along_ref,
    wallward_ref,
    a_buf,
    sems,
):
    planes, rows, nx = side_ref.shape
    parts = sems.shape[0] - 3
    a_rows = a_buf.shape[0] // parts
    fields = [
        pltpu.make_async_copy(source, target, sems.at[i])
        for i, (source, target) in enumerate(((u_hbm, u_ref), (v_hbm, v_ref), (w_hbm, w_ref)))
    ]
    copies = []
    for i in range(parts):
        cut = slice(i * a_rows, (i + 1) * a_rows)
        copies.append(pltpu.make_async_copy(a_hbm.at[cut], a_buf.at[cut], sems.at[3 + i]))
    for copy in fields + copies:
        copy.start()
    levels = (lax.broadcasted_iota(jnp.int32, (rows, LANES), 0) + here_ref[0] % groups * rows).astype(jnp.float32)
    metric = jnp.concatenate([metric_of(levels, groups * rows)] * (nx // LANES), axis=1)
    level = lax.broadcasted_iota(jnp.int32, (rows, nx), 0)

    def plane(y):
        if y < 0 or y == planes:
            return jnp.zeros((rows, nx), jnp.float32)
        return jnp.concatenate([t_ref[0, y], t_ref[1, y]], axis=0)

    own = (1.0 - 3.0 * CONDUCTION_PART) - CONDUCTION_PART * metric
    near, far = 0.5 * CONDUCTION_PART * metric, TRANSPORT_PART * metric
    for y in range(planes):
        t, ahead, behind = plane(y), plane(y + 1), plane(y - 1)
        east = pltpu.roll(t, nx - 1, 1)
        west = pltpu.roll(t, 1, 1)
        above = jnp.where(level == rows - 1, 0.0, pltpu.roll(t, rows - 1, 0))
        below = jnp.where(level == 0, 0.0, pltpu.roll(t, 1, 0))
        side_ref[y] = (
            own * t
            + CONDUCTION_PART * (ahead + behind)
            + 0.5 * CONDUCTION_PART * (east + west)
            + near * (above + below)
        )
        along_ref[y] = 0.5 * TRANSPORT_PART * (east - west)
        wallward_ref[y] = far * (above - below)
    for copy in fields:
        copy.wait()
    for y in range(planes):
        u = u_ref[y].astype(jnp.float32)
        v = v_ref[y].astype(jnp.float32)
        w = w_ref[y].astype(jnp.float32)
        across = 0.5 * TRANSPORT_PART * (plane(y + 1) - plane(y - 1))
        side_ref[y] = side_ref[y] - (u * along_ref[y] + v * across + w * wallward_ref[y])
        cl_ref[y : y + 1, :] = (metric * (0.5 * CONDUCTION_PART + TRANSPORT_PART * w))[:1, :]
        ch_ref[y : y + 1, :] = (metric * (0.5 * CONDUCTION_PART - TRANSPORT_PART * w))[rows - 1 :, :]
        if y == 0:
            cb_ref[...] = CONDUCTION_PART + 0.5 * TRANSPORT_PART * v
        if y == planes - 1:
            ca_ref[...] = CONDUCTION_PART - 0.5 * TRANSPORT_PART * v
    for i in range(parts):
        cut = slice(i * a_rows, (i + 1) * a_rows)
        copies[i].wait()
        ah_ref[cut], al_ref[cut] = halves(a_buf[cut])


def prepare(here, t, u, v, w, a, groups):
    planes, rows, nx = u.shape
    a16 = jax.ShapeDtypeStruct(a.shape, jnp.bfloat16)
    plane = jax.ShapeDtypeStruct((rows, nx), t.dtype)
    level = jax.ShapeDtypeStruct((planes, nx), t.dtype)
    parts = 4
    return pl.pallas_call(
        functools.partial(prepare_kernel, groups),
        in_specs=[SMEM, VMEM] + [HBM] * 4,
        out_specs=[VMEM] * 7,
        out_shape=[jax.ShapeDtypeStruct(u.shape, t.dtype), plane, plane, level, level, a16, a16],
        scratch_shapes=[pltpu.VMEM(x.shape, x.dtype) for x in (u, v, w)]
        + [pltpu.VMEM(u.shape, t.dtype)] * 2
        + [pltpu.VMEM(a.shape, a.dtype)]
        + [pltpu.SemaphoreType.DMA((3 + parts,))],
        compiler_params=pltpu.CompilerParams(vmem_limit_bytes=20 * 2**20),
        cost_estimate=pl.CostEstimate(
            flops=4 * a.size + 40 * t.size, bytes_accessed=8 * a.size + 14 * t.size, transcendentals=0
        ),
        name="prepare",
    )(here, t, *(pinned(x) for x in (u, v, w, a)))


def row_kernel(
    here_ref, side_ref, cb_ref, ca_ref, cl_ref, ch_ref, yc_ref, yd_ref, za_ref, zb_ref, ah_ref, al_ref, out_ref, both
):
    planes, rows, nx = side_ref.shape
    groups = out_ref.shape[0]
    pencil_even, slab_even = here_ref[0] % 2 == 0, here_ref[0] // groups % 2 == 0
    low = cl_ref[...] * jnp.where(pencil_even, za_ref[...], zb_ref[...])
    high = ch_ref[...] * jnp.where(pencil_even, zb_ref[...], za_ref[...])
    level = lax.broadcasted_iota(jnp.int32, (rows, nx), 0)
    extent = planes * rows
    for y in range(planes):
        side = side_ref[y]
        if y == 0:
            side = side + cb_ref[...] * jnp.where(slab_even, yd_ref[...], yc_ref[...])
        if y == planes - 1:
            side = side + ca_ref[...] * jnp.where(slab_even, yc_ref[...], yd_ref[...])
        side = side + jnp.where(level == 0, low[y : y + 1, :], 0.0)
        side = side + jnp.where(level == rows - 1, high[y : y + 1, :], 0.0)
        high_part, low_part = halves(side)
        both[y * rows : (y + 1) * rows, :] = high_part
        both[extent + y * rows : extent + (y + 1) * rows, :] = low_part
    wide = 2 * LANES
    unit_rows = 3 * rows
    blocks = nx // LANES
    for c in range(nx // wide):
        ah = ah_ref[c * wide : (c + 1) * wide, :]
        al = al_ref[c * wide : (c + 1) * wide, :]

        def dot(x, m):
            return lax.dot_general(x, m, (((1,), (1,)), ((), ())), preferred_element_type=jnp.float32)

        main = dot(both[...], ah)
        solved = main[:extent] + (dot(both[:extent, :], al) + main[extent:])
        for q in range(planes // 3):
            for h in range(2):
                piece = solved[q * unit_rows : (q + 1) * unit_rows, h * LANES : (h + 1) * LANES]
                out_ref[q * blocks + 2 * c + h] = piece.reshape(3, rows, LANES)


def row_solve(here, parts, halos, ah, al, groups):
    planes, rows, nx = parts[0].shape
    return pl.pallas_call(
        row_kernel,
        in_specs=[SMEM] + [VMEM] * 11,
        out_specs=VMEM,
        out_shape=jax.ShapeDtypeStruct((groups, 3, rows, LANES), jnp.float32),
        scratch_shapes=[pltpu.VMEM((2 * planes * rows, nx), jnp.bfloat16)],
        compiler_params=pltpu.CompilerParams(vmem_limit_bytes=32 * 2**20),
        cost_estimate=pl.CostEstimate(
            flops=6 * planes * rows * nx * nx, bytes_accessed=8 * 2**20, transcendentals=0
        ),
        name="row_solve",
    )(here, *parts, *halos, ah, al)


def column_kernel(blocks, here_ref, seg_ref, w_ref, x_ref, out_ref):
    groups, units, rows, lanes = x_ref.shape
    column = lax.broadcasted_iota(jnp.int32, (8, lanes), 1) + here_ref[0] % blocks * lanes
    crossed = jnp.zeros((8, lanes), jnp.int32)
    end = jnp.int32(0)
    for s in range(seg_ref.shape[0]):
        end = end + seg_ref[s]
        crossed = crossed + jnp.where(column >= end, 1, 0)
    insulated = jnp.concatenate([(crossed % 2)[:1, :]] * units, axis=1) == 1
    extent = groups * rows
    lines = jnp.concatenate([x_ref[:, i].reshape(extent, lanes) for i in range(units)], axis=1)
    width = units * lanes
    both = jnp.concatenate(
        [
            jnp.concatenate(halves(jnp.where(insulated, 0.0, lines)), axis=1),
            jnp.concatenate(halves(jnp.where(insulated, lines, 0.0)), axis=1),
        ],
        axis=0,
    )
    step = 256
    for k in range(0, extent, step):
        wh, wl = halves(jnp.concatenate([w_ref[0, k : k + step], w_ref[1, k : k + step]], axis=1))
        d = jnp.dot(wh, both, preferred_element_type=jnp.float32)
        e = jnp.dot(wl, both[:, :width], preferred_element_type=jnp.float32)
        solved = d[:, :width] + (d[:, width:] + e)
        for i in range(units):
            piece = solved[:, i * lanes : (i + 1) * lanes]
            out_ref[k // rows : (k + step) // rows, i] = piece.reshape(step // rows, rows, lanes)


def column_solve(here, segments, w, x, blocks):
    return pl.pallas_call(
        functools.partial(column_kernel, blocks),
        in_specs=[SMEM, SMEM, VMEM, VMEM],
        out_specs=VMEM,
        out_shape=jax.ShapeDtypeStruct(x.shape, jnp.float32),
        compiler_params=pltpu.CompilerParams(vmem_limit_bytes=32 * 2**20),
        cost_estimate=pl.CostEstimate(
            flops=12 * w.shape[1] * x.size, bytes_accessed=4 * 2**20, transcendentals=0
        ),
        name="column_solve",
    )(here, segments, w, x)


def place_kernel(x_ref, out_ref):
    groups = x_ref.shape[0]
    blocks = out_ref.shape[2] // LANES
    for p in range(groups):
        q, b = p // blocks, p % blocks
        out_ref[3 * q : 3 * q + 3, :, b * LANES : (b + 1) * LANES] = x_ref[p]


def place(x, shape):
    return pl.pallas_call(
        place_kernel,
        in_specs=[VMEM],
        out_specs=VMEM,
        out_shape=jax.ShapeDtypeStruct(shape, jnp.float32),
        compiler_params=pltpu.CompilerParams(vmem_limit_bytes=16 * 2**20),
        name="place",
    )(x)


def swapped(x):
    return lax.all_to_all(x, "pencil", split_axis=0, concat_axis=0, tiled=True)


def on_device(t, u, v, w, downstream_solver_matrix, wallward_solver_matrices, wall_segments):
    planes, rows, nx = t.shape
    slabs, groups = lax.axis_size("slab"), lax.axis_size("pencil")
    here = lax.axis_index(("slab", "pencil")).astype(jnp.int32).reshape(1)
    yc, yd, za, zb, t_halves = edges(here, t, groups)
    yc = lax.ppermute(yc, "slab", [(i, i ^ 1) for i in range(slabs)])
    yd = lax.ppermute(yd, "slab", [(i, ((i - 1) ^ 1) + 1 & slabs - 1) for i in range(slabs)])
    za = lax.ppermute(za, "pencil", [(i, ((i - 1) ^ 1) + 1) for i in range(1, groups - 1)])
    zb = lax.ppermute(zb, "pencil", [(i, i ^ 1) for i in range(groups)])
    halos = yc, yd, za, zb
    *parts, ah, al = prepare(here, t_halves, u, v, w, downstream_solver_matrix, groups)
    x = swapped(row_solve(here, parts, halos, ah, al, groups))
    x = swapped(column_solve(here, wall_segments, wallward_solver_matrices, x, nx // LANES))
    return place(x, t.shape)


def solution(mesh):
    field = P("slab", "pencil", None)
    return jax.shard_map(
        on_device,
        mesh=mesh,
        in_specs=(field, field, field, field, P(), P(), P()),
        out_specs=field,
        check_vma=False,
    )
```

```python
import functools

import jax
import jax.numpy as jnp
from jax import lax
from jax.experimental import pallas as pl
from jax.experimental.pallas import tpu as pltpu
from jax.sharding import PartitionSpec as P

TRANSPORT_PART = 0.25
CONDUCTION_PART = 0.2
LANES = 128
VMEM = pl.BlockSpec(memory_space=pltpu.VMEM)
HBM = pl.BlockSpec(memory_space=pltpu.HBM)
SMEM = pl.BlockSpec(memory_space=pltpu.SMEM)


def metric_of(levels, extent):
    return 0.5 / (1.0 + jnp.sin(jnp.pi * (levels + 0.5) / extent))


def pinned(x):
    return pltpu.with_memory_space_constraint(x, pltpu.HBM)


def halves(wide):
    high = wide.astype(jnp.bfloat16)
    return high, (wide - high.astype(jnp.float32)).astype(jnp.bfloat16)


def edge_kernel(groups, here_ref, t_hbm, yc_ref, yd_ref, za_ref, zb_ref, buf, sems):
    planes, rows, _ = t_hbm.shape
    half = buf.shape[2]
    pencil_even, slab_even = here_ref[0] % 2 == 0, here_ref[0] // groups % 2 == 0
    copies = [
        pltpu.make_async_copy(t_hbm.at[:, pl.ds(0, half)], buf.at[0], sems.at[0]),
        pltpu.make_async_copy(t_hbm.at[:, pl.ds(rows - half, half)], buf.at[1], sems.at[1]),
        pltpu.make_async_copy(t_hbm.at[jnp.where(slab_even, planes - 1, 0)], yc_ref, sems.at[2]),
        pltpu.make_async_copy(t_hbm.at[jnp.where(slab_even, 0, planes - 1)], yd_ref, sems.at[3]),
    ]
    for copy in copies:
        copy.start()
    copies[0].wait()
    copies[1].wait()
    for y in range(planes):
        low, high = buf[0, y, :1, :], buf[1, y, half - 1 :, :]
        za_ref[y : y + 1, :] = jnp.where(pencil_even, low, high)
        zb_ref[y : y + 1, :] = jnp.where(pencil_even, high, low)
    copies[2].wait()
    copies[3].wait()


def edges(here, t, groups):
    planes, rows, nx = t.shape
    half = rows // 2
    plane = jax.ShapeDtypeStruct((rows, nx), t.dtype)
    level = jax.ShapeDtypeStruct((planes, nx), t.dtype)
    return pl.pallas_call(
        functools.partial(edge_kernel, groups),
        in_specs=[SMEM, HBM],
        out_specs=[VMEM] * 5,
        out_shape=[plane, plane, level, level, jax.ShapeDtypeStruct((2, planes, half, nx), t.dtype)],
        scratch_shapes=[pltpu.SemaphoreType.DMA((4,))],
        compiler_params=pltpu.CompilerParams(vmem_limit_bytes=8 * 2**20),
        name="edges",
    )(here, pinned(t))


def prepare_kernel(
    groups,
    here_ref,
    t_ref,
    u_hbm,
    v_hbm,
    w_hbm,
    a_hbm,
    side_ref,
    cb_ref,
    ca_ref,
    cl_ref,
    ch_ref,
    ah_ref,
    al_ref,
    u_ref,
    v_ref,
    w_ref,
    along_ref,
    wallward_ref,
    a_buf,
    sems,
):
    planes, rows, nx = side_ref.shape
    parts = sems.shape[0] - 3
    a_rows = a_buf.shape[0] // parts
    fields = [
        pltpu.make_async_copy(source, target, sems.at[i])
        for i, (source, target) in enumerate(((u_hbm, u_ref), (v_hbm, v_ref), (w_hbm, w_ref)))
    ]
    copies = []
    for i in range(parts):
        cut = slice(i * a_rows, (i + 1) * a_rows)
        copies.append(pltpu.make_async_copy(a_hbm.at[cut], a_buf.at[cut], sems.at[3 + i]))
    for copy in fields + copies:
        copy.start()
    levels = (lax.broadcasted_iota(jnp.int32, (rows, LANES), 0) + here_ref[0] % groups * rows).astype(jnp.float32)
    metric = jnp.concatenate([metric_of(levels, groups * rows)] * (nx // LANES), axis=1)
    level = lax.broadcasted_iota(jnp.int32, (rows, nx), 0)

    def plane(y):
        if y < 0 or y == planes:
            return jnp.zeros((rows, nx), jnp.float32)
        return jnp.concatenate([t_ref[0, y], t_ref[1, y]], axis=0)

    own = (1.0 - 3.0 * CONDUCTION_PART) - CONDUCTION_PART * metric
    near, far = 0.5 * CONDUCTION_PART * metric, TRANSPORT_PART * metric
    for y in range(planes):
        t, ahead, behind = plane(y), plane(y + 1), plane(y - 1)
        east = pltpu.roll(t, nx - 1, 1)
        west = pltpu.roll(t, 1, 1)
        above = jnp.where(level == rows - 1, 0.0, pltpu.roll(t, rows - 1, 0))
        below = jnp.where(level == 0, 0.0, pltpu.roll(t, 1, 0))
        side_ref[y] = (
            own * t
            + CONDUCTION_PART * (ahead + behind)
            + 0.5 * CONDUCTION_PART * (east + west)
            + near * (above + below)
        )
        along_ref[y] = 0.5 * TRANSPORT_PART * (east - west)
        wallward_ref[y] = far * (above - below)
    for copy in fields:
        copy.wait()
    for y in range(planes):
        u = u_ref[y].astype(jnp.float32)
        v = v_ref[y].astype(jnp.float32)
        w = w_ref[y].astype(jnp.float32)
        across = 0.5 * TRANSPORT_PART * (plane(y + 1) - plane(y - 1))
        side_ref[y] = side_ref[y] - (u * along_ref[y] + v * across + w * wallward_ref[y])
        cl_ref[y : y + 1, :] = (metric * (0.5 * CONDUCTION_PART + TRANSPORT_PART * w))[:1, :]
        ch_ref[y : y + 1, :] = (metric * (0.5 * CONDUCTION_PART - TRANSPORT_PART * w))[rows - 1 :, :]
        if y == 0:
            cb_ref[...] = CONDUCTION_PART + 0.5 * TRANSPORT_PART * v
        if y == planes - 1:
            ca_ref[...] = CONDUCTION_PART - 0.5 * TRANSPORT_PART * v
    for i in range(parts):
        cut = slice(i * a_rows, (i + 1) * a_rows)
        copies[i].wait()
        ah_ref[cut], al_ref[cut] = halves(a_buf[cut])


def prepare(here, t, u, v, w, a, groups):
    planes, rows, nx = u.shape
    a16 = jax.ShapeDtypeStruct(a.shape, jnp.bfloat16)
    plane = jax.ShapeDtypeStruct((rows, nx), t.dtype)
    level = jax.ShapeDtypeStruct((planes, nx), t.dtype)
    parts = 4
    return pl.pallas_call(
        functools.partial(prepare_kernel, groups),
        in_specs=[SMEM, VMEM] + [HBM] * 4,
        out_specs=[VMEM] * 7,
        out_shape=[jax.ShapeDtypeStruct(u.shape, t.dtype), plane, plane, level, level, a16, a16],
        scratch_shapes=[pltpu.VMEM(x.shape, x.dtype) for x in (u, v, w)]
        + [pltpu.VMEM(u.shape, t.dtype)] * 2
        + [pltpu.VMEM(a.shape, a.dtype)]
        + [pltpu.SemaphoreType.DMA((3 + parts,))],
        compiler_params=pltpu.CompilerParams(vmem_limit_bytes=20 * 2**20),
        cost_estimate=pl.CostEstimate(
            flops=4 * a.size + 40 * t.size, bytes_accessed=8 * a.size + 14 * t.size, transcendentals=0
        ),
        name="prepare",
    )(here, t, *(pinned(x) for x in (u, v, w, a)))


def row_kernel(
    here_ref, side_ref, cb_ref, ca_ref, cl_ref, ch_ref, yc_ref, yd_ref, za_ref, zb_ref, ah_ref, al_ref, out_ref, both
):
    planes, rows, nx = side_ref.shape
    groups = out_ref.shape[0]
    pencil_even, slab_even = here_ref[0] % 2 == 0, here_ref[0] // groups % 2 == 0
    low = cl_ref[...] * jnp.where(pencil_even, za_ref[...], zb_ref[...])
    high = ch_ref[...] * jnp.where(pencil_even, zb_ref[...], za_ref[...])
    level = lax.broadcasted_iota(jnp.int32, (rows, nx), 0)
    extent = planes * rows
    for y in range(planes):
        side = side_ref[y]
        if y == 0:
            side = side + cb_ref[...] * jnp.where(slab_even, yd_ref[...], yc_ref[...])
        if y == planes - 1:
            side = side + ca_ref[...] * jnp.where(slab_even, yc_ref[...], yd_ref[...])
        side = side + jnp.where(level == 0, low[y : y + 1, :], 0.0)
        side = side + jnp.where(level == rows - 1, high[y : y + 1, :], 0.0)
        high_part, low_part = halves(side)
        both[y * rows : (y + 1) * rows, :] = high_part
        both[extent + y * rows : extent + (y + 1) * rows, :] = low_part
    wide = 2 * LANES
    unit_rows = 3 * rows
    blocks = nx // LANES
    for c in range(nx // wide):
        ah = ah_ref[c * wide : (c + 1) * wide, :]
        al = al_ref[c * wide : (c + 1) * wide, :]

        def dot(x, m):
            return lax.dot_general(x, m, (((1,), (1,)), ((), ())), preferred_element_type=jnp.float32)

        main = dot(both[...], ah)
        solved = main[:extent] + (dot(both[:extent, :], al) + main[extent:])
        for q in range(planes // 3):
            for h in range(2):
                piece = solved[q * unit_rows : (q + 1) * unit_rows, h * LANES : (h + 1) * LANES]
                out_ref[q * blocks + 2 * c + h] = piece.reshape(3, rows, LANES)


def row_solve(here, parts, halos, ah, al, groups):
    planes, rows, nx = parts[0].shape
    return pl.pallas_call(
        row_kernel,
        in_specs=[SMEM] + [VMEM] * 11,
        out_specs=VMEM,
        out_shape=jax.ShapeDtypeStruct((groups, 3, rows, LANES), jnp.float32),
        scratch_shapes=[pltpu.VMEM((2 * planes * rows, nx), jnp.bfloat16)],
        compiler_params=pltpu.CompilerParams(vmem_limit_bytes=32 * 2**20),
        cost_estimate=pl.CostEstimate(
            flops=6 * planes * rows * nx * nx, bytes_accessed=8 * 2**20, transcendentals=0
        ),
        name="row_solve",
    )(here, *parts, *halos, ah, al)


def column_kernel(blocks, here_ref, seg_ref, w_ref, x_ref, out_ref, high, low, both):
    groups, units, rows, lanes = x_ref.shape
    column = lax.broadcasted_iota(jnp.int32, (8, lanes), 1) + here_ref[0] % blocks * lanes
    crossed = jnp.zeros((8, lanes), jnp.int32)
    end = jnp.int32(0)
    for s in range(seg_ref.shape[0]):
        end = end + seg_ref[s]
        crossed = crossed + jnp.where(column >= end, 1, 0)
    insulated = jnp.concatenate([(crossed % 2)[:1, :]] * units, axis=1) == 1
    extent = groups * rows
    width = units * lanes
    for i in range(units):
        at = i * lanes
        both[:, at : at + lanes], both[:, width + at : width + at + lanes] = halves(
            x_ref[:, i].reshape(extent, lanes)
        )
    step = 128
    for k in range(0, extent, step):
        cut = slice(k, k + step)
        for c in range(2):
            high[c, cut], low[c, cut] = halves(w_ref[c, cut])

    def solve(c, cut):
        d = jnp.dot(high[c, cut], both[...], preferred_element_type=jnp.float32)
        e = jnp.dot(low[c, cut], both[:, :width], preferred_element_type=jnp.float32)
        return d[:, :width] + (d[:, width:] + e)

    for k in range(0, extent, step):
        cut = slice(k, k + step)
        solved = jnp.where(insulated, solve(1, cut), solve(0, cut))
        for i in range(units):
            piece = solved[:, i * lanes : (i + 1) * lanes]
            out_ref[k // rows : (k + step) // rows, i] = piece.reshape(step // rows, rows, lanes)


def column_solve(here, segments, w, x, blocks):
    return pl.pallas_call(
        functools.partial(column_kernel, blocks),
        in_specs=[SMEM, SMEM, VMEM, VMEM],
        out_specs=VMEM,
        out_shape=jax.ShapeDtypeStruct(x.shape, jnp.float32),
        scratch_shapes=[pltpu.VMEM(w.shape, jnp.bfloat16)] * 2
        + [pltpu.VMEM((w.shape[1], 2 * x.shape[1] * LANES), jnp.bfloat16)],
        compiler_params=pltpu.CompilerParams(vmem_limit_bytes=32 * 2**20),
        cost_estimate=pl.CostEstimate(
            flops=12 * w.shape[1] * x.size, bytes_accessed=4 * 2**20, transcendentals=0
        ),
        name="column_solve",
    )(here, segments, w, x)


def place_kernel(x_ref, out_ref):
    groups = x_ref.shape[0]
    blocks = out_ref.shape[2] // LANES
    for p in range(groups):
        q, b = p // blocks, p % blocks
        out_ref[3 * q : 3 * q + 3, :, b * LANES : (b + 1) * LANES] = x_ref[p]


def place(x, shape):
    return pl.pallas_call(
        place_kernel,
        in_specs=[VMEM],
        out_specs=VMEM,
        out_shape=jax.ShapeDtypeStruct(shape, jnp.float32),
        compiler_params=pltpu.CompilerParams(vmem_limit_bytes=16 * 2**20),
        name="place",
    )(x)


def swapped(x):
    return lax.all_to_all(x, "pencil", split_axis=0, concat_axis=0, tiled=True)


def on_device(t, u, v, w, downstream_solver_matrix, wallward_solver_matrices, wall_segments):
    planes, rows, nx = t.shape
    slabs, groups = lax.axis_size("slab"), lax.axis_size("pencil")
    here = lax.axis_index(("slab", "pencil")).astype(jnp.int32).reshape(1)
    yc, yd, za, zb, t_halves = edges(here, t, groups)
    yc = lax.ppermute(yc, "slab", [(i, i ^ 1) for i in range(slabs)])
    yd = lax.ppermute(yd, "slab", [(i, ((i - 1) ^ 1) + 1 & slabs - 1) for i in range(slabs)])
    za = lax.ppermute(za, "pencil", [(i, ((i - 1) ^ 1) + 1) for i in range(1, groups - 1)])
    zb = lax.ppermute(zb, "pencil", [(i, i ^ 1) for i in range(groups)])
    halos = yc, yd, za, zb
    *parts, ah, al = prepare(here, t_halves, u, v, w, downstream_solver_matrix, groups)
    x = swapped(row_solve(here, parts, halos, ah, al, groups))
    x = swapped(column_solve(here, wall_segments, wallward_solver_matrices, x, nx // LANES))
    return place(x, t.shape)


def solution(mesh):
    field = P("slab", "pencil", None)
    return jax.shard_map(
        on_device,
        mesh=mesh,
        in_specs=(field, field, field, field, P(), P(), P()),
        out_specs=field,
        check_vma=False,
    )
```

```python
import functools

import jax
import jax.numpy as jnp
from jax import lax
from jax.experimental import pallas as pl
from jax.experimental.pallas import tpu as pltpu
from jax.sharding import PartitionSpec as P

TRANSPORT_PART = 0.25
CONDUCTION_PART = 0.2
LANES = 128
VMEM = pl.BlockSpec(memory_space=pltpu.VMEM)
HBM = pl.BlockSpec(memory_space=pltpu.HBM)
SMEM = pl.BlockSpec(memory_space=pltpu.SMEM)


def metric_of(levels, extent):
    return 0.5 / (1.0 + jnp.sin(jnp.pi * (levels + 0.5) / extent))


def pinned(x):
    return pltpu.with_memory_space_constraint(x, pltpu.HBM)


def halves(wide):
    high = wide.astype(jnp.bfloat16)
    return high, (wide - high.astype(jnp.float32)).astype(jnp.bfloat16)


def edge_kernel(groups, here_ref, t_hbm, yc_ref, yd_ref, za_ref, zb_ref, buf, sems):
    planes, rows, _ = t_hbm.shape
    half = buf.shape[2]
    cuts = (sems.shape[0] - 2) // 2
    some = planes // cuts
    pencil_even, slab_even = here_ref[0] % 2 == 0, here_ref[0] // groups % 2 == 0
    ends = [
        pltpu.make_async_copy(t_hbm.at[jnp.where(slab_even, planes - 1, 0)], yc_ref, sems.at[0]),
        pltpu.make_async_copy(t_hbm.at[jnp.where(slab_even, 0, planes - 1)], yd_ref, sems.at[1]),
    ]
    copies = []
    for i in range(cuts):
        for h in range(2):
            source = t_hbm.at[pl.ds(i * some, some), pl.ds(h * half, half)]
            copies.append(pltpu.make_async_copy(source, buf.at[h, pl.ds(i * some, some)], sems.at[2 + 2 * i + h]))
    for copy in copies + ends:
        copy.start()
    for copy in copies:
        copy.wait()
    for y in range(planes):
        low, high = buf[0, y, :1, :], buf[1, y, half - 1 :, :]
        za_ref[y : y + 1, :] = jnp.where(pencil_even, low, high)
        zb_ref[y : y + 1, :] = jnp.where(pencil_even, high, low)
    for copy in ends:
        copy.wait()


def edges(here, t, groups):
    planes, rows, nx = t.shape
    half = rows // 2
    plane = jax.ShapeDtypeStruct((rows, nx), t.dtype)
    level = jax.ShapeDtypeStruct((planes, nx), t.dtype)
    return pl.pallas_call(
        functools.partial(edge_kernel, groups),
        in_specs=[SMEM, HBM],
        out_specs=[VMEM] * 5,
        out_shape=[plane, plane, level, level, jax.ShapeDtypeStruct((2, planes, half, nx), t.dtype)],
        scratch_shapes=[pltpu.SemaphoreType.DMA((10,))],
        compiler_params=pltpu.CompilerParams(vmem_limit_bytes=8 * 2**20),
        name="edges",
    )(here, pinned(t))


def prepare_kernel(
    groups,
    here_ref,
    t_ref,
    u_hbm,
    v_hbm,
    w_hbm,
    a_hbm,
    side_ref,
    cb_ref,
    ca_ref,
    cl_ref,
    ch_ref,
    ah_ref,
    al_ref,
    u_ref,
    v_ref,
    w_ref,
    along_ref,
    wallward_ref,
    a_buf,
    sems,
):
    planes, rows, nx = side_ref.shape
    parts = sems.shape[0] - 3
    a_rows = a_buf.shape[0] // parts
    fields = [
        pltpu.make_async_copy(source, target, sems.at[i])
        for i, (source, target) in enumerate(((u_hbm, u_ref), (v_hbm, v_ref), (w_hbm, w_ref)))
    ]
    copies = []
    for i in range(parts):
        cut = slice(i * a_rows, (i + 1) * a_rows)
        copies.append(pltpu.make_async_copy(a_hbm.at[cut], a_buf.at[cut], sems.at[3 + i]))
    for copy in fields + copies:
        copy.start()
    levels = (lax.broadcasted_iota(jnp.int32, (rows, LANES), 0) + here_ref[0] % groups * rows).astype(jnp.float32)
    metric = jnp.concatenate([metric_of(levels, groups * rows)] * (nx // LANES), axis=1)
    level = lax.broadcasted_iota(jnp.int32, (rows, nx), 0)

    def plane(y):
        if y < 0 or y == planes:
            return jnp.zeros((rows, nx), jnp.float32)
        return jnp.concatenate([t_ref[0, y], t_ref[1, y]], axis=0)

    own = (1.0 - 3.0 * CONDUCTION_PART) - CONDUCTION_PART * metric
    near, far = 0.5 * CONDUCTION_PART * metric, TRANSPORT_PART * metric
    for y in range(planes):
        t, ahead, behind = plane(y), plane(y + 1), plane(y - 1)
        east = pltpu.roll(t, nx - 1, 1)
        west = pltpu.roll(t, 1, 1)
        above = jnp.where(level == rows - 1, 0.0, pltpu.roll(t, rows - 1, 0))
        below = jnp.where(level == 0, 0.0, pltpu.roll(t, 1, 0))
        side_ref[y] = (
            own * t
            + CONDUCTION_PART * (ahead + behind)
            + 0.5 * CONDUCTION_PART * (east + west)
            + near * (above + below)
        )
        along_ref[y] = 0.5 * TRANSPORT_PART * (east - west)
        wallward_ref[y] = far * (above - below)
    for copy in fields:
        copy.wait()
    for y in range(planes):
        u = u_ref[y].astype(jnp.float32)
        v = v_ref[y].astype(jnp.float32)
        w = w_ref[y].astype(jnp.float32)
        across = 0.5 * TRANSPORT_PART * (plane(y + 1) - plane(y - 1))
        side_ref[y] = side_ref[y] - (u * along_ref[y] + v * across + w * wallward_ref[y])
        cl_ref[y : y + 1, :] = (metric * (0.5 * CONDUCTION_PART + TRANSPORT_PART * w))[:1, :]
        ch_ref[y : y + 1, :] = (metric * (0.5 * CONDUCTION_PART - TRANSPORT_PART * w))[rows - 1 :, :]
        if y == 0:
            cb_ref[...] = CONDUCTION_PART + 0.5 * TRANSPORT_PART * v
        if y == planes - 1:
            ca_ref[...] = CONDUCTION_PART - 0.5 * TRANSPORT_PART * v
    for i in range(parts):
        cut = slice(i * a_rows, (i + 1) * a_rows)
        copies[i].wait()
        ah_ref[cut], al_ref[cut] = halves(a_buf[cut])


def prepare(here, t, u, v, w, a, groups):
    planes, rows, nx = u.shape
    a16 = jax.ShapeDtypeStruct(a.shape, jnp.bfloat16)
    plane = jax.ShapeDtypeStruct((rows, nx), t.dtype)
    level = jax.ShapeDtypeStruct((planes, nx), t.dtype)
    parts = 8
    return pl.pallas_call(
        functools.partial(prepare_kernel, groups),
        in_specs=[SMEM, VMEM] + [HBM] * 4,
        out_specs=[VMEM] * 7,
        out_shape=[jax.ShapeDtypeStruct(u.shape, t.dtype), plane, plane, level, level, a16, a16],
        scratch_shapes=[pltpu.VMEM(x.shape, x.dtype) for x in (u, v, w)]
        + [pltpu.VMEM(u.shape, t.dtype)] * 2
        + [pltpu.VMEM(a.shape, a.dtype)]
        + [pltpu.SemaphoreType.DMA((3 + parts,))],
        compiler_params=pltpu.CompilerParams(vmem_limit_bytes=20 * 2**20),
        cost_estimate=pl.CostEstimate(
            flops=4 * a.size + 40 * t.size, bytes_accessed=8 * a.size + 14 * t.size, transcendentals=0
        ),
        name="prepare",
    )(here, t, *(pinned(x) for x in (u, v, w, a)))


def row_kernel(
    here_ref, side_ref, cb_ref, ca_ref, cl_ref, ch_ref, yc_ref, yd_ref, za_ref, zb_ref, ah_ref, al_ref, out_ref, both
):
    planes, rows, nx = side_ref.shape
    groups = out_ref.shape[0]
    pencil_even, slab_even = here_ref[0] % 2 == 0, here_ref[0] // groups % 2 == 0
    low = cl_ref[...] * jnp.where(pencil_even, za_ref[...], zb_ref[...])
    high = ch_ref[...] * jnp.where(pencil_even, zb_ref[...], za_ref[...])
    level = lax.broadcasted_iota(jnp.int32, (rows, nx), 0)
    extent = planes * rows
    for y in range(planes):
        side = side_ref[y]
        if y == 0:
            side = side + cb_ref[...] * jnp.where(slab_even, yd_ref[...], yc_ref[...])
        if y == planes - 1:
            side = side + ca_ref[...] * jnp.where(slab_even, yc_ref[...], yd_ref[...])
        side = side + jnp.where(level == 0, low[y : y + 1, :], 0.0)
        side = side + jnp.where(level == rows - 1, high[y : y + 1, :], 0.0)
        high_part, low_part = halves(side)
        both[y * rows : (y + 1) * rows, :] = high_part
        both[extent + y * rows : extent + (y + 1) * rows, :] = low_part
    wide = 2 * LANES
    unit_rows = 3 * rows
    blocks = nx // LANES
    for c in range(nx // wide):
        ah = ah_ref[c * wide : (c + 1) * wide, :]
        al = al_ref[c * wide : (c + 1) * wide, :]

        def dot(x, m):
            return lax.dot_general(x, m, (((1,), (1,)), ((), ())), preferred_element_type=jnp.float32)

        main = dot(both[...], ah)
        solved = main[:extent] + (dot(both[:extent, :], al) + main[extent:])
        for q in range(planes // 3):
            for h in range(2):
                piece = solved[q * unit_rows : (q + 1) * unit_rows, h * LANES : (h + 1) * LANES]
                out_ref[q * blocks + 2 * c + h] = piece.reshape(3, rows, LANES)


def row_solve(here, parts, halos, ah, al, groups):
    planes, rows, nx = parts[0].shape
    return pl.pallas_call(
        row_kernel,
        in_specs=[SMEM] + [VMEM] * 11,
        out_specs=VMEM,
        out_shape=jax.ShapeDtypeStruct((groups, 3, rows, LANES), jnp.float32),
        scratch_shapes=[pltpu.VMEM((2 * planes * rows, nx), jnp.bfloat16)],
        compiler_params=pltpu.CompilerParams(vmem_limit_bytes=32 * 2**20),
        cost_estimate=pl.CostEstimate(
            flops=6 * planes * rows * nx * nx, bytes_accessed=8 * 2**20, transcendentals=0
        ),
        name="row_solve",
    )(here, *parts, *halos, ah, al)


def column_kernel(blocks, here_ref, seg_ref, w_ref, x_ref, out_ref):
    groups, units, rows, lanes = x_ref.shape
    column = lax.broadcasted_iota(jnp.int32, (8, lanes), 1) + here_ref[0] % blocks * lanes
    crossed = jnp.zeros((8, lanes), jnp.int32)
    end = jnp.int32(0)
    for s in range(seg_ref.shape[0]):
        end = end + seg_ref[s]
        crossed = crossed + jnp.where(column >= end, 1, 0)
    insulated = jnp.concatenate([(crossed % 2)[:1, :]] * units, axis=1) == 1
    extent = groups * rows
    lines = jnp.concatenate([x_ref[:, i].reshape(extent, lanes) for i in range(units)], axis=1)
    xh, xl = halves(lines)
    both = jnp.concatenate([xh, xl], axis=1)
    width = units * lanes

    def solve(c, cut):
        wh, wl = halves(w_ref[c, cut])
        d = jnp.dot(wh, both, preferred_element_type=jnp.float32)
        e = jnp.dot(wl, xh, preferred_element_type=jnp.float32)
        return d[:, :width] + (d[:, width:] + e)

    step = 256
    for k in range(0, extent, step):
        cut = slice(k, k + step)
        solved = jnp.where(insulated, solve(1, cut), solve(0, cut))
        for i in range(units):
            piece = solved[:, i * lanes : (i + 1) * lanes]
            out_ref[k // rows : (k + step) // rows, i] = piece.reshape(step // rows, rows, lanes)


def column_solve(here, segments, w, x, blocks):
    return pl.pallas_call(
        functools.partial(column_kernel, blocks),
        in_specs=[SMEM, SMEM, VMEM, VMEM],
        out_specs=VMEM,
        out_shape=jax.ShapeDtypeStruct(x.shape, jnp.float32),
        compiler_params=pltpu.CompilerParams(vmem_limit_bytes=32 * 2**20),
        cost_estimate=pl.CostEstimate(
            flops=12 * w.shape[1] * x.size, bytes_accessed=4 * 2**20, transcendentals=0
        ),
        name="column_solve",
    )(here, segments, w, x)


def place_kernel(x_ref, out_ref):
    groups = x_ref.shape[0]
    blocks = out_ref.shape[2] // LANES
    for p in range(groups):
        q, b = p // blocks, p % blocks
        out_ref[3 * q : 3 * q + 3, :, b * LANES : (b + 1) * LANES] = x_ref[p]


def place(x, shape):
    return pl.pallas_call(
        place_kernel,
        in_specs=[VMEM],
        out_specs=VMEM,
        out_shape=jax.ShapeDtypeStruct(shape, jnp.float32),
        compiler_params=pltpu.CompilerParams(vmem_limit_bytes=16 * 2**20),
        name="place",
    )(x)


def swapped(x):
    return lax.all_to_all(x, "pencil", split_axis=0, concat_axis=0, tiled=True)


def on_device(t, u, v, w, downstream_solver_matrix, wallward_solver_matrices, wall_segments):
    planes, rows, nx = t.shape
    slabs, groups = lax.axis_size("slab"), lax.axis_size("pencil")
    here = lax.axis_index(("slab", "pencil")).astype(jnp.int32).reshape(1)
    yc, yd, za, zb, t_halves = edges(here, t, groups)
    yc = lax.ppermute(yc, "slab", [(i, i ^ 1) for i in range(slabs)])
    yd = lax.ppermute(yd, "slab", [(i, ((i - 1) ^ 1) + 1 & slabs - 1) for i in range(slabs)])
    za = lax.ppermute(za, "pencil", [(i, ((i - 1) ^ 1) + 1) for i in range(1, groups - 1)])
    zb = lax.ppermute(zb, "pencil", [(i, i ^ 1) for i in range(groups)])
    halos = yc, yd, za, zb
    *parts, ah, al = prepare(here, t_halves, u, v, w, downstream_solver_matrix, groups)
    x = swapped(row_solve(here, parts, halos, ah, al, groups))
    x = swapped(column_solve(here, wall_segments, wallward_solver_matrices, x, nx // LANES))
    return place(x, t.shape)


def solution(mesh):
    field = P("slab", "pencil", None)
    return jax.shard_map(
        on_device,
        mesh=mesh,
        in_specs=(field, field, field, field, P(), P(), P()),
        out_specs=field,
        check_vma=False,
    )
```

```python
import functools

import jax
import jax.numpy as jnp
from jax import lax
from jax.experimental import pallas as pl
from jax.experimental.pallas import tpu as pltpu
from jax.sharding import PartitionSpec as P

TRANSPORT_PART = 0.25
CONDUCTION_PART = 0.2
LANES = 128
VMEM = pl.BlockSpec(memory_space=pltpu.VMEM)
HBM = pl.BlockSpec(memory_space=pltpu.HBM)
SMEM = pl.BlockSpec(memory_space=pltpu.SMEM)


def metric_of(levels, extent):
    return 0.5 / (1.0 + jnp.sin(jnp.pi * (levels + 0.5) / extent))


def pinned(x):
    return pltpu.with_memory_space_constraint(x, pltpu.HBM)


def halves(wide):
    high = wide.astype(jnp.bfloat16)
    return high, (wide - high.astype(jnp.float32)).astype(jnp.bfloat16)


def edge_kernel(groups, here_ref, t_hbm, yc_ref, yd_ref, za_ref, zb_ref, buf, sems):
    planes, rows, _ = t_hbm.shape
    pencil_even, slab_even = here_ref[0] % 2 == 0, here_ref[0] // groups % 2 == 0
    copies = [
        pltpu.make_async_copy(t_hbm, buf, sems.at[0]),
        pltpu.make_async_copy(t_hbm.at[jnp.where(slab_even, planes - 1, 0)], yc_ref, sems.at[1]),
        pltpu.make_async_copy(t_hbm.at[jnp.where(slab_even, 0, planes - 1)], yd_ref, sems.at[2]),
    ]
    for copy in copies:
        copy.start()
    copies[0].wait()
    for y in range(planes):
        low, high = buf[y, :1, :], buf[y, rows - 1 :, :]
        za_ref[y : y + 1, :] = jnp.where(pencil_even, low, high)
        zb_ref[y : y + 1, :] = jnp.where(pencil_even, high, low)
    copies[1].wait()
    copies[2].wait()


def edges(here, t, groups):
    planes, rows, nx = t.shape
    plane = jax.ShapeDtypeStruct((rows, nx), t.dtype)
    level = jax.ShapeDtypeStruct((planes, nx), t.dtype)
    return pl.pallas_call(
        functools.partial(edge_kernel, groups),
        in_specs=[SMEM, HBM],
        out_specs=[VMEM] * 5,
        out_shape=[plane, plane, level, level, jax.ShapeDtypeStruct(t.shape, t.dtype)],
        scratch_shapes=[pltpu.SemaphoreType.DMA((3,))],
        compiler_params=pltpu.CompilerParams(vmem_limit_bytes=8 * 2**20),
        name="edges",
    )(here, pinned(t))


def prepare_kernel(
    groups,
    here_ref,
    t_ref,
    u_hbm,
    v_hbm,
    w_hbm,
    a_hbm,
    side_ref,
    cb_ref,
    ca_ref,
    cl_ref,
    ch_ref,
    ah_ref,
    al_ref,
    u_ref,
    v_ref,
    w_ref,
    along_ref,
    wallward_ref,
    a_buf,
    sems,
):
    planes, rows, nx = side_ref.shape
    parts = sems.shape[0] - 3
    a_rows = a_buf.shape[0] // parts
    fields = [
        pltpu.make_async_copy(source, target, sems.at[i])
        for i, (source, target) in enumerate(((u_hbm, u_ref), (v_hbm, v_ref), (w_hbm, w_ref)))
    ]
    copies = []
    for i in range(parts):
        cut = slice(i * a_rows, (i + 1) * a_rows)
        copies.append(pltpu.make_async_copy(a_hbm.at[cut], a_buf.at[cut], sems.at[3 + i]))
    for copy in fields + copies:
        copy.start()
    levels = (lax.broadcasted_iota(jnp.int32, (rows, LANES), 0) + here_ref[0] % groups * rows).astype(jnp.float32)
    metric = jnp.concatenate([metric_of(levels, groups * rows)] * (nx // LANES), axis=1)
    level = lax.broadcasted_iota(jnp.int32, (rows, nx), 0)

    def plane(y):
        if y < 0 or y == planes:
            return jnp.zeros((rows, nx), jnp.float32)
        return t_ref[y]

    own = (1.0 - 3.0 * CONDUCTION_PART) - CONDUCTION_PART * metric
    near, far = 0.5 * CONDUCTION_PART * metric, TRANSPORT_PART * metric
    for y in range(planes):
        t, ahead, behind = plane(y), plane(y + 1), plane(y - 1)
        east = pltpu.roll(t, nx - 1, 1)
        west = pltpu.roll(t, 1, 1)
        above = jnp.where(level == rows - 1, 0.0, pltpu.roll(t, rows - 1, 0))
        below = jnp.where(level == 0, 0.0, pltpu.roll(t, 1, 0))
        side_ref[y] = (
            own * t
            + CONDUCTION_PART * (ahead + behind)
            + 0.5 * CONDUCTION_PART * (east + west)
            + near * (above + below)
        )
        along_ref[y] = 0.5 * TRANSPORT_PART * (east - west)
        wallward_ref[y] = far * (above - below)
    for copy in fields:
        copy.wait()
    for y in range(planes):
        u = u_ref[y].astype(jnp.float32)
        v = v_ref[y].astype(jnp.float32)
        w = w_ref[y].astype(jnp.float32)
        across = 0.5 * TRANSPORT_PART * (plane(y + 1) - plane(y - 1))
        side_ref[y] = side_ref[y] - (u * along_ref[y] + v * across + w * wallward_ref[y])
        cl_ref[y : y + 1, :] = (metric * (0.5 * CONDUCTION_PART + TRANSPORT_PART * w))[:1, :]
        ch_ref[y : y + 1, :] = (metric * (0.5 * CONDUCTION_PART - TRANSPORT_PART * w))[rows - 1 :, :]
        if y == 0:
            cb_ref[...] = CONDUCTION_PART + 0.5 * TRANSPORT_PART * v
        if y == planes - 1:
            ca_ref[...] = CONDUCTION_PART - 0.5 * TRANSPORT_PART * v
    for i in range(parts):
        cut = slice(i * a_rows, (i + 1) * a_rows)
        copies[i].wait()
        ah_ref[cut], al_ref[cut] = halves(a_buf[cut])


def prepare(here, t, u, v, w, a, groups):
    planes, rows, nx = u.shape
    a16 = jax.ShapeDtypeStruct(a.shape, jnp.bfloat16)
    plane = jax.ShapeDtypeStruct((rows, nx), t.dtype)
    level = jax.ShapeDtypeStruct((planes, nx), t.dtype)
    parts = 4
    return pl.pallas_call(
        functools.partial(prepare_kernel, groups),
        in_specs=[SMEM, VMEM] + [HBM] * 4,
        out_specs=[VMEM] * 7,
        out_shape=[jax.ShapeDtypeStruct(u.shape, t.dtype), plane, plane, level, level, a16, a16],
        scratch_shapes=[pltpu.VMEM(x.shape, x.dtype) for x in (u, v, w)]
        + [pltpu.VMEM(u.shape, t.dtype)] * 2
        + [pltpu.VMEM(a.shape, a.dtype)]
        + [pltpu.SemaphoreType.DMA((3 + parts,))],
        compiler_params=pltpu.CompilerParams(vmem_limit_bytes=20 * 2**20),
        cost_estimate=pl.CostEstimate(
            flops=4 * a.size + 40 * t.size, bytes_accessed=8 * a.size + 14 * t.size, transcendentals=0
        ),
        name="prepare",
    )(here, t, *(pinned(x) for x in (u, v, w, a)))


def row_kernel(
    here_ref, side_ref, cb_ref, ca_ref, cl_ref, ch_ref, yc_ref, yd_ref, za_ref, zb_ref, ah_ref, al_ref, out_ref, both
):
    planes, rows, nx = side_ref.shape
    groups = out_ref.shape[0]
    pencil_even, slab_even = here_ref[0] % 2 == 0, here_ref[0] // groups % 2 == 0
    low = cl_ref[...] * jnp.where(pencil_even, za_ref[...], zb_ref[...])
    high = ch_ref[...] * jnp.where(pencil_even, zb_ref[...], za_ref[...])
    level = lax.broadcasted_iota(jnp.int32, (rows, nx), 0)
    extent = planes * rows
    for y in range(planes):
        side = side_ref[y]
        if y == 0:
            side = side + cb_ref[...] * jnp.where(slab_even, yd_ref[...], yc_ref[...])
        if y == planes - 1:
            side = side + ca_ref[...] * jnp.where(slab_even, yc_ref[...], yd_ref[...])
        side = side + jnp.where(level == 0, low[y : y + 1, :], 0.0)
        side = side + jnp.where(level == rows - 1, high[y : y + 1, :], 0.0)
        high_part, low_part = halves(side)
        both[y * rows : (y + 1) * rows, :] = high_part
        both[extent + y * rows : extent + (y + 1) * rows, :] = low_part
    wide = 2 * LANES
    unit_rows = 3 * rows
    blocks = nx // LANES
    for c in range(nx // wide):
        ah = ah_ref[c * wide : (c + 1) * wide, :]
        al = al_ref[c * wide : (c + 1) * wide, :]

        def dot(x, m):
            return lax.dot_general(x, m, (((1,), (1,)), ((), ())), preferred_element_type=jnp.float32)

        main = dot(both[...], ah)
        solved = main[:extent] + (dot(both[:extent, :], al) + main[extent:])
        for q in range(planes // 3):
            for h in range(2):
                piece = solved[q * unit_rows : (q + 1) * unit_rows, h * LANES : (h + 1) * LANES]
                out_ref[q * blocks + 2 * c + h] = piece.reshape(3, rows, LANES)


def row_solve(here, parts, halos, ah, al, groups):
    planes, rows, nx = parts[0].shape
    return pl.pallas_call(
        row_kernel,
        in_specs=[SMEM] + [VMEM] * 11,
        out_specs=VMEM,
        out_shape=jax.ShapeDtypeStruct((groups, 3, rows, LANES), jnp.float32),
        scratch_shapes=[pltpu.VMEM((2 * planes * rows, nx), jnp.bfloat16)],
        compiler_params=pltpu.CompilerParams(vmem_limit_bytes=32 * 2**20),
        cost_estimate=pl.CostEstimate(
            flops=6 * planes * rows * nx * nx, bytes_accessed=8 * 2**20, transcendentals=0
        ),
        name="row_solve",
    )(here, *parts, *halos, ah, al)


def column_kernel(blocks, here_ref, seg_ref, w_ref, x_ref, out_ref):
    groups, units, rows, lanes = x_ref.shape
    column = lax.broadcasted_iota(jnp.int32, (8, lanes), 1) + here_ref[0] % blocks * lanes
    crossed = jnp.zeros((8, lanes), jnp.int32)
    end = jnp.int32(0)
    for s in range(seg_ref.shape[0]):
        end = end + seg_ref[s]
        crossed = crossed + jnp.where(column >= end, 1, 0)
    insulated = jnp.concatenate([(crossed % 2)[:1, :]] * units, axis=1) == 1
    extent = groups * rows
    lines = jnp.concatenate([x_ref[:, i].reshape(extent, lanes) for i in range(units)], axis=1)
    xh, xl = halves(lines)
    both = jnp.concatenate([xh, xl], axis=1)
    width = units * lanes

    def solve(c, cut):
        wh, wl = halves(w_ref[c, cut])
        d = jnp.dot(wh, both, preferred_element_type=jnp.float32)
        e = jnp.dot(wl, xh, preferred_element_type=jnp.float32)
        return d[:, :width] + (d[:, width:] + e)

    step = 256
    for k in range(0, extent, step):
        cut = slice(k, k + step)
        solved = jnp.where(insulated, solve(1, cut), solve(0, cut))
        for i in range(units):
            piece = solved[:, i * lanes : (i + 1) * lanes]
            out_ref[k // rows : (k + step) // rows, i] = piece.reshape(step // rows, rows, lanes)


def column_solve(here, segments, w, x, blocks):
    return pl.pallas_call(
        functools.partial(column_kernel, blocks),
        in_specs=[SMEM, SMEM, VMEM, VMEM],
        out_specs=VMEM,
        out_shape=jax.ShapeDtypeStruct(x.shape, jnp.float32),
        compiler_params=pltpu.CompilerParams(vmem_limit_bytes=32 * 2**20),
        cost_estimate=pl.CostEstimate(
            flops=12 * w.shape[1] * x.size, bytes_accessed=4 * 2**20, transcendentals=0
        ),
        name="column_solve",
    )(here, segments, w, x)


def place_kernel(x_ref, out_ref):
    groups = x_ref.shape[0]
    blocks = out_ref.shape[2] // LANES
    for p in range(groups):
        q, b = p // blocks, p % blocks
        out_ref[3 * q : 3 * q + 3, :, b * LANES : (b + 1) * LANES] = x_ref[p]


def place(x, shape):
    return pl.pallas_call(
        place_kernel,
        in_specs=[VMEM],
        out_specs=VMEM,
        out_shape=jax.ShapeDtypeStruct(shape, jnp.float32),
        compiler_params=pltpu.CompilerParams(vmem_limit_bytes=16 * 2**20),
        name="place",
    )(x)


def swapped(x):
    return lax.all_to_all(x, "pencil", split_axis=0, concat_axis=0, tiled=True)


def on_device(t, u, v, w, downstream_solver_matrix, wallward_solver_matrices, wall_segments):
    planes, rows, nx = t.shape
    slabs, groups = lax.axis_size("slab"), lax.axis_size("pencil")
    here = lax.axis_index(("slab", "pencil")).astype(jnp.int32).reshape(1)
    yc, yd, za, zb, t_here = edges(here, t, groups)
    yc = lax.ppermute(yc, "slab", [(i, i ^ 1) for i in range(slabs)])
    yd = lax.ppermute(yd, "slab", [(i, ((i - 1) ^ 1) + 1 & slabs - 1) for i in range(slabs)])
    za = lax.ppermute(za, "pencil", [(i, ((i - 1) ^ 1) + 1) for i in range(1, groups - 1)])
    zb = lax.ppermute(zb, "pencil", [(i, i ^ 1) for i in range(groups)])
    halos = yc, yd, za, zb
    *parts, ah, al = prepare(here, t_here, u, v, w, downstream_solver_matrix, groups)
    x = swapped(row_solve(here, parts, halos, ah, al, groups))
    x = swapped(column_solve(here, wall_segments, wallward_solver_matrices, x, nx // LANES))
    return place(x, t.shape)


def solution(mesh):
    field = P("slab", "pencil", None)
    return jax.shard_map(
        on_device,
        mesh=mesh,
        in_specs=(field, field, field, field, P(), P(), P()),
        out_specs=field,
        check_vma=False,
    )
```

```python
import functools

import jax
import jax.numpy as jnp
from jax import lax
from jax.experimental import pallas as pl
from jax.experimental.pallas import tpu as pltpu
from jax.sharding import PartitionSpec as P

TRANSPORT_PART = 0.25
CONDUCTION_PART = 0.2
LANES = 128
VMEM = pl.BlockSpec(memory_space=pltpu.VMEM)
HBM = pl.BlockSpec(memory_space=pltpu.HBM)
SMEM = pl.BlockSpec(memory_space=pltpu.SMEM)


def metric_of(levels, extent):
    return 0.5 / (1.0 + jnp.sin(jnp.pi * (levels + 0.5) / extent))


def pinned(x):
    return pltpu.with_memory_space_constraint(x, pltpu.HBM)


def halves(wide):
    high = wide.astype(jnp.bfloat16)
    return high, (wide - high.astype(jnp.float32)).astype(jnp.bfloat16)


def edge_kernel(groups, here_ref, t_hbm, yc_ref, yd_ref, za_ref, zb_ref, buf, sem):
    planes, rows, _ = t_hbm.shape
    pencil_even, slab_even = here_ref[0] % 2 == 0, here_ref[0] // groups % 2 == 0
    copy = pltpu.make_async_copy(t_hbm, buf, sem)
    copy.start()
    copy.wait()
    yc_ref[...] = jnp.where(slab_even, buf[planes - 1], buf[0])
    yd_ref[...] = jnp.where(slab_even, buf[0], buf[planes - 1])
    for y in range(planes):
        low, high = buf[y, :1, :], buf[y, rows - 1 :, :]
        za_ref[y : y + 1, :] = jnp.where(pencil_even, low, high)
        zb_ref[y : y + 1, :] = jnp.where(pencil_even, high, low)


def edges(here, t, groups):
    planes, rows, nx = t.shape
    plane = jax.ShapeDtypeStruct((rows, nx), t.dtype)
    level = jax.ShapeDtypeStruct((planes, nx), t.dtype)
    return pl.pallas_call(
        functools.partial(edge_kernel, groups),
        in_specs=[SMEM, HBM],
        out_specs=[VMEM] * 5,
        out_shape=[plane, plane, level, level, jax.ShapeDtypeStruct(t.shape, t.dtype)],
        scratch_shapes=[pltpu.SemaphoreType.DMA],
        compiler_params=pltpu.CompilerParams(vmem_limit_bytes=8 * 2**20),
        name="edges",
    )(here, pinned(t))


def prepare_kernel(
    groups,
    here_ref,
    t_ref,
    u_hbm,
    v_hbm,
    w_hbm,
    a_hbm,
    side_ref,
    cb_ref,
    ca_ref,
    cl_ref,
    ch_ref,
    ah_ref,
    al_ref,
    u_ref,
    v_ref,
    w_ref,
    along_ref,
    wallward_ref,
    a_buf,
    sems,
):
    planes, rows, nx = side_ref.shape
    parts = sems.shape[0] - 3
    a_rows = a_buf.shape[0] // parts
    fields = [
        pltpu.make_async_copy(source, target, sems.at[i])
        for i, (source, target) in enumerate(((u_hbm, u_ref), (v_hbm, v_ref), (w_hbm, w_ref)))
    ]
    copies = []
    for i in range(parts):
        cut = slice(i * a_rows, (i + 1) * a_rows)
        copies.append(pltpu.make_async_copy(a_hbm.at[cut], a_buf.at[cut], sems.at[3 + i]))
    for copy in fields + copies:
        copy.start()
    levels = (lax.broadcasted_iota(jnp.int32, (rows, LANES), 0) + here_ref[0] % groups * rows).astype(jnp.float32)
    metric = jnp.concatenate([metric_of(levels, groups * rows)] * (nx // LANES), axis=1)
    level = lax.broadcasted_iota(jnp.int32, (rows, nx), 0)

    def plane(y):
        if y < 0 or y == planes:
            return jnp.zeros((rows, nx), jnp.float32)
        return t_ref[y]

    own = (1.0 - 3.0 * CONDUCTION_PART) - CONDUCTION_PART * metric
    near, far = 0.5 * CONDUCTION_PART * metric, TRANSPORT_PART * metric
    for y in range(planes):
        t, ahead, behind = plane(y), plane(y + 1), plane(y - 1)
        east = pltpu.roll(t, nx - 1, 1)
        west = pltpu.roll(t, 1, 1)
        above = jnp.where(level == rows - 1, 0.0, pltpu.roll(t, rows - 1, 0))
        below = jnp.where(level == 0, 0.0, pltpu.roll(t, 1, 0))
        side_ref[y] = (
            own * t
            + CONDUCTION_PART * (ahead + behind)
            + 0.5 * CONDUCTION_PART * (east + west)
            + near * (above + below)
        )
        along_ref[y] = 0.5 * TRANSPORT_PART * (east - west)
        wallward_ref[y] = far * (above - below)
    for copy in fields:
        copy.wait()
    for y in range(planes):
        u = u_ref[y].astype(jnp.float32)
        v = v_ref[y].astype(jnp.float32)
        w = w_ref[y].astype(jnp.float32)
        across = 0.5 * TRANSPORT_PART * (plane(y + 1) - plane(y - 1))
        side_ref[y] = side_ref[y] - (u * along_ref[y] + v * across + w * wallward_ref[y])
        cl_ref[y : y + 1, :] = (metric * (0.5 * CONDUCTION_PART + TRANSPORT_PART * w))[:1, :]
        ch_ref[y : y + 1, :] = (metric * (0.5 * CONDUCTION_PART - TRANSPORT_PART * w))[rows - 1 :, :]
        if y == 0:
            cb_ref[...] = CONDUCTION_PART + 0.5 * TRANSPORT_PART * v
        if y == planes - 1:
            ca_ref[...] = CONDUCTION_PART - 0.5 * TRANSPORT_PART * v
    for i in range(parts):
        cut = slice(i * a_rows, (i + 1) * a_rows)
        copies[i].wait()
        ah_ref[cut], al_ref[cut] = halves(a_buf[cut])


def prepare(here, t, u, v, w, a, groups):
    planes, rows, nx = u.shape
    a16 = jax.ShapeDtypeStruct(a.shape, jnp.bfloat16)
    plane = jax.ShapeDtypeStruct((rows, nx), t.dtype)
    level = jax.ShapeDtypeStruct((planes, nx), t.dtype)
    parts = 4
    return pl.pallas_call(
        functools.partial(prepare_kernel, groups),
        in_specs=[SMEM, VMEM] + [HBM] * 4,
        out_specs=[VMEM] * 7,
        out_shape=[jax.ShapeDtypeStruct(u.shape, t.dtype), plane, plane, level, level, a16, a16],
        scratch_shapes=[pltpu.VMEM(x.shape, x.dtype) for x in (u, v, w)]
        + [pltpu.VMEM(u.shape, t.dtype)] * 2
        + [pltpu.VMEM(a.shape, a.dtype)]
        + [pltpu.SemaphoreType.DMA((3 + parts,))],
        compiler_params=pltpu.CompilerParams(vmem_limit_bytes=20 * 2**20),
        cost_estimate=pl.CostEstimate(
            flops=4 * a.size + 40 * t.size, bytes_accessed=8 * a.size + 14 * t.size, transcendentals=0
        ),
        name="prepare",
    )(here, t, *(pinned(x) for x in (u, v, w, a)))


def row_kernel(
    here_ref, side_ref, cb_ref, ca_ref, cl_ref, ch_ref, yc_ref, yd_ref, za_ref, zb_ref, ah_ref, al_ref, out_ref, both
):
    planes, rows, nx = side_ref.shape
    groups = out_ref.shape[0]
    pencil_even, slab_even = here_ref[0] % 2 == 0, here_ref[0] // groups % 2 == 0
    low = cl_ref[...] * jnp.where(pencil_even, za_ref[...], zb_ref[...])
    high = ch_ref[...] * jnp.where(pencil_even, zb_ref[...], za_ref[...])
    level = lax.broadcasted_iota(jnp.int32, (rows, nx), 0)
    extent = planes * rows
    for y in range(planes):
        side = side_ref[y]
        if y == 0:
            side = side + cb_ref[...] * jnp.where(slab_even, yd_ref[...], yc_ref[...])
        if y == planes - 1:
            side = side + ca_ref[...] * jnp.where(slab_even, yc_ref[...], yd_ref[...])
        side = side + jnp.where(level == 0, low[y : y + 1, :], 0.0)
        side = side + jnp.where(level == rows - 1, high[y : y + 1, :], 0.0)
        high_part, low_part = halves(side)
        both[y * rows : (y + 1) * rows, :] = high_part
        both[extent + y * rows : extent + (y + 1) * rows, :] = low_part
    wide = 2 * LANES
    unit_rows = 3 * rows
    blocks = nx // LANES
    for c in range(nx // wide):
        ah = ah_ref[c * wide : (c + 1) * wide, :]
        al = al_ref[c * wide : (c + 1) * wide, :]

        def dot(x, m):
            return lax.dot_general(x, m, (((1,), (1,)), ((), ())), preferred_element_type=jnp.float32)

        main = dot(both[...], ah)
        solved = main[:extent] + (dot(both[:extent, :], al) + main[extent:])
        for q in range(planes // 3):
            for h in range(2):
                piece = solved[q * unit_rows : (q + 1) * unit_rows, h * LANES : (h + 1) * LANES]
                out_ref[q * blocks + 2 * c + h] = piece.reshape(3, rows, LANES)


def row_solve(here, parts, halos, ah, al, groups):
    planes, rows, nx = parts[0].shape
    return pl.pallas_call(
        row_kernel,
        in_specs=[SMEM] + [VMEM] * 11,
        out_specs=VMEM,
        out_shape=jax.ShapeDtypeStruct((groups, 3, rows, LANES), jnp.float32),
        scratch_shapes=[pltpu.VMEM((2 * planes * rows, nx), jnp.bfloat16)],
        compiler_params=pltpu.CompilerParams(vmem_limit_bytes=32 * 2**20),
        cost_estimate=pl.CostEstimate(
            flops=6 * planes * rows * nx * nx, bytes_accessed=8 * 2**20, transcendentals=0
        ),
        name="row_solve",
    )(here, *parts, *halos, ah, al)


def column_kernel(blocks, here_ref, seg_ref, w_ref, x_ref, out_ref):
    groups, units, rows, lanes = x_ref.shape
    column = lax.broadcasted_iota(jnp.int32, (8, lanes), 1) + here_ref[0] % blocks * lanes
    crossed = jnp.zeros((8, lanes), jnp.int32)
    end = jnp.int32(0)
    for s in range(seg_ref.shape[0]):
        end = end + seg_ref[s]
        crossed = crossed + jnp.where(column >= end, 1, 0)
    insulated = jnp.concatenate([(crossed % 2)[:1, :]] * units, axis=1) == 1
    extent = groups * rows
    lines = jnp.concatenate([x_ref[:, i].reshape(extent, lanes) for i in range(units)], axis=1)
    xh, xl = halves(lines)
    both = jnp.concatenate([xh, xl], axis=1)
    width = units * lanes

    def solve(c, cut):
        wh, wl = halves(w_ref[c, cut])
        d = jnp.dot(wh, both, preferred_element_type=jnp.float32)
        e = jnp.dot(wl, xh, preferred_element_type=jnp.float32)
        return d[:, :width] + (d[:, width:] + e)

    step = 256
    for k in range(0, extent, step):
        cut = slice(k, k + step)
        solved = jnp.where(insulated, solve(1, cut), solve(0, cut))
        for i in range(units):
            piece = solved[:, i * lanes : (i + 1) * lanes]
            out_ref[k // rows : (k + step) // rows, i] = piece.reshape(step // rows, rows, lanes)


def column_solve(here, segments, w, x, blocks):
    return pl.pallas_call(
        functools.partial(column_kernel, blocks),
        in_specs=[SMEM, SMEM, VMEM, VMEM],
        out_specs=VMEM,
        out_shape=jax.ShapeDtypeStruct(x.shape, jnp.float32),
        compiler_params=pltpu.CompilerParams(vmem_limit_bytes=32 * 2**20),
        cost_estimate=pl.CostEstimate(
            flops=12 * w.shape[1] * x.size, bytes_accessed=4 * 2**20, transcendentals=0
        ),
        name="column_solve",
    )(here, segments, w, x)


def place_kernel(x_ref, out_ref):
    groups = x_ref.shape[0]
    blocks = out_ref.shape[2] // LANES
    for p in range(groups):
        q, b = p // blocks, p % blocks
        out_ref[3 * q : 3 * q + 3, :, b * LANES : (b + 1) * LANES] = x_ref[p]


def place(x, shape):
    return pl.pallas_call(
        place_kernel,
        in_specs=[VMEM],
        out_specs=VMEM,
        out_shape=jax.ShapeDtypeStruct(shape, jnp.float32),
        compiler_params=pltpu.CompilerParams(vmem_limit_bytes=16 * 2**20),
        name="place",
    )(x)


def swapped(x):
    return lax.all_to_all(x, "pencil", split_axis=0, concat_axis=0, tiled=True)


def on_device(t, u, v, w, downstream_solver_matrix, wallward_solver_matrices, wall_segments):
    planes, rows, nx = t.shape
    slabs, groups = lax.axis_size("slab"), lax.axis_size("pencil")
    here = lax.axis_index(("slab", "pencil")).astype(jnp.int32).reshape(1)
    yc, yd, za, zb, t_here = edges(here, t, groups)
    yc = lax.ppermute(yc, "slab", [(i, i ^ 1) for i in range(slabs)])
    yd = lax.ppermute(yd, "slab", [(i, ((i - 1) ^ 1) + 1 & slabs - 1) for i in range(slabs)])
    za = lax.ppermute(za, "pencil", [(i, ((i - 1) ^ 1) + 1) for i in range(1, groups - 1)])
    zb = lax.ppermute(zb, "pencil", [(i, i ^ 1) for i in range(groups)])
    halos = yc, yd, za, zb
    *parts, ah, al = prepare(here, t_here, u, v, w, downstream_solver_matrix, groups)
    x = swapped(row_solve(here, parts, halos, ah, al, groups))
    x = swapped(column_solve(here, wall_segments, wallward_solver_matrices, x, nx // LANES))
    return place(x, t.shape)


def solution(mesh):
    field = P("slab", "pencil", None)
    return jax.shard_map(
        on_device,
        mesh=mesh,
        in_specs=(field, field, field, field, P(), P(), P()),
        out_specs=field,
        check_vma=False,
    )
```

```python
import functools

import jax
import jax.numpy as jnp
from jax import lax
from jax.experimental import pallas as pl
from jax.experimental.pallas import tpu as pltpu
from jax.sharding import PartitionSpec as P

TRANSPORT_PART = 0.25
CONDUCTION_PART = 0.2
LANES = 128
VMEM = pl.BlockSpec(memory_space=pltpu.VMEM)
HBM = pl.BlockSpec(memory_space=pltpu.HBM)
SMEM = pl.BlockSpec(memory_space=pltpu.SMEM)


def metric_of(levels, extent):
    return 0.5 / (1.0 + jnp.sin(jnp.pi * (levels + 0.5) / extent))


def pinned(x):
    return pltpu.with_memory_space_constraint(x, pltpu.HBM)


def halves(wide):
    high = wide.astype(jnp.bfloat16)
    return high, (wide - high.astype(jnp.float32)).astype(jnp.bfloat16)


def edge_kernel(groups, here_ref, t_hbm, yc_ref, yd_ref, za_ref, zb_ref, buf, sems):
    planes, rows, _ = t_hbm.shape
    pencil_even, slab_even = here_ref[0] % 2 == 0, here_ref[0] // groups % 2 == 0
    copies = [
        pltpu.make_async_copy(t_hbm, buf, sems.at[0]),
        pltpu.make_async_copy(t_hbm.at[jnp.where(slab_even, planes - 1, 0)], yc_ref, sems.at[1]),
        pltpu.make_async_copy(t_hbm.at[jnp.where(slab_even, 0, planes - 1)], yd_ref, sems.at[2]),
    ]
    for copy in copies:
        copy.start()
    copies[0].wait()
    for y in range(planes):
        low, high = buf[y, :1, :], buf[y, rows - 1 :, :]
        za_ref[y : y + 1, :] = jnp.where(pencil_even, low, high)
        zb_ref[y : y + 1, :] = jnp.where(pencil_even, high, low)
    copies[1].wait()
    copies[2].wait()


def edges(here, t, groups):
    planes, rows, nx = t.shape
    plane = jax.ShapeDtypeStruct((rows, nx), t.dtype)
    level = jax.ShapeDtypeStruct((planes, nx), t.dtype)
    return pl.pallas_call(
        functools.partial(edge_kernel, groups),
        in_specs=[SMEM, HBM],
        out_specs=[VMEM] * 5,
        out_shape=[plane, plane, level, level, jax.ShapeDtypeStruct(t.shape, t.dtype)],
        scratch_shapes=[pltpu.SemaphoreType.DMA((3,))],
        compiler_params=pltpu.CompilerParams(vmem_limit_bytes=8 * 2**20),
        name="edges",
    )(here, pinned(t))


def prepare_kernel(
    groups,
    here_ref,
    t_ref,
    u_hbm,
    v_hbm,
    w_hbm,
    a_hbm,
    side_ref,
    cb_ref,
    ca_ref,
    cl_ref,
    ch_ref,
    ah_ref,
    al_ref,
    u_ref,
    v_ref,
    w_ref,
    along_ref,
    wallward_ref,
    a_buf,
    sems,
):
    planes, rows, nx = side_ref.shape
    parts = sems.shape[0] - 3
    a_rows = a_buf.shape[0] // parts
    fields = [
        pltpu.make_async_copy(source, target, sems.at[i])
        for i, (source, target) in enumerate(((u_hbm, u_ref), (v_hbm, v_ref), (w_hbm, w_ref)))
    ]
    copies = []
    for i in range(parts):
        cut = slice(i * a_rows, (i + 1) * a_rows)
        copies.append(pltpu.make_async_copy(a_hbm.at[cut], a_buf.at[cut], sems.at[3 + i]))
    for copy in fields + copies:
        copy.start()
    levels = (lax.broadcasted_iota(jnp.int32, (rows, LANES), 0) + here_ref[0] % groups * rows).astype(jnp.float32)
    metric = jnp.concatenate([metric_of(levels, groups * rows)] * (nx // LANES), axis=1)
    level = lax.broadcasted_iota(jnp.int32, (rows, nx), 0)

    def plane(y):
        if y < 0 or y == planes:
            return jnp.zeros((rows, nx), jnp.float32)
        return t_ref[y]

    own = (1.0 - 3.0 * CONDUCTION_PART) - CONDUCTION_PART * metric
    near, far = 0.5 * CONDUCTION_PART * metric, TRANSPORT_PART * metric
    for y in range(planes):
        t, ahead, behind = plane(y), plane(y + 1), plane(y - 1)
        east = pltpu.roll(t, nx - 1, 1)
        west = pltpu.roll(t, 1, 1)
        above = jnp.where(level == rows - 1, 0.0, pltpu.roll(t, rows - 1, 0))
        below = jnp.where(level == 0, 0.0, pltpu.roll(t, 1, 0))
        side_ref[y] = (
            own * t
            + CONDUCTION_PART * (ahead + behind)
            + 0.5 * CONDUCTION_PART * (east + west)
            + near * (above + below)
        )
        along_ref[y] = 0.5 * TRANSPORT_PART * (east - west)
        wallward_ref[y] = far * (above - below)
    for copy in fields:
        copy.wait()
    for y in range(planes):
        u = u_ref[y].astype(jnp.float32)
        v = v_ref[y].astype(jnp.float32)
        w = w_ref[y].astype(jnp.float32)
        across = 0.5 * TRANSPORT_PART * (plane(y + 1) - plane(y - 1))
        side_ref[y] = side_ref[y] - (u * along_ref[y] + v * across + w * wallward_ref[y])
        cl_ref[y : y + 1, :] = (metric * (0.5 * CONDUCTION_PART + TRANSPORT_PART * w))[:1, :]
        ch_ref[y : y + 1, :] = (metric * (0.5 * CONDUCTION_PART - TRANSPORT_PART * w))[rows - 1 :, :]
        if y == 0:
            cb_ref[...] = CONDUCTION_PART + 0.5 * TRANSPORT_PART * v
        if y == planes - 1:
            ca_ref[...] = CONDUCTION_PART - 0.5 * TRANSPORT_PART * v
    for i in range(parts):
        cut = slice(i * a_rows, (i + 1) * a_rows)
        copies[i].wait()
        ah_ref[cut], al_ref[cut] = halves(a_buf[cut])


def prepare(here, t, u, v, w, a, groups):
    planes, rows, nx = u.shape
    a16 = jax.ShapeDtypeStruct(a.shape, jnp.bfloat16)
    plane = jax.ShapeDtypeStruct((rows, nx), t.dtype)
    level = jax.ShapeDtypeStruct((planes, nx), t.dtype)
    parts = 2
    return pl.pallas_call(
        functools.partial(prepare_kernel, groups),
        in_specs=[SMEM, VMEM] + [HBM] * 4,
        out_specs=[VMEM] * 7,
        out_shape=[jax.ShapeDtypeStruct(u.shape, t.dtype), plane, plane, level, level, a16, a16],
        scratch_shapes=[pltpu.VMEM(x.shape, x.dtype) for x in (u, v, w)]
        + [pltpu.VMEM(u.shape, t.dtype)] * 2
        + [pltpu.VMEM(a.shape, a.dtype)]
        + [pltpu.SemaphoreType.DMA((3 + parts,))],
        compiler_params=pltpu.CompilerParams(vmem_limit_bytes=20 * 2**20),
        cost_estimate=pl.CostEstimate(
            flops=4 * a.size + 40 * t.size, bytes_accessed=8 * a.size + 14 * t.size, transcendentals=0
        ),
        name="prepare",
    )(here, t, *(pinned(x) for x in (u, v, w, a)))


def row_kernel(
    here_ref, side_ref, cb_ref, ca_ref, cl_ref, ch_ref, yc_ref, yd_ref, za_ref, zb_ref, ah_ref, al_ref, out_ref, both
):
    planes, rows, nx = side_ref.shape
    groups = out_ref.shape[0]
    pencil_even, slab_even = here_ref[0] % 2 == 0, here_ref[0] // groups % 2 == 0
    low = cl_ref[...] * jnp.where(pencil_even, za_ref[...], zb_ref[...])
    high = ch_ref[...] * jnp.where(pencil_even, zb_ref[...], za_ref[...])
    level = lax.broadcasted_iota(jnp.int32, (rows, nx), 0)
    extent = planes * rows
    for y in range(planes):
        side = side_ref[y]
        if y == 0:
            side = side + cb_ref[...] * jnp.where(slab_even, yd_ref[...], yc_ref[...])
        if y == planes - 1:
            side = side + ca_ref[...] * jnp.where(slab_even, yc_ref[...], yd_ref[...])
        side = side + jnp.where(level == 0, low[y : y + 1, :], 0.0)
        side = side + jnp.where(level == rows - 1, high[y : y + 1, :], 0.0)
        high_part, low_part = halves(side)
        both[y * rows : (y + 1) * rows, :] = high_part
        both[extent + y * rows : extent + (y + 1) * rows, :] = low_part
    wide = 2 * LANES
    unit_rows = 3 * rows
    blocks = nx // LANES
    for c in range(nx // wide):
        ah = ah_ref[c * wide : (c + 1) * wide, :]
        al = al_ref[c * wide : (c + 1) * wide, :]

        def dot(x, m):
            return lax.dot_general(x, m, (((1,), (1,)), ((), ())), preferred_element_type=jnp.float32)

        main = dot(both[...], ah)
        solved = main[:extent] + (dot(both[:extent, :], al) + main[extent:])
        for q in range(planes // 3):
            for h in range(2):
                piece = solved[q * unit_rows : (q + 1) * unit_rows, h * LANES : (h + 1) * LANES]
                out_ref[q * blocks + 2 * c + h] = piece.reshape(3, rows, LANES)


def row_solve(here, parts, halos, ah, al, groups):
    planes, rows, nx = parts[0].shape
    return pl.pallas_call(
        row_kernel,
        in_specs=[SMEM] + [VMEM] * 11,
        out_specs=VMEM,
        out_shape=jax.ShapeDtypeStruct((groups, 3, rows, LANES), jnp.float32),
        scratch_shapes=[pltpu.VMEM((2 * planes * rows, nx), jnp.bfloat16)],
        compiler_params=pltpu.CompilerParams(vmem_limit_bytes=32 * 2**20),
        cost_estimate=pl.CostEstimate(
            flops=6 * planes * rows * nx * nx, bytes_accessed=8 * 2**20, transcendentals=0
        ),
        name="row_solve",
    )(here, *parts, *halos, ah, al)


def column_kernel(blocks, here_ref, seg_ref, w_ref, x_ref, out_ref):
    groups, units, rows, lanes = x_ref.shape
    column = lax.broadcasted_iota(jnp.int32, (8, lanes), 1) + here_ref[0] % blocks * lanes
    crossed = jnp.zeros((8, lanes), jnp.int32)
    end = jnp.int32(0)
    for s in range(seg_ref.shape[0]):
        end = end + seg_ref[s]
        crossed = crossed + jnp.where(column >= end, 1, 0)
    insulated = jnp.concatenate([(crossed % 2)[:1, :]] * units, axis=1) == 1
    extent = groups * rows
    lines = jnp.concatenate([x_ref[:, i].reshape(extent, lanes) for i in range(units)], axis=1)
    xh, xl = halves(lines)
    both = jnp.concatenate([xh, xl], axis=1)
    width = units * lanes

    def solve(c, cut):
        wh, wl = halves(w_ref[c, cut])
        d = jnp.dot(wh, both, preferred_element_type=jnp.float32)
        e = jnp.dot(wl, xh, preferred_element_type=jnp.float32)
        return d[:, :width] + (d[:, width:] + e)

    step = 256
    for k in range(0, extent, step):
        cut = slice(k, k + step)
        solved = jnp.where(insulated, solve(1, cut), solve(0, cut))
        for i in range(units):
            piece = solved[:, i * lanes : (i + 1) * lanes]
            out_ref[k // rows : (k + step) // rows, i] = piece.reshape(step // rows, rows, lanes)


def column_solve(here, segments, w, x, blocks):
    return pl.pallas_call(
        functools.partial(column_kernel, blocks),
        in_specs=[SMEM, SMEM, VMEM, VMEM],
        out_specs=VMEM,
        out_shape=jax.ShapeDtypeStruct(x.shape, jnp.float32),
        compiler_params=pltpu.CompilerParams(vmem_limit_bytes=32 * 2**20),
        cost_estimate=pl.CostEstimate(
            flops=12 * w.shape[1] * x.size, bytes_accessed=4 * 2**20, transcendentals=0
        ),
        name="column_solve",
    )(here, segments, w, x)


def place_kernel(x_ref, out_ref):
    groups = x_ref.shape[0]
    blocks = out_ref.shape[2] // LANES
    for p in range(groups):
        q, b = p // blocks, p % blocks
        out_ref[3 * q : 3 * q + 3, :, b * LANES : (b + 1) * LANES] = x_ref[p]


def place(x, shape):
    return pl.pallas_call(
        place_kernel,
        in_specs=[VMEM],
        out_specs=VMEM,
        out_shape=jax.ShapeDtypeStruct(shape, jnp.float32),
        compiler_params=pltpu.CompilerParams(vmem_limit_bytes=16 * 2**20),
        name="place",
    )(x)


def swapped(x):
    return lax.all_to_all(x, "pencil", split_axis=0, concat_axis=0, tiled=True)


def on_device(t, u, v, w, downstream_solver_matrix, wallward_solver_matrices, wall_segments):
    planes, rows, nx = t.shape
    slabs, groups = lax.axis_size("slab"), lax.axis_size("pencil")
    here = lax.axis_index(("slab", "pencil")).astype(jnp.int32).reshape(1)
    yc, yd, za, zb, t_here = edges(here, t, groups)
    yc = lax.ppermute(yc, "slab", [(i, i ^ 1) for i in range(slabs)])
    yd = lax.ppermute(yd, "slab", [(i, ((i - 1) ^ 1) + 1 & slabs - 1) for i in range(slabs)])
    za = lax.ppermute(za, "pencil", [(i, ((i - 1) ^ 1) + 1) for i in range(1, groups - 1)])
    zb = lax.ppermute(zb, "pencil", [(i, i ^ 1) for i in range(groups)])
    halos = yc, yd, za, zb
    *parts, ah, al = prepare(here, t_here, u, v, w, downstream_solver_matrix, groups)
    x = swapped(row_solve(here, parts, halos, ah, al, groups))
    x = swapped(column_solve(here, wall_segments, wallward_solver_matrices, x, nx // LANES))
    return place(x, t.shape)


def solution(mesh):
    field = P("slab", "pencil", None)
    return jax.shard_map(
        on_device,
        mesh=mesh,
        in_specs=(field, field, field, field, P(), P(), P()),
        out_specs=field,
        check_vma=False,
    )
```
